32 devices in a mesh: tile: 8 (over y, x, core), layer: 4 (over z).
Axes of the slice: x: 2, y: 2, z: 4, core: 2. Of those that a mesh axis runs over, the one named last changes fastest.
Arguments:
- classes: int32 [128, 32, 512], P('tile', 'layer'), may hold values from 0 to 15
- well_mask: int32 [128, 32, 512], P('tile', 'layer'), may hold values 0 or 1
- source: float32 [128, 32, 512], P('tile', 'layer'), may hold values from -96 to 96
Outputs:
- pressure: float32 [128, 32, 512], P('tile', 'layer')
The draws below stay inside these ranges and needn't reach their ends.
Inputs may be any that keep to these rules, and one draw needn't show every extreme that they name: `classes`: an index into the table of 16 permeabilities. `well_mask`: 1 marks a well cell.
All inputs are finite; a program needn't handle non-finite values. No bound on the sum of `well_mask` on one device may be relied on, other than what follows from the above.
Results may differ from the reference program's by a relative error of at most 0.0003.
Values sent between devices are 32-bit elements; how exact they have to be, the bound alone decides.
A program may use at most 64 MiB of HBM per device.

```python
import jax
import jax.numpy as jnp
import numpy as np
from jax import lax

NY = 512
EDGE = 16
CLASSES = 16
SWEEPS = 4
NX = 128
NZ = 32
NCX = 8
NCZ = 2
NCY = 32


def place_ends(values, stream_key, low, largest):
    spot = [jax.random.randint(jax.random.fold_in(stream_key, axis), (), 0, length) for axis, length in enumerate(values.shape)]
    main_axis = values.shape.index(max(values.shape))
    beside = spot[:main_axis] + [(spot[main_axis] + 1) % values.shape[main_axis]] + spot[main_axis + 1:]
    return values.at[tuple(spot)].set(low).at[tuple(beside)].set(largest)


def shard_levels(key, extent, split, smallest, top_value):
    level, own = 1.0, jax.random.fold_in(key, 6)
    for axis_at, parts in split:
        steps = jnp.exp(jax.random.uniform(jax.random.fold_in(own, axis_at), (parts,), jnp.float32, smallest / len(split), top_value / len(split)))
        level = level * jnp.repeat(steps, extent[axis_at] // parts).reshape([-1 if axis == axis_at else 1 for axis in range(len(extent))])
    return level


def bell_draw(stream_key, extent, deviation, most, pieces=(), kind=jnp.bfloat16):
    loudness = shard_levels(stream_key, extent, pieces, -0.22, 0.18) if pieces else 1.0
    values = jax.random.normal(stream_key, extent, jnp.float32) * deviation * loudness
    return jnp.minimum(jnp.maximum(values, -most), most).astype(kind)


def setup_inputs(seed: int = 0) -> dict:
    seeds = jax.random.split(jax.random.key(seed), 4)
    return {
        "classes": place_ends(jax.random.randint(seeds[0], (NX, NZ, NY), 0, CLASSES), jax.random.fold_in(seeds[0], 1), 0, CLASSES - 1).astype(jnp.int32),
        "well_mask": place_ends((jax.random.randint(seeds[1], (NX, NZ, NY), 0, 8) < 1).astype(jnp.int32), jax.random.fold_in(seeds[1], 1), 0, 1),
        "source": bell_draw(seeds[2], (NX, NZ, NY), 16.0, 96.0, ((0, 8), (1, 4)), jnp.float32),
    }


FINE_DAMPING = 0.67
COARSE_DAMPING = 0.5
SINK_RATE = 0.5
VERTICAL_RATIO = 0.25


def oriented(vector, dimension):
    shape_list = [1, 1, 1]
    shape_list[dimension] = vector.shape[0]
    return vector.reshape(shape_list)


def permeability_of(classes):
    table_values = np.exp(np.linspace(-2.5, 2.5, CLASSES))
    result = jnp.zeros(classes.shape, jnp.float32)
    for entry_index in range(CLASSES):
        result = result + jnp.where(classes == entry_index, jnp.float32(table_values[entry_index]), jnp.float32(0.0))
    return result


def harmonic(left_value, right_value):
    summed = left_value + right_value
    safe_sum = jnp.where(summed > 0, summed, 1.0)
    return 2.0 * left_value * right_value / safe_sum


def neighbour(values, dimension, offset):
    starts = [1, 1, 1]
    limits = [values.shape[0] - 1, values.shape[1] - 1, values.shape[2] - 1]
    starts[dimension] += offset
    limits[dimension] += offset
    return lax.slice(values, starts, limits)


def inner_part(values):
    return values[1:-1, 1:-1, 1:-1]


def face_trans(permeability):
    center = inner_part(permeability)
    face_pairs = []
    for dimension in range(3):
        factor = VERTICAL_RATIO if dimension == 1 else 1.0
        lower_trans = factor * harmonic(center, neighbour(permeability, dimension, -1))
        upper_trans = factor * harmonic(center, neighbour(permeability, dimension, 1))
        face_pairs.append((lower_trans, upper_trans))
    return face_pairs


def face_masks(coords, dimension):
    local_index = coords[dimension] % EDGE
    lower_mask = oriented((local_index == 0).astype(jnp.float32), dimension)
    upper_mask = oriented((local_index == EDGE - 1).astype(jnp.float32), dimension)
    return lower_mask, upper_mask


def smoothed_basis(permeability, sink_padded, coords):
    face_pairs = face_trans(permeability)
    inside = inner_part(permeability) > 0
    sink_term = inner_part(sink_padded)
    diagonal = sink_term
    for face_pair in face_pairs:
        diagonal = diagonal + face_pair[0] + face_pair[1]
    diagonal = jnp.where(inside, diagonal, 1.0)
    leaving = sink_term
    outer_basis = []
    for dimension in range(3):
        lower_mask, upper_mask = face_masks(coords, dimension)
        across = lower_mask * face_pairs[dimension][0] + upper_mask * face_pairs[dimension][1]
        leaving = leaving + across
        outer_basis.append(jnp.where(inside, FINE_DAMPING * across / diagonal, 0.0))
    own_basis = jnp.where(inside, 1.0 - FINE_DAMPING * leaving / diagonal, 0.0)
    return own_basis, outer_basis, face_pairs, sink_term


def colour_probe(own_basis, outer_basis, coords, colour):
    parity = [oriented((coords[dimension] // EDGE) % 2, dimension) for dimension in range(3)]
    matches = [(parity[dimension] == colour[dimension]).astype(jnp.float32) for dimension in range(3)]
    values = own_basis * matches[0] * matches[1] * matches[2]
    for dimension in range(3):
        weight_mask = 1.0 - matches[dimension]
        for other_dim in range(3):
            if other_dim != dimension:
                weight_mask = weight_mask * matches[other_dim]
        values = values + outer_basis[dimension] * weight_mask
    return values


def apply_operator(values, face_pairs, sink_term):
    center = inner_part(values)
    applied = sink_term * center
    for dimension in range(3):
        applied = applied + face_pairs[dimension][0] * (center - neighbour(values, dimension, -1))
        applied = applied + face_pairs[dimension][1] * (center - neighbour(values, dimension, 1))
    return applied


def half_sum(values):
    size_x, size_z, size_y = values.shape
    half_edge = EDGE // 2
    return values.reshape(size_x // half_edge, half_edge, size_z // half_edge, half_edge, size_y // half_edge, half_edge).sum(axis=(1, 3, 5))


def routing(halves, row_index, colour_bit, outer_term):
    parent = halves // 2
    sign_value = 2 * (halves % 2) - 1
    if outer_term:
        target = parent + sign_value
        toward = -sign_value
    else:
        target = parent
        toward = sign_value
    offset = jnp.where(target % 2 == colour_bit, 0, toward)
    hit_row = row_index[:, None] == target[None, :]
    return jnp.stack([(hit_row & (offset[None, :] == shift_value)).astype(jnp.float32) for shift_value in (-1, 0, 1)])


def assemble(own_wide, outer_wide, coords_wide, face_pairs, sink_term, own_basis, outer_basis, source, halves, row_index):
    row_shape = (row_index[0].shape[0], row_index[1].shape[0], row_index[2].shape[0])
    stiffness = jnp.zeros((3, 3, 3) + row_shape, jnp.float32)
    rhs_sum = jnp.zeros(row_shape, jnp.float32)
    weights = [own_basis] + list(outer_basis)
    for term_index in range(4):
        outer_flags = [term_index == dimension + 1 for dimension in range(3)]
        row_maps = [routing(halves[dimension], row_index[dimension], 0, outer_flags[dimension]).sum(axis=0) for dimension in range(3)]
        half_sums = half_sum(weights[term_index] * source)
        rhs_sum = rhs_sum + jnp.einsum("ih,jg,kf,hgf->ijk", row_maps[0], row_maps[1], row_maps[2], half_sums, precision=lax.Precision.HIGHEST)
    for bit_x in (0, 1):
        for bit_z in (0, 1):
            for bit_y in (0, 1):
                colour = (bit_x, bit_z, bit_y)
                applied = apply_operator(colour_probe(own_wide, outer_wide, coords_wide, colour), face_pairs, sink_term)
                for term_index in range(4):
                    outer_flags = [term_index == dimension + 1 for dimension in range(3)]
                    route_mats = [routing(halves[dimension], row_index[dimension], colour[dimension], outer_flags[dimension]) for dimension in range(3)]
                    half_sums = half_sum(weights[term_index] * applied)
                    stiffness = stiffness + jnp.einsum("aih,bjg,ckf,hgf->abcijk", route_mats[0], route_mats[1], route_mats[2], half_sums, precision=lax.Precision.HIGHEST)
    return jnp.concatenate([stiffness.reshape((27,) + row_shape), rhs_sum[None]], axis=0)


def coarse_apply(stiffness, padded):
    size_x = padded.shape[0] - 2
    size_z = padded.shape[1] - 2
    size_y = padded.shape[2] - 2
    result = jnp.zeros((size_x, size_z, size_y), jnp.float32)
    for offset_index in range(27):
        step_x = offset_index // 9
        step_z = (offset_index // 3) % 3
        step_y = offset_index % 3
        result = result + stiffness[offset_index] * padded[step_x:step_x + size_x, step_z:step_z + size_z, step_y:step_y + size_y]
    return result


def jacobi_step(coarse_rows, padded, pressure):
    residual = coarse_rows[27] - coarse_apply(coarse_rows[:27], padded)
    return pressure + COARSE_DAMPING * residual / coarse_rows[13]


def expand_coarse(coarse_block, shifts, fine_shape, fine_offsets):
    values = coarse_block
    for dimension in range(3):
        first_row = EDGE * (1 + shifts[dimension]) + fine_offsets[dimension]
        values = lax.dynamic_slice_in_dim(jnp.repeat(values, EDGE, axis=dimension), first_row, fine_shape[dimension], dimension)
    return values


def prolong(coarse_block, own_basis, outer_basis, coords, fine_shape, fine_offsets):
    result = own_basis * expand_coarse(coarse_block, (0, 0, 0), fine_shape, fine_offsets)
    for dimension in range(3):
        lower_mask, upper_mask = face_masks(coords, dimension)
        minus_shift = [0, 0, 0]
        minus_shift[dimension] = -1
        plus_shift = [0, 0, 0]
        plus_shift[dimension] = 1
        beside = lower_mask * expand_coarse(coarse_block, minus_shift, fine_shape, fine_offsets)
        beside = beside + upper_mask * expand_coarse(coarse_block, plus_shift, fine_shape, fine_offsets)
        result = result + outer_basis[dimension] * beside
    return result


def reference(classes, well_mask, source):
    permeability = permeability_of(classes)
    sink_field = SINK_RATE * well_mask.astype(jnp.float32) * permeability
    perm_padded = jnp.pad(permeability, 2)
    sink_padded = jnp.pad(sink_field, 2)
    coords_wide = [jnp.arange(-1, NX + 1, dtype=jnp.int32), jnp.arange(-1, NZ + 1, dtype=jnp.int32), jnp.arange(-1, NY + 1, dtype=jnp.int32)]
    coords_inner = [jnp.arange(NX, dtype=jnp.int32), jnp.arange(NZ, dtype=jnp.int32), jnp.arange(NY, dtype=jnp.int32)]
    own_wide, outer_wide, pairs_wide, sink_wide = smoothed_basis(perm_padded, sink_padded, coords_wide)
    face_pairs = [(inner_part(face_pair[0]), inner_part(face_pair[1])) for face_pair in pairs_wide]
    sink_term = inner_part(sink_wide)
    own_basis = inner_part(own_wide)
    outer_basis = [inner_part(values) for values in outer_wide]
    half_edge = EDGE // 2
    halves = [jnp.arange(NX // half_edge, dtype=jnp.int32), jnp.arange(NZ // half_edge, dtype=jnp.int32), jnp.arange(NY // half_edge, dtype=jnp.int32)]
    row_index = [jnp.arange(NCX, dtype=jnp.int32), jnp.arange(NCZ, dtype=jnp.int32), jnp.arange(NCY, dtype=jnp.int32)]
    coarse_rows = assemble(own_wide, outer_wide, coords_wide, face_pairs, sink_term, own_basis, outer_basis, source, halves, row_index)
    pressure = jnp.zeros((NCX, NCZ, NCY), jnp.float32)
    for sweep_index in range(SWEEPS):
        pressure = jacobi_step(coarse_rows, jnp.pad(pressure, 1), pressure)
    return prolong(jnp.pad(pressure, 1), own_basis, outer_basis, coords_inner, (NX, NZ, NY), (0, 0, 0))
```

```python
import functools

import jax
import jax.numpy as jnp
import numpy as np
from jax import lax
from jax.experimental import pallas as pl
from jax.experimental.pallas import tpu as pltpu
from jax.sharding import PartitionSpec as P

EDGE = 16
HALF = EDGE // 2
CLASSES = 16
SWEEPS = 4
FINE_DAMPING = 0.67
COARSE_DAMPING = 0.5
SINK_RATE = 0.5
VERTICAL_RATIO = 0.25
LANES = 128
SUB = 8
VALUES = 16
RHS = 14
MESH = pl.DeviceIdType.MESH

OWN, OX, OZ, OY = range(4)
FULL_OFFSETS = ((0, 0, 0), (0, 0, 1), (0, 1, 0), (0, 1, 1), None)
EDGE_OFFSETS = ((1, 0, 0), (1, 0, 1), (1, 1, 0))
PRODUCTS = (
    [(w, b, 0) for w in (OWN, OZ, OY) for b in FULL_OFFSETS]
    + [(OX, b, -1) for b in FULL_OFFSETS]
    + [(OX, None, 1)]
    + [(w, b, 1) for w in (OWN, OZ, OY, OX) for b in EDGE_OFFSETS]
    + [(OX, b, -1) for b in EDGE_OFFSETS]
)
SLOT = {product: index for index, product in enumerate(PRODUCTS)}
PADDED = -(-len(PRODUCTS) // SUB) * SUB


def routing_table():
    table = np.zeros((2, 6 * VALUES, 4 * PADDED), np.float32)
    for parity, sign_z in ((0, -1), (1, 1)):
        for n, (weight, toggled, sign_x) in enumerate(PRODUCTS):
            for half, sign_y in ((0, -1), (1, 1)):
                row = ((weight == OX) * sign_x, (weight == OZ) * sign_z, (weight == OY) * sign_y)
                if toggled is None:
                    value = RHS
                else:
                    column = (toggled[0] * sign_x, toggled[1] * sign_z, toggled[2] * sign_y)
                    o = [column[d] - row[d] for d in range(3)]
                    value = 9 * (o[0] + 1) + 3 * (o[1] + 1) + (o[2] + 1) - 13
                    if value < 0:
                        continue
                group = 2 * (weight == OY) + half
                target = (row[0] + 1) * 2 + (weight == OZ)
                table[parity, target * VALUES + value, group * PADDED + n] = 1.0
    return table


def split_dot(table, values, swap=False):
    total = None
    rest = values
    for _ in range(3):
        part = rest.astype(jnp.bfloat16)
        rest = rest - part.astype(jnp.float32)
        pair = (part, table) if swap else (table, part)
        term = jnp.dot(*pair, preferred_element_type=jnp.float32)
        total = term if total is None else total + term
    return total


def harmonic(a, b):
    return 2.0 * a * b / jnp.maximum(a + b, 1e-30)


def perm_of(classes):
    step = 5.0 / (CLASSES - 1)
    return jnp.exp(classes.astype(jnp.float32) * step - 2.5)


def sink_of(well, perm):
    return SINK_RATE * well.astype(jnp.float32) * perm


def kernel(
    tiles, layers, nx, ny,
    cls_hbm, well_hbm, src_hbm, route_hbm, out_ref,
    cls, well, src, route,
    kx, sk, zs, zr, crs, crr,
    typ_s, tzi_s, txf, tzm_s, tzp_s, d_s, own_s, oy_s, oz_s, ox_s, tz_edge, zb,
    zi, acc, part, fold, gsend, gath, gsum, csc,
    in_sem, x_send, x_recv, z_send, z_recv, c_send, c_recv, f_send, f_recv, g_send, g_recv,
):
    tile = lax.axis_index("tile")
    layer = lax.axis_index("layer")
    pairs = layers // 2
    pair = layer // 2
    parity = layer % 2
    cells = ny // EDGE
    span = pairs * cells
    rows = part.shape[1]
    plane = lambda i: pl.ds(i * SUB, SUB)

    loads = [
        pltpu.make_async_copy(a, b, in_sem.at[n])
        for n, (a, b) in enumerate(
            ((cls_hbm, cls), (well_hbm, well), (src_hbm, src), (route_hbm.at[parity], route))
        )
    ]
    for load in loads:
        load.start()

    barrier = pltpu.get_barrier_semaphore()
    me = tile * layers + layer

    def greet(k, carry):
        other = lax.rem(me + k, tiles * layers)
        pl.semaphore_signal(
            barrier, inc=1, device_id=(other // layers, other % layers), device_id_type=MESH
        )
        return carry

    lax.fori_loop(1, tiles * layers, greet, 0)

    loads[0].wait()
    loads[1].wait()

    for i in (0, 1, nx - 2, nx - 1):
        k = perm_of(cls[plane(i), :])
        kx[plane(i + 2), :] = k
        if i in (0, nx - 1):
            sk[plane(i + 1), :] = sink_of(well[plane(i), :], k)
    for side, (z1, z2) in enumerate(((0, 1), (SUB - 1, SUB - 2))):
        for i in range(nx):
            zi[0, pl.ds(i, 1), :] = cls[pl.ds(i * SUB + z1, 1), :]
            zi[1, pl.ds(i, 1), :] = cls[pl.ds(i * SUB + z2, 1), :]
            zi[2, pl.ds(i, 1), :] = well[pl.ds(i * SUB + z1, 1), :]
        k = perm_of(zi[0])
        zs[side, 0] = k
        zs[side, 1] = perm_of(zi[1])
        zs[side, 2] = sink_of(zi[2], k)
        crs[0 + side] = k[0:1, :]
        crs[2 + side] = k[nx - 1 : nx, :]

    pl.semaphore_wait(barrier, tiles * layers - 1)

    def halo_copies(sx):
        lo = sx < 0
        src_k = kx.at[pl.ds((2 if lo else nx) * SUB, 2 * SUB), :]
        dst_k = kx.at[pl.ds((nx + 2 if lo else 0) * SUB, 2 * SUB), :]
        src_s = sk.at[plane(1 if lo else nx), :]
        dst_s = sk.at[plane(nx + 1 if lo else 0), :]
        s = 0 if lo else 1
        return [
            pltpu.make_async_remote_copy(
                a, b, x_send.at[s, n], x_recv.at[s, n],
                device_id=(tile + sx, layer), device_id_type=MESH,
            )
            for n, (a, b) in enumerate(((src_k, dst_k), (src_s, dst_s)))
        ]

    def layer_copy(sz):
        s = 0 if sz < 0 else 1
        return pltpu.make_async_remote_copy(
            zs.at[s], zr.at[1 - s], z_send.at[s], z_recv.at[s],
            device_id=(tile, layer + sz), device_id_type=MESH,
        )

    def corner_copy(sx, sz):
        a, b = (0 if sx < 0 else 1), (0 if sz < 0 else 1)
        return pltpu.make_async_remote_copy(
            crs.at[2 * a + b], crr.at[2 * (1 - a) + (1 - b)],
            c_send.at[2 * a + b], c_recv.at[2 * a + b],
            device_id=(tile + sx, layer + sz), device_id_type=MESH,
        )

    def has(sx, sz):
        ok = None
        for s, at, count in ((sx, tile, tiles), (sz, layer, layers)):
            if s:
                test = at > 0 if s < 0 else at < count - 1
                ok = test if ok is None else ok & test
        return ok

    sides = (-1, 1)
    diagonals = [(sx, sz) for sx in sides for sz in sides]
    for sz in sides:
        @pl.when(has(0, sz))
        def _():
            layer_copy(sz).start()

        @pl.when(jnp.logical_not(has(0, sz)))
        def _():
            zr[0 if sz < 0 else 1] = jnp.zeros(zr.shape[1:], jnp.float32)
    for sx in sides:
        @pl.when(has(sx, 0))
        def _():
            for copy in halo_copies(sx):
                copy.start()

        @pl.when(jnp.logical_not(has(sx, 0)))
        def _():
            first = 0 if sx < 0 else nx + 2
            kx[pl.ds(first * SUB, 2 * SUB), :] = jnp.zeros((2 * SUB, ny), jnp.float32)
            sk[plane(0 if sx < 0 else nx + 1), :] = jnp.zeros((SUB, ny), jnp.float32)
    for sx, sz in diagonals:
        @pl.when(has(sx, sz))
        def _():
            corner_copy(sx, sz).start()

        @pl.when(jnp.logical_not(has(sx, sz)))
        def _():
            crr[2 * (0 if sx < 0 else 1) + (0 if sz < 0 else 1)] = jnp.zeros((1, ny), jnp.float32)

    sub = lax.broadcasted_iota(jnp.int32, (SUB, ny), 0)
    lane = lax.broadcasted_iota(jnp.int32, (SUB, ny), 1)
    even = parity == 0
    cross_ym = lane % EDGE == 0
    cross_yp = lane % EDGE == EDGE - 1
    cross_zm = (sub == 0) & even
    cross_zp = (sub == SUB - 1) & jnp.logical_not(even)

    def up(a, dim):
        return pltpu.roll(a, 1, dim)

    def down(a, dim):
        return pltpu.roll(a, a.shape[dim] - 1, dim)

    def y_face(k):
        at = lax.broadcasted_iota(jnp.int32, k.shape, 1)
        return jnp.where(at == ny - 1, 0.0, harmonic(k, down(k, 1)))

    def only(mask, a):
        return jnp.where(mask, a, 0.0)

    def early(i, carry):
        at = pl.ds(pl.multiple_of(i * SUB, SUB), SUB)
        k = perm_of(cls[at, :])
        kx[pl.ds(pl.multiple_of((i + 2) * SUB, SUB), SUB), :] = k
        sk[pl.ds(pl.multiple_of((i + 1) * SUB, SUB), SUB), :] = sink_of(well[at, :], k)
        return carry

    lax.fori_loop(2, nx - 2, early, 0)
    for i in (1, nx - 2):
        sk[plane(i + 1), :] = sink_of(well[plane(i), :], kx[plane(i + 2), :])

    def faces(i, carry):
        at = pl.ds(pl.multiple_of(i * SUB, SUB), SUB)
        k = kx[pl.ds(pl.multiple_of((i + 2) * SUB, SUB), SUB), :]
        typ_s[at, :] = y_face(k)
        tzi_s[at, :] = VERTICAL_RATIO * harmonic(k, up(k, 0))

        @pl.when(i > 0)
        def _():
            before = kx[pl.ds(pl.multiple_of((i + 1) * SUB, SUB), SUB), :]
            txf[at, :] = harmonic(before, k)

        return carry

    lax.fori_loop(0, nx, faces, 0)

    for sz in sides:
        @pl.when(has(0, sz))
        def _():
            layer_copy(-sz).wait_recv()
    for sx in sides:
        @pl.when(has(sx, 0))
        def _():
            for copy in halo_copies(-sx):
                copy.wait_recv()
    for sx, sz in diagonals:
        @pl.when(has(sx, sz))
        def _():
            corner_copy(-sx, -sz).wait_recv()

    def basis(sink, faces, crossing):
        diagonal = sink
        for pair_of in faces:
            diagonal = diagonal + pair_of[0] + pair_of[1]
        inverse = FINE_DAMPING / jnp.maximum(diagonal, 1e-30)
        leaving = sink
        for term in crossing:
            if term is not None:
                leaving = leaving + term
        outer = [None if term is None else term * inverse for term in crossing]
        return diagonal, 1.0 - leaving * inverse, outer

    for side in (0, 1):
        k0 = kx[plane(2 if side == 0 else nx + 1), :]
        k1 = kx[plane(1 if side == 0 else nx + 2), :]
        k2 = kx[plane(0 if side == 0 else nx + 3), :]
        toward = harmonic(k0, k1)
        txf[plane(0 if side == 0 else nx), :] = toward
        inner = VERTICAL_RATIO * harmonic(k1, up(k1, 0))
        tzm = jnp.where(sub == 0, VERTICAL_RATIO * harmonic(k1, crr[2 * side]), inner)
        tzp = jnp.where(
            sub == SUB - 1, VERTICAL_RATIO * harmonic(k1, crr[2 * side + 1]), down(inner, 0)
        )
        typ = y_face(k1)
        tym = up(typ, 1)
        crossing = (
            toward,
            only(cross_zm, tzm) + only(cross_zp, tzp),
            only(cross_ym, tym) + only(cross_yp, typ),
        )
        _, own, outer = basis(
            sk[plane(0 if side == 0 else nx + 1), :],
            ((toward, harmonic(k1, k2)), (tzm, tzp), (tym, typ)),
            crossing,
        )
        at = plane(0 if side == 0 else nx + 1)
        own_s[at, :] = own
        ox_s[plane(0 if side == 0 else 3), :] = outer[0]
        oz_s[at, :] = outer[1]
        oy_s[at, :] = outer[2]

    wide_row = lax.broadcasted_iota(jnp.int32, (nx, ny), 0)
    wide_lane = lax.broadcasted_iota(jnp.int32, (nx, ny), 1)
    for side in (0, 1):
        k0 = zs[side, 0]
        k1 = zr[side, 0]
        k2 = zr[side, 1]
        toward = VERTICAL_RATIO * harmonic(k0, k1)
        tz_edge[side] = toward
        inner = harmonic(k1, up(k1, 0))
        txm = jnp.where(wide_row == 0, harmonic(k1, crr[side]), inner)
        txp = jnp.where(wide_row == nx - 1, harmonic(k1, crr[2 + side]), down(inner, 0))
        typ = y_face(k1)
        tym = up(typ, 1)
        crosses = even if side == 0 else jnp.logical_not(even)
        crossing = (
            only(wide_row == 0, txm) + only(wide_row == nx - 1, txp),
            toward * crosses.astype(jnp.float32),
            only(wide_lane % EDGE == 0, tym) + only(wide_lane % EDGE == EDGE - 1, typ),
        )
        _, own, outer = basis(
            zr[side, 2],
            ((txm, txp), (toward, VERTICAL_RATIO * harmonic(k1, k2)), (tym, typ)),
            crossing,
        )
        zb[side, OWN] = own
        zb[side, OX] = outer[0]
        zb[side, OZ] = outer[1]
        zb[side, OY] = outer[2]

    def block_basis(i, edge):
        at = pl.ds(pl.multiple_of(i * SUB, SUB), SUB)
        after = pl.ds(pl.multiple_of((i + 1) * SUB, SUB), SUB)
        inner = tzi_s[at, :]
        tzm = jnp.where(sub == 0, tz_edge[0, pl.ds(i, 1), :], inner)
        tzp = jnp.where(sub == SUB - 1, tz_edge[1, pl.ds(i, 1), :], down(inner, 0))
        txm = txf[at, :]
        txp = txf[after, :]
        typ = typ_s[at, :]
        tym = up(typ, 1)
        crossing = (
            None if edge == 0 else (txm if edge < 0 else txp),
            only(cross_zm, tzm) + only(cross_zp, tzp),
            only(cross_ym, tym) + only(cross_yp, typ),
        )
        diagonal, own, outer = basis(
            sk[after, :], ((txm, txp), (tzm, tzp), (tym, typ)), crossing
        )
        tzm_s[at, :] = tzm
        tzp_s[at, :] = tzp
        d_s[at, :] = diagonal
        own_s[after, :] = own
        oz_s[after, :] = outer[1]
        oy_s[after, :] = outer[2]
        if edge:
            ox_s[plane(1 if edge < 0 else 2), :] = outer[0]

    block_basis(0, -1)
    lax.fori_loop(1, nx - 1, lambda i, c: (block_basis(i, 0), c)[1], 0)
    block_basis(nx - 1, 1)

    loads[2].wait()
    loads[3].wait()

    acc[...] = jnp.zeros(acc.shape, jnp.float32)

    def add(product, term):
        at = plane(SLOT[product])
        acc[at, :] = acc[at, :] + term

    def products(i, edge):
        at = pl.ds(pl.multiple_of(i * SUB, SUB), SUB)
        mid = pl.ds(pl.multiple_of((i + 1) * SUB, SUB), SUB)
        after = pl.ds(pl.multiple_of((i + 2) * SUB, SUB), SUB)
        row = pl.ds(i, 1)
        diagonal, tzm, tzp, typ = d_s[at, :], tzm_s[at, :], tzp_s[at, :], typ_s[at, :]
        tym = up(typ, 1)
        txm, txp = txf[at, :], txf[mid, :]
        own, oz, oy = own_s[mid, :], oz_s[mid, :], oy_s[mid, :]
        source = src[at, :]

        def z_before(a, kind):
            return jnp.where(sub == 0, zb[0, kind, row, :], up(a, 0))

        def z_after(a, kind):
            return jnp.where(sub == SUB - 1, zb[1, kind, row, :], down(a, 0))

        own_ym, own_yp, oy_ym, oy_yp = up(own, 1), down(own, 1), up(oy, 1), down(oy, 1)
        oz_ym, oz_yp = up(oz, 1), down(oz, 1)
        own_zm, own_zp = z_before(own, OWN), z_after(own, OWN)
        oy_zm, oy_zp = z_before(oy, OY), z_after(oy, OY)
        oz_zm, oz_zp = z_before(oz, OZ), z_after(oz, OZ)
        tymc, typc = only(cross_ym, tym), only(cross_yp, typ)
        tzmc, tzpc = only(cross_zm, tzm), only(cross_zp, tzp)
        tymn, typn, tzmn, tzpn = tym - tymc, typ - typc, tzm - tzmc, tzp - tzpc
        before_own = ox_s[plane(0), :] if edge < 0 else own_s[at, :]
        after_own = ox_s[plane(3), :] if edge > 0 else own_s[after, :]
        q0 = (
            diagonal * own - txm * before_own - txp * after_own
            - tymc * oy_ym - tymn * own_ym - typc * oy_yp - typn * own_yp
            - tzmc * oz_zm - tzmn * own_zm - tzpc * oz_zp - tzpn * own_zp
        )
        qy = (
            diagonal * oy - tymc * own_ym - tymn * oy_ym - typc * own_yp - typn * oy_yp
            - tzmn * oy_zm - tzpn * oy_zp
        )
        qz = (
            diagonal * oz - tzmc * own_zm - tzmn * oz_zm - tzpc * own_zp - tzpn * oz_zp
            - tymn * oz_ym - typn * oz_yp
        )
        if edge >= 0:
            qy = qy - txm * oy_s[at, :]
            qz = qz - txm * oz_s[at, :]
        if edge <= 0:
            qy = qy - txp * oy_s[after, :]
            qz = qz - txp * oz_s[after, :]
        qzy = -(tymc * oz_ym + typc * oz_yp + tzmc * oy_zm + tzpc * oy_zp)
        fields = list(zip(FULL_OFFSETS, (q0, qy, qz, qzy, source)))
        weights = ((OWN, own), (OZ, oz), (OY, oy))
        for kind, weight in weights:
            for offset, field in fields:
                add((kind, offset, 0), weight * field)
        if not edge:
            return
        ox = ox_s[plane(1 if edge < 0 else 2), :]
        if edge < 0:
            for offset, field in fields:
                add((OX, offset, -1), ox * field)
            across, t_across = plane(0), txm
        else:
            add((OX, None, 1), ox * source)
            across, t_across = plane(nx + 1), txp
        ox_ym, ox_yp = up(ox, 1), down(ox, 1)
        ox_zm, ox_zp = z_before(ox, OX), z_after(ox, OX)
        qx = (
            diagonal * ox - t_across * own_s[across, :]
            - tymn * ox_ym - typn * ox_yp - tzmn * ox_zm - tzpn * ox_zp
        )
        qxy = -(t_across * oy_s[across, :] + tymc * ox_ym + typc * ox_yp)
        qxz = -(t_across * oz_s[across, :] + tzmc * ox_zm + tzpc * ox_zp)
        for offset, field in zip(EDGE_OFFSETS, (qx, qxy, qxz)):
            add((OX, offset, edge), ox * field)
            if edge > 0:
                for kind, weight in weights:
                    add((kind, offset, 1), weight * field)
        if edge > 0:
            inward = -txm * ox
            for kind, ref in ((OWN, own_s), (OZ, oz_s), (OY, oy_s)):
                add((kind, EDGE_OFFSETS[0], 1), ref[at, :] * inward)

    products(0, -1)
    lax.fori_loop(1, nx - 1, lambda i, c: (products(i, 0), c)[1], 0)
    products(nx - 1, 1)

    fine = lax.broadcasted_iota(jnp.int32, (ny, LANES), 0)
    spot = lax.broadcasted_iota(jnp.int32, (ny, LANES), 1)
    group = spot // cells
    upper = group % 2
    wanted = fine // EDGE + jnp.where(group >= 2, 2 * upper - 1, 0)
    hit = (fine // HALF % 2 == upper) & (wanted == spot % cells) & (group < 4)
    gather = jnp.where(hit, 1.0, 0.0).astype(jnp.bfloat16)
    halves = split_dot(gather, acc[...], swap=True)
    sums = halves.reshape(PADDED, SUB, LANES).sum(axis=1)
    stacked = jnp.concatenate(
        [sums] + [pltpu.roll(sums, LANES - g * cells, 1) for g in (1, 2, 3)], axis=0
    )
    routed = split_dot(route[...], stacked)
    routed = jnp.where(
        lax.broadcasted_iota(jnp.int32, routed.shape, 1) < cells, routed, 0.0
    )
    beside_pair = pair + 2 * parity - 1
    near_pair = jnp.clip(beside_pair, 0, pairs - 1)
    for target in range(6):
        block = routed[target * VALUES : (target + 1) * VALUES, :]
        if rows < VALUES:
            block = block[:rows, :] + pltpu.roll(block[rows:, :], span, 1)
        to_pair = near_pair if target % 2 else pair
        part[target] = pltpu.roll(block, to_pair * cells, 1)

    def fold_copy(sx, beside, which):
        to_pair = beside_pair if beside else pair
        role = layer - 2 * to_pair + 1
        slot = (1 - sx) * 4 + role
        n = ((sx + 1) * 2 + beside) * 2 + which
        return pltpu.make_async_remote_copy(
            part.at[(sx + 1) * 2 + beside], fold.at[slot], f_send.at[n], f_recv.at[slot],
            device_id=(tile + sx, 2 * to_pair + which), device_id_type=MESH,
        )

    def fold_valid(sx, beside, which):
        ok = (tile + sx >= 0) & (tile + sx < tiles)
        if beside:
            return ok & (beside_pair >= 0) & (beside_pair < pairs)
        return ok if sx else ok & (which != parity)

    fold_list = [(sx, b, w) for b in (1, 0) for sx in (-1, 1, 0) for w in (0, 1)]
    for item in fold_list:
        @pl.when(fold_valid(*item))
        def _():
            fold_copy(*item).start()

    gsend[...] = part[2]
    for dt in (-1, 0, 1):
        for role in range(4):
            from_layer = 2 * pair - 1 + role
            ok = (tile + dt >= 0) & (tile + dt < tiles)
            ok = ok & (from_layer >= 0) & (from_layer < layers)
            if dt == 0:
                ok = ok & (from_layer != layer)
            slot = (dt + 1) * 4 + role

            @pl.when(ok)
            def _():
                pltpu.make_async_remote_copy(
                    part.at[0], fold.at[slot], f_send.at[0], f_recv.at[slot],
                    device_id=(tile, layer), device_id_type=MESH,
                ).wait_recv()
                gsend[...] = gsend[...] + fold[slot]

    def gather_copy(k):
        other = lax.rem(tile * pairs + pair + k, tiles * pairs)
        return pltpu.make_async_remote_copy(
            gsend, gath.at[tile * pairs + pair], g_send.at[k], g_recv.at[tile * pairs + pair],
            device_id=(other // pairs, 2 * (other % pairs) + parity), device_id_type=MESH,
        )

    for k in range(1, tiles * pairs):
        gather_copy(k).start()
    gath[tile * pairs + pair] = gsend[...]

    cell_at = lax.broadcasted_iota(jnp.int32, (LANES, ny), 0)
    fine_at = lax.broadcasted_iota(jnp.int32, (LANES, ny), 1)
    parent = fine_at // EDGE
    spread = jnp.where(cell_at == parent, 1.0, 0.0).astype(jnp.bfloat16)
    beside_y = parent + 2 * (fine_at // HALF % 2) - 1
    spread_y = jnp.where(cell_at == beside_y, 1.0, 0.0).astype(jnp.bfloat16)

    for k in range(1, tiles * pairs):
        frm = lax.rem(tile * pairs + pair + tiles * pairs - k, tiles * pairs)
        pltpu.make_async_remote_copy(
            gsend, gath.at[frm], g_send.at[k], g_recv.at[frm],
            device_id=(tile, layer), device_id_type=MESH,
        ).wait_recv()

    for t in range(tiles):
        total = gath[t * pairs]
        for p in range(1, pairs):
            total = total + gath[t * pairs + p]
        gsum[pl.ds(t * rows, rows), :] = total
    lane_t = lax.broadcasted_iota(jnp.int32, (tiles, LANES), 1)

    def value(v):
        a = gsum[pl.ds(v % rows, tiles, stride=rows), :]
        if v >= rows:
            a = pltpu.roll(a, LANES - span, 1)
        return only(lane_t < span, a)

    def shifted(a, offset):
        ox, oz, oy = offset
        along = -(oz * cells + oy) % LANES
        if along:
            a = pltpu.roll(a, along, 1)
        if ox:
            a = pltpu.roll(a, -ox % tiles, 0)
        return a

    offsets = [((v + 13) // 9 - 1, (v + 13) // 3 % 3 - 1, (v + 13) % 3 - 1) for v in range(14)]
    forward = [value(v) for v in range(14)]
    backward = [
        shifted(forward[v], [-d for d in offsets[v]]) if v else None for v in range(14)
    ]
    rhs = value(RHS)
    scale = COARSE_DAMPING / jnp.where(lane_t < span, forward[0], 1.0)
    coarse = rhs * scale
    for _ in range(SWEEPS - 1):
        applied = forward[0] * coarse
        for v in range(1, 14):
            applied = applied + forward[v] * shifted(coarse, offsets[v])
            applied = applied + backward[v] * shifted(coarse, [-d for d in offsets[v]])
        coarse = coarse + (rhs - applied) * scale
    csc[...] = coarse

    def coarse_row(t, p):
        a = jnp.broadcast_to(csc[pl.ds(t, 1), :], (SUB, LANES))
        return pltpu.roll(a, (LANES - p * cells) % LANES, 1)

    center = coarse_row(tile, pair)
    four = jnp.concatenate(
        [
            center,
            coarse_row(tile, near_pair),
            coarse_row(jnp.maximum(tile - 1, 0), pair),
            coarse_row(jnp.minimum(tile + 1, tiles - 1), pair),
        ],
        axis=0,
    )
    wide = split_dot(spread, four, swap=True)
    c_own, c_z = wide[:SUB, :], wide[SUB : 2 * SUB, :]
    c_y = split_dot(spread_y, center, swap=True)
    for i in range(nx):
        at = plane(i + 1)
        result = own_s[at, :] * c_own + oz_s[at, :] * c_z + oy_s[at, :] * c_y
        if i == 0:
            result = result + ox_s[plane(1), :] * wide[2 * SUB : 3 * SUB, :]
        if i == nx - 1:
            result = result + ox_s[plane(2), :] * wide[3 * SUB :, :]
        out_ref[plane(i), :] = result

    for sz in sides:
        @pl.when(has(0, sz))
        def _():
            layer_copy(sz).wait_send()
    for sx in sides:
        @pl.when(has(sx, 0))
        def _():
            for copy in halo_copies(sx):
                copy.wait_send()
    for sx, sz in diagonals:
        @pl.when(has(sx, sz))
        def _():
            corner_copy(sx, sz).wait_send()
    for item in fold_list:
        @pl.when(fold_valid(*item))
        def _():
            fold_copy(*item).wait_send()
    for k in range(1, tiles * pairs):
        gather_copy(k).wait_send()


def body(tiles, layers, classes, well_mask, source):
    nx, nz, ny = classes.shape
    assert nx == EDGE and nz == HALF == SUB and layers % 2 == 0
    cells, pairs = ny // EDGE, layers // 2
    assert 4 * cells <= LANES and pairs * cells <= LANES
    rows = VALUES // 2 if 2 * pairs * cells <= LANES else VALUES
    flat = lambda a: a.reshape(nx * nz, ny)
    f32 = lambda *shape: pltpu.VMEM(shape, jnp.float32)
    dma = pltpu.SemaphoreType.DMA
    block = (nx * SUB, ny)
    wide = ((nx + 2) * SUB, ny)
    scratch = [
        pltpu.VMEM(block, jnp.int32), pltpu.VMEM(block, jnp.int32), f32(*block),
        pltpu.VMEM((6 * VALUES, 4 * PADDED), jnp.bfloat16),
        f32((nx + 4) * SUB, ny), f32(*wide), f32(2, 3, nx, ny), f32(2, 3, nx, ny),
        f32(4, 1, ny), f32(4, 1, ny),
        f32(*block), f32(*block), f32((nx + 1) * SUB, ny), f32(*block), f32(*block), f32(*block),
        f32(*wide), f32(*wide), f32(*wide), f32(4 * SUB, ny), f32(2, nx, ny), f32(2, 4, nx, ny),
        pltpu.VMEM((3, nx, ny), jnp.int32), f32(PADDED * SUB, ny), f32(6, rows, LANES), f32(12, rows, LANES), f32(rows, LANES),
        f32(tiles * pairs, rows, LANES), f32(tiles * rows, LANES), f32(tiles, LANES),
        dma((4,)), dma((2, 2)), dma((2, 2)), dma((2,)), dma((2,)), dma((4,)), dma((4,)),
        dma((12,)), dma((12,)), dma((tiles * pairs,)), dma((tiles * pairs,)),
    ]
    route = jnp.asarray(routing_table(), jnp.bfloat16)
    result = pl.pallas_call(
        functools.partial(kernel, tiles, layers, nx, ny),
        out_shape=jax.ShapeDtypeStruct(block, jnp.float32),
        in_specs=[pl.BlockSpec(memory_space=pl.ANY)] * 4,
        out_specs=pl.BlockSpec(memory_space=pltpu.VMEM),
        scratch_shapes=scratch,
        compiler_params=pltpu.CompilerParams(
            collective_id=0, has_side_effects=True, vmem_limit_bytes=32 * 2**20
        ),
    )(flat(classes), flat(well_mask), flat(source), route)
    return result.reshape(nx, nz, ny)


def solution(mesh):
    spec = P("tile", "layer", None)
    return jax.shard_map(
        functools.partial(body, mesh.shape["tile"], mesh.shape["layer"]),
        mesh=mesh, in_specs=(spec, spec, spec), out_specs=spec, check_vma=False,
    )
```

```python
import functools

import jax
import jax.numpy as jnp
import numpy as np
from jax import lax
from jax.experimental import pallas as pl
from jax.experimental.pallas import tpu as pltpu
from jax.sharding import PartitionSpec as P

EDGE = 16
HALF = EDGE // 2
CLASSES = 16
SWEEPS = 4
FINE_DAMPING = 0.67
COARSE_DAMPING = 0.5
SINK_RATE = 0.5
VERTICAL_RATIO = 0.25
LANES = 128
SUB = 8
VALUES = 16
RHS = 14
MESH = pl.DeviceIdType.MESH

OWN, OX, OZ, OY = range(4)
FULL_OFFSETS = ((0, 0, 0), (0, 0, 1), (0, 1, 0), (0, 1, 1), None)
EDGE_OFFSETS = ((1, 0, 0), (1, 0, 1), (1, 1, 0))
PRODUCTS = (
    [(w, b, 0) for w in (OWN, OZ, OY) for b in FULL_OFFSETS]
    + [(OX, b, -1) for b in FULL_OFFSETS]
    + [(OX, None, 1)]
    + [(w, b, 1) for w in (OWN, OZ, OY, OX) for b in EDGE_OFFSETS]
    + [(OX, b, -1) for b in EDGE_OFFSETS]
)
SLOT = {product: index for index, product in enumerate(PRODUCTS)}
PADDED = -(-len(PRODUCTS) // SUB) * SUB


def routing_table():
    table = np.zeros((2, 6 * VALUES, 4 * PADDED), np.float32)
    for parity, sign_z in ((0, -1), (1, 1)):
        for n, (weight, toggled, sign_x) in enumerate(PRODUCTS):
            for half, sign_y in ((0, -1), (1, 1)):
                row = ((weight == OX) * sign_x, (weight == OZ) * sign_z, (weight == OY) * sign_y)
                if toggled is None:
                    value = RHS
                else:
                    column = (toggled[0] * sign_x, toggled[1] * sign_z, toggled[2] * sign_y)
                    o = [column[d] - row[d] for d in range(3)]
                    value = 9 * (o[0] + 1) + 3 * (o[1] + 1) + (o[2] + 1) - 13
                    if value < 0:
                        continue
                group = 2 * (weight == OY) + half
                target = (row[0] + 1) * 2 + (weight == OZ)
                table[parity, target * VALUES + value, group * PADDED + n] = 1.0
    return table


def split_dot(table, values, swap=False):
    total = None
    rest = values
    for _ in range(3):
        part = rest.astype(jnp.bfloat16)
        rest = rest - part.astype(jnp.float32)
        pair = (part, table) if swap else (table, part)
        term = jnp.dot(*pair, preferred_element_type=jnp.float32)
        total = term if total is None else total + term
    return total


def harmonic(a, b):
    return 2.0 * a * b / jnp.maximum(a + b, 1e-30)


def perm_of(classes):
    step = 5.0 / (CLASSES - 1)
    return jnp.exp(classes.astype(jnp.float32) * step - 2.5)


def sink_of(well, perm):
    return SINK_RATE * well.astype(jnp.float32) * perm


def kernel(
    tiles, layers, nx, ny,
    cls_hbm, well_hbm, src_hbm, route_hbm, out_ref,
    cls, well, src, route,
    kx, sk, zs, zr, crs, crr,
    typ_s, tzi_s, txf, tzm_s, tzp_s, d_s, own_s, oy_s, oz_s, ox_s, tz_edge, zb,
    zi, acc, part, fold, gsend, gath, gsum, csc,
    in_sem, x_send, x_recv, z_send, z_recv, c_send, c_recv, f_send, f_recv, g_send, g_recv,
):
    tile = lax.axis_index("tile")
    layer = lax.axis_index("layer")
    pairs = layers // 2
    pair = layer // 2
    parity = layer % 2
    cells = ny // EDGE
    span = pairs * cells
    rows = part.shape[1]
    plane = lambda i: pl.ds(i * SUB, SUB)

    loads = [
        pltpu.make_async_copy(a, b, in_sem.at[n])
        for n, (a, b) in enumerate(
            ((cls_hbm, cls), (well_hbm, well), (src_hbm, src), (route_hbm.at[parity], route))
        )
    ]
    for load in loads:
        load.start()

    barrier = pltpu.get_barrier_semaphore()
    me = tile * layers + layer

    def greet(k, carry):
        other = lax.rem(me + k, tiles * layers)
        pl.semaphore_signal(
            barrier, inc=1, device_id=(other // layers, other % layers), device_id_type=MESH
        )
        return carry

    lax.fori_loop(1, tiles * layers, greet, 0)

    loads[0].wait()
    loads[1].wait()

    for i in (0, 1, nx - 2, nx - 1):
        k = perm_of(cls[plane(i), :])
        kx[plane(i + 2), :] = k
        if i in (0, nx - 1):
            sk[plane(i + 1), :] = sink_of(well[plane(i), :], k)
    for side, (z1, z2) in enumerate(((0, 1), (SUB - 1, SUB - 2))):
        for i in range(nx):
            zi[0, pl.ds(i, 1), :] = cls[pl.ds(i * SUB + z1, 1), :]
            zi[1, pl.ds(i, 1), :] = cls[pl.ds(i * SUB + z2, 1), :]
            zi[2, pl.ds(i, 1), :] = well[pl.ds(i * SUB + z1, 1), :]
        k = perm_of(zi[0])
        zs[side, 0] = k
        zs[side, 1] = perm_of(zi[1])
        zs[side, 2] = sink_of(zi[2], k)
        crs[0 + side] = k[0:1, :]
        crs[2 + side] = k[nx - 1 : nx, :]

    pl.semaphore_wait(barrier, tiles * layers - 1)

    def halo_copies(sx):
        lo = sx < 0
        src_k = kx.at[pl.ds((2 if lo else nx) * SUB, 2 * SUB), :]
        dst_k = kx.at[pl.ds((nx + 2 if lo else 0) * SUB, 2 * SUB), :]
        src_s = sk.at[plane(1 if lo else nx), :]
        dst_s = sk.at[plane(nx + 1 if lo else 0), :]
        s = 0 if lo else 1
        return [
            pltpu.make_async_remote_copy(
                a, b, x_send.at[s, n], x_recv.at[s, n],
                device_id=(tile + sx, layer), device_id_type=MESH,
            )
            for n, (a, b) in enumerate(((src_k, dst_k), (src_s, dst_s)))
        ]

    def layer_copy(sz):
        s = 0 if sz < 0 else 1
        return pltpu.make_async_remote_copy(
            zs.at[s], zr.at[1 - s], z_send.at[s], z_recv.at[s],
            device_id=(tile, layer + sz), device_id_type=MESH,
        )

    def corner_copy(sx, sz):
        a, b = (0 if sx < 0 else 1), (0 if sz < 0 else 1)
        return pltpu.make_async_remote_copy(
            crs.at[2 * a + b], crr.at[2 * (1 - a) + (1 - b)],
            c_send.at[2 * a + b], c_recv.at[2 * a + b],
            device_id=(tile + sx, layer + sz), device_id_type=MESH,
        )

    def has(sx, sz):
        ok = None
        for s, at, count in ((sx, tile, tiles), (sz, layer, layers)):
            if s:
                test = at > 0 if s < 0 else at < count - 1
                ok = test if ok is None else ok & test
        return ok

    sides = (-1, 1)
    diagonals = [(sx, sz) for sx in sides for sz in sides]
    for sz in sides:
        @pl.when(has(0, sz))
        def _():
            layer_copy(sz).start()

        @pl.when(jnp.logical_not(has(0, sz)))
        def _():
            zr[0 if sz < 0 else 1] = jnp.zeros(zr.shape[1:], jnp.float32)
    for sx in sides:
        @pl.when(has(sx, 0))
        def _():
            for copy in halo_copies(sx):
                copy.start()

        @pl.when(jnp.logical_not(has(sx, 0)))
        def _():
            first = 0 if sx < 0 else nx + 2
            kx[pl.ds(first * SUB, 2 * SUB), :] = jnp.zeros((2 * SUB, ny), jnp.float32)
            sk[plane(0 if sx < 0 else nx + 1), :] = jnp.zeros((SUB, ny), jnp.float32)
    for sx, sz in diagonals:
        @pl.when(has(sx, sz))
        def _():
            corner_copy(sx, sz).start()

        @pl.when(jnp.logical_not(has(sx, sz)))
        def _():
            crr[2 * (0 if sx < 0 else 1) + (0 if sz < 0 else 1)] = jnp.zeros((1, ny), jnp.float32)

    sub = lax.broadcasted_iota(jnp.int32, (SUB, ny), 0)
    lane = lax.broadcasted_iota(jnp.int32, (SUB, ny), 1)
    even = parity == 0
    cross_ym = lane % EDGE == 0
    cross_yp = lane % EDGE == EDGE - 1
    cross_zm = (sub == 0) & even
    cross_zp = (sub == SUB - 1) & jnp.logical_not(even)

    def up(a, dim):
        return pltpu.roll(a, 1, dim)

    def down(a, dim):
        return pltpu.roll(a, a.shape[dim] - 1, dim)

    def y_face(k):
        at = lax.broadcasted_iota(jnp.int32, k.shape, 1)
        return jnp.where(at == ny - 1, 0.0, harmonic(k, down(k, 1)))

    def only(mask, a):
        return jnp.where(mask, a, 0.0)

    for i in range(2, nx - 2):
        k = perm_of(cls[plane(i), :])
        kx[plane(i + 2), :] = k
        sk[plane(i + 1), :] = sink_of(well[plane(i), :], k)
    for i in (1, nx - 2):
        sk[plane(i + 1), :] = sink_of(well[plane(i), :], kx[plane(i + 2), :])

    def faces(i):
        at = plane(i)
        k = kx[plane(i + 2), :]
        typ_s[at, :] = y_face(k)
        tzi_s[at, :] = VERTICAL_RATIO * harmonic(k, up(k, 0))

        if i > 0:
            txf[at, :] = harmonic(kx[plane(i + 1), :], k)

    for i in range(nx):
        faces(i)

    for sz in sides:
        @pl.when(has(0, sz))
        def _():
            layer_copy(-sz).wait_recv()
    for sx in sides:
        @pl.when(has(sx, 0))
        def _():
            for copy in halo_copies(-sx):
                copy.wait_recv()
    for sx, sz in diagonals:
        @pl.when(has(sx, sz))
        def _():
            corner_copy(-sx, -sz).wait_recv()

    def basis(sink, faces, crossing):
        diagonal = sink
        for pair_of in faces:
            diagonal = diagonal + pair_of[0] + pair_of[1]
        inverse = FINE_DAMPING / jnp.maximum(diagonal, 1e-30)
        leaving = sink
        for term in crossing:
            if term is not None:
                leaving = leaving + term
        outer = [None if term is None else term * inverse for term in crossing]
        return diagonal, 1.0 - leaving * inverse, outer

    for side in (0, 1):
        k0 = kx[plane(2 if side == 0 else nx + 1), :]
        k1 = kx[plane(1 if side == 0 else nx + 2), :]
        k2 = kx[plane(0 if side == 0 else nx + 3), :]
        toward = harmonic(k0, k1)
        txf[plane(0 if side == 0 else nx), :] = toward
        inner = VERTICAL_RATIO * harmonic(k1, up(k1, 0))
        tzm = jnp.where(sub == 0, VERTICAL_RATIO * harmonic(k1, crr[2 * side]), inner)
        tzp = jnp.where(
            sub == SUB - 1, VERTICAL_RATIO * harmonic(k1, crr[2 * side + 1]), down(inner, 0)
        )
        typ = y_face(k1)
        tym = up(typ, 1)
        crossing = (
            toward,
            only(cross_zm, tzm) + only(cross_zp, tzp),
            only(cross_ym, tym) + only(cross_yp, typ),
        )
        _, own, outer = basis(
            sk[plane(0 if side == 0 else nx + 1), :],
            ((toward, harmonic(k1, k2)), (tzm, tzp), (tym, typ)),
            crossing,
        )
        at = plane(0 if side == 0 else nx + 1)
        own_s[at, :] = own
        ox_s[plane(0 if side == 0 else 3), :] = outer[0]
        oz_s[at, :] = outer[1]
        oy_s[at, :] = outer[2]

    wide_row = lax.broadcasted_iota(jnp.int32, (nx, ny), 0)
    wide_lane = lax.broadcasted_iota(jnp.int32, (nx, ny), 1)
    for side in (0, 1):
        k0 = zs[side, 0]
        k1 = zr[side, 0]
        k2 = zr[side, 1]
        toward = VERTICAL_RATIO * harmonic(k0, k1)
        tz_edge[side] = toward
        inner = harmonic(k1, up(k1, 0))
        txm = jnp.where(wide_row == 0, harmonic(k1, crr[side]), inner)
        txp = jnp.where(wide_row == nx - 1, harmonic(k1, crr[2 + side]), down(inner, 0))
        typ = y_face(k1)
        tym = up(typ, 1)
        crosses = even if side == 0 else jnp.logical_not(even)
        crossing = (
            only(wide_row == 0, txm) + only(wide_row == nx - 1, txp),
            toward * crosses.astype(jnp.float32),
            only(wide_lane % EDGE == 0, tym) + only(wide_lane % EDGE == EDGE - 1, typ),
        )
        _, own, outer = basis(
            zr[side, 2],
            ((txm, txp), (toward, VERTICAL_RATIO * harmonic(k1, k2)), (tym, typ)),
            crossing,
        )
        zb[side, OWN] = own
        zb[side, OX] = outer[0]
        zb[side, OZ] = outer[1]
        zb[side, OY] = outer[2]

    def block_basis(i, edge):
        at = plane(i)
        after = plane(i + 1)
        inner = tzi_s[at, :]
        tzm = jnp.where(sub == 0, tz_edge[0, pl.ds(i, 1), :], inner)
        tzp = jnp.where(sub == SUB - 1, tz_edge[1, pl.ds(i, 1), :], down(inner, 0))
        txm = txf[at, :]
        txp = txf[after, :]
        typ = typ_s[at, :]
        tym = up(typ, 1)
        crossing = (
            None if edge == 0 else (txm if edge < 0 else txp),
            only(cross_zm, tzm) + only(cross_zp, tzp),
            only(cross_ym, tym) + only(cross_yp, typ),
        )
        diagonal, own, outer = basis(
            sk[after, :], ((txm, txp), (tzm, tzp), (tym, typ)), crossing
        )
        tzm_s[at, :] = tzm
        tzp_s[at, :] = tzp
        d_s[at, :] = diagonal
        own_s[after, :] = own
        oz_s[after, :] = outer[1]
        oy_s[after, :] = outer[2]
        if edge:
            ox_s[plane(1 if edge < 0 else 2), :] = outer[0]

    for i in range(nx):
        block_basis(i, -1 if i == 0 else int(i == nx - 1))

    loads[2].wait()
    loads[3].wait()

    acc[...] = jnp.zeros(acc.shape, jnp.float32)

    def add(product, term):
        at = plane(SLOT[product])
        acc[at, :] = acc[at, :] + term

    def products(i, edge):
        at = plane(i)
        mid = plane(i + 1)
        after = plane(i + 2)
        row = pl.ds(i, 1)
        diagonal, tzm, tzp, typ = d_s[at, :], tzm_s[at, :], tzp_s[at, :], typ_s[at, :]
        tym = up(typ, 1)
        txm, txp = txf[at, :], txf[mid, :]
        own, oz, oy = own_s[mid, :], oz_s[mid, :], oy_s[mid, :]
        source = src[at, :]

        def z_before(a, kind):
            return jnp.where(sub == 0, zb[0, kind, row, :], up(a, 0))

        def z_after(a, kind):
            return jnp.where(sub == SUB - 1, zb[1, kind, row, :], down(a, 0))

        own_ym, own_yp, oy_ym, oy_yp = up(own, 1), down(own, 1), up(oy, 1), down(oy, 1)
        oz_ym, oz_yp = up(oz, 1), down(oz, 1)
        own_zm, own_zp = z_before(own, OWN), z_after(own, OWN)
        oy_zm, oy_zp = z_before(oy, OY), z_after(oy, OY)
        oz_zm, oz_zp = z_before(oz, OZ), z_after(oz, OZ)
        tymc, typc = only(cross_ym, tym), only(cross_yp, typ)
        tzmc, tzpc = only(cross_zm, tzm), only(cross_zp, tzp)
        tymn, typn, tzmn, tzpn = tym - tymc, typ - typc, tzm - tzmc, tzp - tzpc
        before_own = ox_s[plane(0), :] if edge < 0 else own_s[at, :]
        after_own = ox_s[plane(3), :] if edge > 0 else own_s[after, :]
        q0 = (
            diagonal * own - txm * before_own - txp * after_own
            - tymc * oy_ym - tymn * own_ym - typc * oy_yp - typn * own_yp
            - tzmc * oz_zm - tzmn * own_zm - tzpc * oz_zp - tzpn * own_zp
        )
        qy = (
            diagonal * oy - tymc * own_ym - tymn * oy_ym - typc * own_yp - typn * oy_yp
            - tzmn * oy_zm - tzpn * oy_zp
        )
        qz = (
            diagonal * oz - tzmc * own_zm - tzmn * oz_zm - tzpc * own_zp - tzpn * oz_zp
            - tymn * oz_ym - typn * oz_yp
        )
        if edge >= 0:
            qy = qy - txm * oy_s[at, :]
            qz = qz - txm * oz_s[at, :]
        if edge <= 0:
            qy = qy - txp * oy_s[after, :]
            qz = qz - txp * oz_s[after, :]
        qzy = -(tymc * oz_ym + typc * oz_yp + tzmc * oy_zm + tzpc * oy_zp)
        fields = list(zip(FULL_OFFSETS, (q0, qy, qz, qzy, source)))
        weights = ((OWN, own), (OZ, oz), (OY, oy))
        for kind, weight in weights:
            for offset, field in fields:
                add((kind, offset, 0), weight * field)
        if not edge:
            return
        ox = ox_s[plane(1 if edge < 0 else 2), :]
        if edge < 0:
            for offset, field in fields:
                add((OX, offset, -1), ox * field)
            across, t_across = plane(0), txm
        else:
            add((OX, None, 1), ox * source)
            across, t_across = plane(nx + 1), txp
        ox_ym, ox_yp = up(ox, 1), down(ox, 1)
        ox_zm, ox_zp = z_before(ox, OX), z_after(ox, OX)
        qx = (
            diagonal * ox - t_across * own_s[across, :]
            - tymn * ox_ym - typn * ox_yp - tzmn * ox_zm - tzpn * ox_zp
        )
        qxy = -(t_across * oy_s[across, :] + tymc * ox_ym + typc * ox_yp)
        qxz = -(t_across * oz_s[across, :] + tzmc * ox_zm + tzpc * ox_zp)
        for offset, field in zip(EDGE_OFFSETS, (qx, qxy, qxz)):
            add((OX, offset, edge), ox * field)
            if edge > 0:
                for kind, weight in weights:
                    add((kind, offset, 1), weight * field)
        if edge > 0:
            inward = -txm * ox
            for kind, ref in ((OWN, own_s), (OZ, oz_s), (OY, oy_s)):
                add((kind, EDGE_OFFSETS[0], 1), ref[at, :] * inward)

    for i in range(nx):
        products(i, -1 if i == 0 else int(i == nx - 1))

    fine = lax.broadcasted_iota(jnp.int32, (ny, LANES), 0)
    spot = lax.broadcasted_iota(jnp.int32, (ny, LANES), 1)
    group = spot // cells
    upper = group % 2
    wanted = fine // EDGE + jnp.where(group >= 2, 2 * upper - 1, 0)
    hit = (fine // HALF % 2 == upper) & (wanted == spot % cells) & (group < 4)
    gather = jnp.where(hit, 1.0, 0.0).astype(jnp.bfloat16)
    halves = split_dot(gather, acc[...], swap=True)
    sums = halves.reshape(PADDED, SUB, LANES).sum(axis=1)
    stacked = jnp.concatenate(
        [sums] + [pltpu.roll(sums, LANES - g * cells, 1) for g in (1, 2, 3)], axis=0
    )
    routed = split_dot(route[...], stacked)
    routed = jnp.where(
        lax.broadcasted_iota(jnp.int32, routed.shape, 1) < cells, routed, 0.0
    )
    beside_pair = pair + 2 * parity - 1
    near_pair = jnp.clip(beside_pair, 0, pairs - 1)
    for target in range(6):
        block = routed[target * VALUES : (target + 1) * VALUES, :]
        if rows < VALUES:
            block = block[:rows, :] + pltpu.roll(block[rows:, :], span, 1)
        to_pair = near_pair if target % 2 else pair
        part[target] = pltpu.roll(block, to_pair * cells, 1)

    def fold_copy(sx, beside, which):
        to_pair = beside_pair if beside else pair
        role = layer - 2 * to_pair + 1
        slot = (1 - sx) * 4 + role
        n = ((sx + 1) * 2 + beside) * 2 + which
        return pltpu.make_async_remote_copy(
            part.at[(sx + 1) * 2 + beside], fold.at[slot], f_send.at[n], f_recv.at[slot],
            device_id=(tile + sx, 2 * to_pair + which), device_id_type=MESH,
        )

    def fold_valid(sx, beside, which):
        ok = (tile + sx >= 0) & (tile + sx < tiles)
        if beside:
            return ok & (beside_pair >= 0) & (beside_pair < pairs)
        return ok if sx else ok & (which != parity)

    fold_list = [(sx, b, w) for b in (1, 0) for sx in (-1, 1, 0) for w in (0, 1)]
    for item in fold_list:
        @pl.when(fold_valid(*item))
        def _():
            fold_copy(*item).start()

    gsend[...] = part[2]
    for dt in (-1, 0, 1):
        for role in range(4):
            from_layer = 2 * pair - 1 + role
            ok = (tile + dt >= 0) & (tile + dt < tiles)
            ok = ok & (from_layer >= 0) & (from_layer < layers)
            if dt == 0:
                ok = ok & (from_layer != layer)
            slot = (dt + 1) * 4 + role

            @pl.when(ok)
            def _():
                pltpu.make_async_remote_copy(
                    part.at[0], fold.at[slot], f_send.at[0], f_recv.at[slot],
                    device_id=(tile, layer), device_id_type=MESH,
                ).wait_recv()
                gsend[...] = gsend[...] + fold[slot]

    def gather_copy(k):
        other = lax.rem(tile * pairs + pair + k, tiles * pairs)
        return pltpu.make_async_remote_copy(
            gsend, gath.at[tile * pairs + pair], g_send.at[k], g_recv.at[tile * pairs + pair],
            device_id=(other // pairs, 2 * (other % pairs) + parity), device_id_type=MESH,
        )

    for k in range(1, tiles * pairs):
        gather_copy(k).start()
    gath[tile * pairs + pair] = gsend[...]

    cell_at = lax.broadcasted_iota(jnp.int32, (LANES, ny), 0)
    fine_at = lax.broadcasted_iota(jnp.int32, (LANES, ny), 1)
    parent = fine_at // EDGE
    spread = jnp.where(cell_at == parent, 1.0, 0.0).astype(jnp.bfloat16)
    beside_y = parent + 2 * (fine_at // HALF % 2) - 1
    spread_y = jnp.where(cell_at == beside_y, 1.0, 0.0).astype(jnp.bfloat16)

    for k in range(1, tiles * pairs):
        frm = lax.rem(tile * pairs + pair + tiles * pairs - k, tiles * pairs)
        pltpu.make_async_remote_copy(
            gsend, gath.at[frm], g_send.at[k], g_recv.at[frm],
            device_id=(tile, layer), device_id_type=MESH,
        ).wait_recv()

    for t in range(tiles):
        total = gath[t * pairs]
        for p in range(1, pairs):
            total = total + gath[t * pairs + p]
        gsum[pl.ds(t * rows, rows), :] = total
    lane_t = lax.broadcasted_iota(jnp.int32, (tiles, LANES), 1)

    def value(v):
        a = gsum[pl.ds(v % rows, tiles, stride=rows), :]
        if v >= rows:
            a = pltpu.roll(a, LANES - span, 1)
        return only(lane_t < span, a)

    def shifted(a, offset):
        ox, oz, oy = offset
        along = -(oz * cells + oy) % LANES
        if along:
            a = pltpu.roll(a, along, 1)
        if ox:
            a = pltpu.roll(a, -ox % tiles, 0)
        return a

    offsets = [((v + 13) // 9 - 1, (v + 13) // 3 % 3 - 1, (v + 13) % 3 - 1) for v in range(14)]
    forward = [value(v) for v in range(14)]
    backward = [
        shifted(forward[v], [-d for d in offsets[v]]) if v else None for v in range(14)
    ]
    rhs = value(RHS)
    scale = COARSE_DAMPING / jnp.where(lane_t < span, forward[0], 1.0)
    coarse = rhs * scale
    for _ in range(SWEEPS - 1):
        applied = forward[0] * coarse
        for v in range(1, 14):
            applied = applied + forward[v] * shifted(coarse, offsets[v])
            applied = applied + backward[v] * shifted(coarse, [-d for d in offsets[v]])
        coarse = coarse + (rhs - applied) * scale
    csc[...] = coarse

    def coarse_row(t, p):
        a = jnp.broadcast_to(csc[pl.ds(t, 1), :], (SUB, LANES))
        return pltpu.roll(a, (LANES - p * cells) % LANES, 1)

    center = coarse_row(tile, pair)
    four = jnp.concatenate(
        [
            center,
            coarse_row(tile, near_pair),
            coarse_row(jnp.maximum(tile - 1, 0), pair),
            coarse_row(jnp.minimum(tile + 1, tiles - 1), pair),
        ],
        axis=0,
    )
    wide = split_dot(spread, four, swap=True)
    c_own, c_z = wide[:SUB, :], wide[SUB : 2 * SUB, :]
    c_y = split_dot(spread_y, center, swap=True)
    for i in range(nx):
        at = plane(i + 1)
        result = own_s[at, :] * c_own + oz_s[at, :] * c_z + oy_s[at, :] * c_y
        if i == 0:
            result = result + ox_s[plane(1), :] * wide[2 * SUB : 3 * SUB, :]
        if i == nx - 1:
            result = result + ox_s[plane(2), :] * wide[3 * SUB :, :]
        out_ref[plane(i), :] = result

    for sz in sides:
        @pl.when(has(0, sz))
        def _():
            layer_copy(sz).wait_send()
    for sx in sides:
        @pl.when(has(sx, 0))
        def _():
            for copy in halo_copies(sx):
                copy.wait_send()
    for sx, sz in diagonals:
        @pl.when(has(sx, sz))
        def _():
            corner_copy(sx, sz).wait_send()
    for item in fold_list:
        @pl.when(fold_valid(*item))
        def _():
            fold_copy(*item).wait_send()
    for k in range(1, tiles * pairs):
        gather_copy(k).wait_send()


def body(tiles, layers, classes, well_mask, source):
    nx, nz, ny = classes.shape
    assert nx == EDGE and nz == HALF == SUB and layers % 2 == 0
    cells, pairs = ny // EDGE, layers // 2
    assert 4 * cells <= LANES and pairs * cells <= LANES
    rows = VALUES // 2 if 2 * pairs * cells <= LANES else VALUES
    flat = lambda a: a.reshape(nx * nz, ny)
    f32 = lambda *shape: pltpu.VMEM(shape, jnp.float32)
    dma = pltpu.SemaphoreType.DMA
    block = (nx * SUB, ny)
    wide = ((nx + 2) * SUB, ny)
    scratch = [
        pltpu.VMEM(block, jnp.int32), pltpu.VMEM(block, jnp.int32), f32(*block),
        pltpu.VMEM((6 * VALUES, 4 * PADDED), jnp.bfloat16),
        f32((nx + 4) * SUB, ny), f32(*wide), f32(2, 3, nx, ny), f32(2, 3, nx, ny),
        f32(4, 1, ny), f32(4, 1, ny),
        f32(*block), f32(*block), f32((nx + 1) * SUB, ny), f32(*block), f32(*block), f32(*block),
        f32(*wide), f32(*wide), f32(*wide), f32(4 * SUB, ny), f32(2, nx, ny), f32(2, 4, nx, ny),
        pltpu.VMEM((3, nx, ny), jnp.int32), f32(PADDED * SUB, ny), f32(6, rows, LANES), f32(12, rows, LANES), f32(rows, LANES),
        f32(tiles * pairs, rows, LANES), f32(tiles * rows, LANES), f32(tiles, LANES),
        dma((4,)), dma((2, 2)), dma((2, 2)), dma((2,)), dma((2,)), dma((4,)), dma((4,)),
        dma((12,)), dma((12,)), dma((tiles * pairs,)), dma((tiles * pairs,)),
    ]
    route = jnp.asarray(routing_table(), jnp.bfloat16)
    result = pl.pallas_call(
        functools.partial(kernel, tiles, layers, nx, ny),
        out_shape=jax.ShapeDtypeStruct(block, jnp.float32),
        in_specs=[pl.BlockSpec(memory_space=pltpu.HBM)] * 4,
        out_specs=pl.BlockSpec(memory_space=pltpu.VMEM),
        scratch_shapes=scratch,
        compiler_params=pltpu.CompilerParams(
            collective_id=0, has_side_effects=True, vmem_limit_bytes=60 * 2**20
        ),
    )(flat(classes), flat(well_mask), flat(source), route)
    return result.reshape(nx, nz, ny)


def solution(mesh):
    spec = P("tile", "layer", None)
    return jax.shard_map(
        functools.partial(body, mesh.shape["tile"], mesh.shape["layer"]),
        mesh=mesh, in_specs=(spec, spec, spec), out_specs=spec, check_vma=False,
    )
```

```python
import functools

import jax
import jax.numpy as jnp
import numpy as np
from jax import lax
from jax.experimental import pallas as pl
from jax.experimental.pallas import tpu as pltpu
from jax.sharding import PartitionSpec as P

EDGE = 16
HALF = EDGE // 2
CLASSES = 16
SWEEPS = 4
FINE_DAMPING = 0.67
COARSE_DAMPING = 0.5
SINK_RATE = 0.5
VERTICAL_RATIO = 0.25
LANES = 128
SUB = 8
VALUES = 16
RHS = 14
MESH = pl.DeviceIdType.MESH

OWN, OX, OZ, OY = range(4)
FULL_OFFSETS = ((0, 0, 0), (0, 0, 1), (0, 1, 0), (0, 1, 1), None)
EDGE_OFFSETS = ((1, 0, 0), (1, 0, 1), (1, 1, 0))
PRODUCTS = (
    [(w, b, 0) for w in (OWN, OZ, OY) for b in FULL_OFFSETS]
    + [(OX, b, -1) for b in FULL_OFFSETS]
    + [(OX, None, 1)]
    + [(w, b, 1) for w in (OWN, OZ, OY, OX) for b in EDGE_OFFSETS]
    + [(OX, b, -1) for b in EDGE_OFFSETS]
)
SLOT = {product: index for index, product in enumerate(PRODUCTS)}
PADDED = -(-len(PRODUCTS) // SUB) * SUB


def routing_table():
    table = np.zeros((2, 6 * VALUES, 4 * PADDED), np.float32)
    for parity, sign_z in ((0, -1), (1, 1)):
        for n, (weight, toggled, sign_x) in enumerate(PRODUCTS):
            for half, sign_y in ((0, -1), (1, 1)):
                row = ((weight == OX) * sign_x, (weight == OZ) * sign_z, (weight == OY) * sign_y)
                if toggled is None:
                    value = RHS
                else:
                    column = (toggled[0] * sign_x, toggled[1] * sign_z, toggled[2] * sign_y)
                    o = [column[d] - row[d] for d in range(3)]
                    value = 9 * (o[0] + 1) + 3 * (o[1] + 1) + (o[2] + 1) - 13
                    if value < 0:
                        continue
                group = 2 * (weight == OY) + half
                target = (row[0] + 1) * 2 + (weight == OZ)
                table[parity, target * VALUES + value, group * PADDED + n] = 1.0
    return table


def split_dot(table, values, swap=False):
    total = None
    rest = values
    for _ in range(2):
        part = rest.astype(jnp.bfloat16)
        rest = rest - part.astype(jnp.float32)
        pair = (part, table) if swap else (table, part)
        term = jnp.dot(*pair, preferred_element_type=jnp.float32)
        total = term if total is None else total + term
    return total


def harmonic(a, b):
    return 2.0 * a * b / jnp.maximum(a + b, 1e-30)


def perm_of(classes):
    step = 5.0 / (CLASSES - 1)
    return jnp.exp(classes.astype(jnp.float32) * step - 2.5)


def sink_of(well, perm):
    return SINK_RATE * well.astype(jnp.float32) * perm


def kernel(
    tiles, layers, nx, ny,
    cls_hbm, well_hbm, src_hbm, route_hbm, out_ref,
    cls, well, src, route,
    kx, sk, zs, zr, crs, crr, zq, ze,
    typ_s, tzi_s, txf, tzm_s, tzp_s, d_s, own_s, oy_s, oz_s, ox_s, tz_edge, zb,
    zi, acc, part, fold, gsend, gath, gsum, csc,
    in_sem, x_send, x_recv, z_send, z_recv, c_send, c_recv, f_send, f_recv, g_send, g_recv,
):
    tile = lax.axis_index("tile")
    layer = lax.axis_index("layer")
    pairs = layers // 2
    pair = layer // 2
    parity = layer % 2
    cells = ny // EDGE
    span = pairs * cells
    rows = part.shape[1]
    plane = lambda i: pl.ds(i * SUB, SUB)

    loads = [
        pltpu.make_async_copy(a, b, in_sem.at[n])
        for n, (a, b) in enumerate(
            ((cls_hbm, cls), (well_hbm, well), (src_hbm, src), (route_hbm.at[parity], route))
        )
    ]
    for load in loads:
        load.start()

    barrier = pltpu.get_barrier_semaphore()
    for a in range(tiles):
        for b in range(layers):
            if a or b:
                pl.semaphore_signal(
                    barrier, inc=1, device_id_type=MESH,
                    device_id=(lax.rem(tile + a, tiles), lax.rem(layer + b, layers)),
                )

    def fold_from(dt, role):
        from_layer = 2 * pair - 1 + role
        ok = (tile + dt >= 0) & (tile + dt < tiles)
        ok = ok & (from_layer >= 0) & (from_layer < layers)
        return ok & (from_layer != layer) if dt == 0 else ok

    for dt in (-1, 0, 1):
        for role in range(4):
            @pl.when(jnp.logical_not(fold_from(dt, role)))
            def _():
                fold[(dt + 1) * 4 + role] = jnp.zeros(fold.shape[1:], jnp.float32)

    loads[0].wait()
    loads[1].wait()

    for i in (0, 1, nx - 2, nx - 1):
        k = perm_of(cls[plane(i), :])
        kx[plane(i + 2), :] = k
        if i in (0, nx - 1):
            sk[plane(i + 1), :] = sink_of(well[plane(i), :], k)
    for side, (z1, z2) in enumerate(((0, 1), (SUB - 1, SUB - 2))):
        for i in range(nx):
            zi[0, pl.ds(i, 1), :] = cls[pl.ds(i * SUB + z1, 1), :]
            zi[1, pl.ds(i, 1), :] = cls[pl.ds(i * SUB + z2, 1), :]
            zi[2, pl.ds(i, 1), :] = well[pl.ds(i * SUB + z1, 1), :]
        k = perm_of(zi[0])
        zs[side, 0] = k
        zs[side, 1] = perm_of(zi[1])
        zs[side, 2] = sink_of(zi[2], k)
        crs[0 + side] = k[0:1, :]
        crs[2 + side] = k[nx - 1 : nx, :]

    pl.semaphore_wait(barrier, tiles * layers - 1)

    def halo_copies(sx):
        lo = sx < 0
        src_k = kx.at[pl.ds((2 if lo else nx) * SUB, 2 * SUB), :]
        dst_k = kx.at[pl.ds((nx + 2 if lo else 0) * SUB, 2 * SUB), :]
        src_s = sk.at[plane(1 if lo else nx), :]
        dst_s = sk.at[plane(nx + 1 if lo else 0), :]
        s = 0 if lo else 1
        return [
            pltpu.make_async_remote_copy(
                a, b, x_send.at[s, n], x_recv.at[s, n],
                device_id=(tile + sx, layer), device_id_type=MESH,
            )
            for n, (a, b) in enumerate(((src_k, dst_k), (src_s, dst_s)))
        ]

    def layer_copy(sz):
        s = 0 if sz < 0 else 1
        return pltpu.make_async_remote_copy(
            zs.at[s], zr.at[1 - s], z_send.at[s], z_recv.at[s],
            device_id=(tile, layer + sz), device_id_type=MESH,
        )

    def corner_copy(sx, sz):
        a, b = (0 if sx < 0 else 1), (0 if sz < 0 else 1)
        return pltpu.make_async_remote_copy(
            crs.at[2 * a + b], crr.at[2 * (1 - a) + (1 - b)],
            c_send.at[2 * a + b], c_recv.at[2 * a + b],
            device_id=(tile + sx, layer + sz), device_id_type=MESH,
        )

    def has(sx, sz):
        ok = None
        for s, at, count in ((sx, tile, tiles), (sz, layer, layers)):
            if s:
                test = at > 0 if s < 0 else at < count - 1
                ok = test if ok is None else ok & test
        return ok

    sides = (-1, 1)
    diagonals = [(sx, sz) for sx in sides for sz in sides]
    for sz in sides:
        @pl.when(has(0, sz))
        def _():
            layer_copy(sz).start()

        @pl.when(jnp.logical_not(has(0, sz)))
        def _():
            zr[0 if sz < 0 else 1] = jnp.zeros(zr.shape[1:], jnp.float32)
    for sx in sides:
        @pl.when(has(sx, 0))
        def _():
            for copy in halo_copies(sx):
                copy.start()

        @pl.when(jnp.logical_not(has(sx, 0)))
        def _():
            first = 0 if sx < 0 else nx + 2
            kx[pl.ds(first * SUB, 2 * SUB), :] = jnp.zeros((2 * SUB, ny), jnp.float32)
            sk[plane(0 if sx < 0 else nx + 1), :] = jnp.zeros((SUB, ny), jnp.float32)
    for sx, sz in diagonals:
        @pl.when(has(sx, sz))
        def _():
            corner_copy(sx, sz).start()

        @pl.when(jnp.logical_not(has(sx, sz)))
        def _():
            crr[2 * (0 if sx < 0 else 1) + (0 if sz < 0 else 1)] = jnp.zeros((1, ny), jnp.float32)

    sub = lax.broadcasted_iota(jnp.int32, (SUB, ny), 0)
    lane = lax.broadcasted_iota(jnp.int32, (SUB, ny), 1)
    even = parity == 0
    cross_ym = lane % EDGE == 0
    cross_yp = lane % EDGE == EDGE - 1
    cross_zm = (sub == 0) & even
    cross_zp = (sub == SUB - 1) & jnp.logical_not(even)

    def up(a, dim):
        return pltpu.roll(a, 1, dim)

    def down(a, dim):
        return pltpu.roll(a, a.shape[dim] - 1, dim)

    def y_face(k):
        at = lax.broadcasted_iota(jnp.int32, k.shape, 1)
        return jnp.where(at == ny - 1, 0.0, harmonic(k, down(k, 1)))

    def only(mask, a):
        return jnp.where(mask, a, 0.0)

    for i in range(2, nx - 2):
        k = perm_of(cls[plane(i), :])
        kx[plane(i + 2), :] = k
        sk[plane(i + 1), :] = sink_of(well[plane(i), :], k)
    for i in (1, nx - 2):
        sk[plane(i + 1), :] = sink_of(well[plane(i), :], kx[plane(i + 2), :])

    def faces(i):
        at = plane(i)
        k = kx[plane(i + 2), :]
        typ_s[at, :] = y_face(k)
        tzi_s[at, :] = VERTICAL_RATIO * harmonic(k, up(k, 0))

        if i > 0:
            txf[at, :] = harmonic(kx[plane(i + 1), :], k)

    for i in range(nx):
        faces(i)

    for sz in sides:
        @pl.when(has(0, sz))
        def _():
            layer_copy(-sz).wait_recv()
    for sx in sides:
        @pl.when(has(sx, 0))
        def _():
            for copy in halo_copies(-sx):
                copy.wait_recv()
    for sx, sz in diagonals:
        @pl.when(has(sx, sz))
        def _():
            corner_copy(-sx, -sz).wait_recv()

    def basis(sink, faces, crossing):
        diagonal = sink
        for pair_of in faces:
            diagonal = diagonal + pair_of[0] + pair_of[1]
        inverse = FINE_DAMPING / jnp.maximum(diagonal, 1e-30)
        leaving = sink
        for term in crossing:
            if term is not None:
                leaving = leaving + term
        outer = [None if term is None else term * inverse for term in crossing]
        return diagonal, 1.0 - leaving * inverse, outer

    for side in (0, 1):
        k0 = kx[plane(2 if side == 0 else nx + 1), :]
        k1 = kx[plane(1 if side == 0 else nx + 2), :]
        k2 = kx[plane(0 if side == 0 else nx + 3), :]
        toward = harmonic(k0, k1)
        txf[plane(0 if side == 0 else nx), :] = toward
        inner = VERTICAL_RATIO * harmonic(k1, up(k1, 0))
        tzm = jnp.where(sub == 0, VERTICAL_RATIO * harmonic(k1, crr[2 * side]), inner)
        tzp = jnp.where(
            sub == SUB - 1, VERTICAL_RATIO * harmonic(k1, crr[2 * side + 1]), down(inner, 0)
        )
        typ = y_face(k1)
        tym = up(typ, 1)
        crossing = (
            toward,
            only(cross_zm, tzm) + only(cross_zp, tzp),
            only(cross_ym, tym) + only(cross_yp, typ),
        )
        _, own, outer = basis(
            sk[plane(0 if side == 0 else nx + 1), :],
            ((toward, harmonic(k1, k2)), (tzm, tzp), (tym, typ)),
            crossing,
        )
        at = plane(0 if side == 0 else nx + 1)
        own_s[at, :] = own
        ox_s[plane(0 if side == 0 else 3), :] = outer[0]
        oz_s[at, :] = outer[1]
        oy_s[at, :] = outer[2]

    wide_row = lax.broadcasted_iota(jnp.int32, (nx, ny), 0)
    wide_lane = lax.broadcasted_iota(jnp.int32, (nx, ny), 1)
    for side in (0, 1):
        k0 = zs[side, 0]
        k1 = zr[side, 0]
        k2 = zr[side, 1]
        toward = VERTICAL_RATIO * harmonic(k0, k1)
        tz_edge[side] = toward
        inner = harmonic(k1, up(k1, 0))
        txm = jnp.where(wide_row == 0, harmonic(k1, crr[side]), inner)
        txp = jnp.where(wide_row == nx - 1, harmonic(k1, crr[2 + side]), down(inner, 0))
        typ = y_face(k1)
        tym = up(typ, 1)
        crosses = even if side == 0 else jnp.logical_not(even)
        crossing = (
            only(wide_row == 0, txm) + only(wide_row == nx - 1, txp),
            toward * crosses.astype(jnp.float32),
            only(wide_lane % EDGE == 0, tym) + only(wide_lane % EDGE == EDGE - 1, typ),
        )
        _, own, outer = basis(
            zr[side, 2],
            ((txm, txp), (toward, VERTICAL_RATIO * harmonic(k1, k2)), (tym, typ)),
            crossing,
        )
        zb[side, OWN] = own
        zb[side, OX] = outer[0]
        zb[side, OZ] = outer[1]
        zb[side, OY] = outer[2]
        zq[side, 0] = jnp.where(crosses, outer[1], own)
        zq[side, 1] = jnp.where(crosses, 0.0, outer[2])

    def block_basis(i, edge):
        at = plane(i)
        after = plane(i + 1)
        inner = tzi_s[at, :]
        tzm = jnp.where(sub == 0, tz_edge[0, pl.ds(i, 1), :], inner)
        tzp = jnp.where(sub == SUB - 1, tz_edge[1, pl.ds(i, 1), :], down(inner, 0))
        txm = txf[at, :]
        txp = txf[after, :]
        typ = typ_s[at, :]
        tym = up(typ, 1)
        crossing = (
            None if edge == 0 else (txm if edge < 0 else txp),
            only(cross_zm, tzm) + only(cross_zp, tzp),
            only(cross_ym, tym) + only(cross_yp, typ),
        )
        diagonal, own, outer = basis(
            sk[after, :], ((txm, txp), (tzm, tzp), (tym, typ)), crossing
        )
        tzm_s[at, :] = tzm
        tzp_s[at, :] = tzp
        d_s[at, :] = diagonal
        own_s[after, :] = own
        if i >= nx - 2:
            oz_s[after, :] = outer[1]
        oy_s[after, :] = outer[2]
        if edge:
            ox_s[plane(1 if edge < 0 else 2), :] = outer[0]

    for i in range(nx):
        block_basis(i, -1 if i == 0 else int(i == nx - 1))

    loads[2].wait()
    loads[3].wait()

    sums_of = {}

    def add(product, term):
        sums_of[product] = sums_of[product] + term if product in sums_of else term

    def products(i, edge):
        at, mid, after, row = plane(i), plane(i + 1), plane(i + 2), pl.ds(i, 1)
        diagonal, tzm, tzp, typ = d_s[at, :], tzm_s[at, :], tzp_s[at, :], typ_s[at, :]
        tym = up(typ, 1)
        txm, txp = txf[at, :], txf[mid, :]
        own, oy = own_s[mid, :], oy_s[mid, :]
        source = src[at, :]
        swap_m, swap_p = jnp.where(cross_yp, oy, own), jnp.where(cross_ym, oy, own)
        keep_m, keep_p = jnp.where(cross_yp, own, oy), jnp.where(cross_ym, own, oy)

        def z_pair(a, kind):
            return (
                jnp.where(sub == 0, zq[0, kind, row, :], up(a, 0)),
                jnp.where(sub == SUB - 1, zq[1, kind, row, :], down(a, 0)),
            )

        own_zm, own_zp = z_pair(own, 0)
        oy_zm, oy_zp = z_pair(oy, 1)
        before_own = ox_s[plane(0), :] if edge < 0 else own_s[at, :]
        after_own = ox_s[plane(3), :] if edge > 0 else own_s[after, :]
        q0 = (
            diagonal * own - txm * before_own - txp * after_own
            - tym * up(swap_m, 1) - typ * down(swap_p, 1) - tzm * own_zm - tzp * own_zp
        )
        qy = (
            diagonal * oy - tym * up(keep_m, 1) - typ * down(keep_p, 1)
            - tzm * oy_zm - tzp * oy_zp
        )
        if edge >= 0:
            qy = qy - txm * oy_s[at, :]
        if edge <= 0:
            qy = qy - txp * oy_s[after, :]
        fields = (((0, 0, 0), q0), ((0, 0, 1), qy), (None, source))
        for kind, weight in ((OWN, own), (OY, oy)):
            for offset, field in fields:
                add((kind, offset, 0), weight * field)
        if not edge:
            return
        ox = ox_s[plane(1 if edge < 0 else 2), :]
        if edge < 0:
            for offset, field in fields:
                add((OX, offset, -1), ox * field)
            across, t_across = plane(0), txm
        else:
            add((OX, None, 1), ox * source)
            across, t_across = plane(nx + 1), txp
        tymc, typc = only(cross_ym, tym), only(cross_yp, typ)
        tzmc, tzpc = only(cross_zm, tzm), only(cross_zp, tzp)
        ox_ym, ox_yp = up(ox, 1), down(ox, 1)
        ox_zm = jnp.where(sub == 0, zb[0, OX, row, :], up(ox, 0))
        ox_zp = jnp.where(sub == SUB - 1, zb[1, OX, row, :], down(ox, 0))
        qx = (
            diagonal * ox - t_across * own_s[across, :] - (tym - tymc) * ox_ym
            - (typ - typc) * ox_yp - (tzm - tzmc) * ox_zm - (tzp - tzpc) * ox_zp
        )
        qxy = -(t_across * oy_s[across, :] + tymc * ox_ym + typc * ox_yp)
        qxz = -(t_across * oz_s[across, :] + tzmc * ox_zm + tzpc * ox_zp)
        for offset, field in zip(EDGE_OFFSETS, (qx, qxy, qxz)):
            add((OX, offset, edge), ox * field)
            if edge > 0:
                for kind, weight in ((OWN, own), (OZ, oz_s[mid, :]), (OY, oy)):
                    add((kind, offset, 1), weight * field)
        if edge > 0:
            inward = -txm * ox
            for kind, ref in ((OWN, own_s), (OZ, oz_s), (OY, oy_s)):
                add((kind, EDGE_OFFSETS[0], 1), ref[at, :] * inward)

    for i in range(nx):
        products(i, -1 if i == 0 else int(i == nx - 1))

    z1 = parity * (SUB - 1)
    z2 = 1 + parity * (SUB - 3)
    for i in range(nx):
        ze[1, pl.ds(i, 1), :] = own_s[pl.ds((i + 1) * SUB + z2, 1), :]
        ze[2, pl.ds(i, 1), :] = oy_s[pl.ds((i + 1) * SUB + z2, 1), :]
        ze[3, pl.ds(i, 1), :] = src[pl.ds(i * SUB + z1, 1), :]
    first, last = wide_row == 0, wide_row == nx - 1
    wide_ym, wide_yp = wide_lane % EDGE == 0, wide_lane % EDGE == EDGE - 1
    k1 = zs[parity, 0]
    t_out = tz_edge[parity]
    t_in = VERTICAL_RATIO * harmonic(k1, zs[parity, 1])
    inner = harmonic(k1, up(k1, 0))
    txm = jnp.where(first, harmonic(k1, kx[pl.ds(SUB + z1, 1), :]), inner)
    txp = jnp.where(last, harmonic(k1, kx[pl.ds((nx + 2) * SUB + z1, 1), :]), down(inner, 0))
    typ = y_face(k1)
    tym = up(typ, 1)
    txmc, txpc = only(first, txm), only(last, txp)
    tymc, typc = only(wide_ym, tym), only(wide_yp, typ)
    diagonal, own, (ox, oz, oy) = basis(
        zs[parity, 2], ((txm, txp), (t_in, t_out), (tym, typ)),
        (txmc + txpc, t_out, tymc + typc),
    )
    ze[0] = oz
    txmn, txpn, tymn, typn = txm - txmc, txp - txpc, tym - tymc, typ - typc
    own_in, oy_in, source = ze[1], ze[2], ze[3]
    ox_before, ox_after = ox_s[pl.ds(z1, 1), :], ox_s[pl.ds(3 * SUB + z1, 1), :]
    oz_ym, oz_yp = up(oz, 1), down(oz, 1)
    q0 = (
        diagonal * own - t_out * zb[parity, OZ] - t_in * own_in
        - txm * jnp.where(first, ox_before, up(own, 0))
        - txp * jnp.where(last, ox_after, down(own, 0))
        - tym * up(jnp.where(wide_yp, oy, own), 1) - typ * down(jnp.where(wide_ym, oy, own), 1)
    )
    qy = (
        diagonal * oy - t_in * oy_in - txmn * up(oy, 0) - txpn * down(oy, 0)
        - tym * up(jnp.where(wide_yp, own, oy), 1) - typ * down(jnp.where(wide_ym, own, oy), 1)
    )
    qz = (
        diagonal * oz - t_out * zb[parity, OWN] - txmn * up(oz, 0) - txpn * down(oz, 0)
        - tymn * oz_ym - typn * oz_yp
    )
    qz_in = -t_in * oz
    qzy = -(tymc * oz_ym + typc * oz_yp + t_out * zb[parity, OY])

    def add_rows(product, term):
        add(product, term[:SUB, :] + term[SUB:, :])

    for offset, field in zip(FULL_OFFSETS, (q0, qy, qz, qzy, source)):
        add_rows((OZ, offset, 0), oz * field)
    add_rows((OWN, FULL_OFFSETS[2], 0), own * qz + own_in * qz_in)
    add_rows((OY, FULL_OFFSETS[2], 0), oy * qz + oy_in * qz_in)
    add_rows((OWN, FULL_OFFSETS[3], 0), own * qzy)
    add_rows((OY, FULL_OFFSETS[3], 0), oy * qzy)
    add_rows((OX, FULL_OFFSETS[3], -1), only(first, ox * qzy))
    ox_in = only(first, ox_s[pl.ds(SUB + z2, 1), :])
    add_rows((OX, FULL_OFFSETS[2], -1), only(first, ox * qz) + ox_in * qz_in)
    for n in range(PADDED):
        acc[plane(n), :] = (
            sums_of[PRODUCTS[n]] if n < len(PRODUCTS) else jnp.zeros((SUB, ny), jnp.float32)
        )

    fine = lax.broadcasted_iota(jnp.int32, (ny, LANES), 0)
    spot = lax.broadcasted_iota(jnp.int32, (ny, LANES), 1)
    group = spot // cells
    upper = group % 2
    wanted = fine // EDGE + jnp.where(group >= 2, 2 * upper - 1, 0)
    hit = (fine // HALF % 2 == upper) & (wanted == spot % cells) & (group < 4)
    gather = jnp.where(hit, 1.0, 0.0).astype(jnp.bfloat16)
    halves = split_dot(gather, acc[...], swap=True)
    sums = halves.reshape(PADDED, SUB, LANES).sum(axis=1)
    stacked = jnp.concatenate(
        [sums] + [pltpu.roll(sums, LANES - g * cells, 1) for g in (1, 2, 3)], axis=0
    )
    routed = split_dot(route[...], stacked)
    routed = jnp.where(
        lax.broadcasted_iota(jnp.int32, routed.shape, 1) < cells, routed, 0.0
    )
    beside_pair = pair + 2 * parity - 1
    near_pair = jnp.clip(beside_pair, 0, pairs - 1)
    for target in range(6):
        block = routed[target * VALUES : (target + 1) * VALUES, :]
        if rows < VALUES:
            block = block[:rows, :] + pltpu.roll(block[rows:, :], span, 1)
        to_pair = near_pair if target % 2 else pair
        part[target] = pltpu.roll(block, to_pair * cells, 1)

    def fold_copy(sx, beside, which):
        to_pair = beside_pair if beside else pair
        role = layer - 2 * to_pair + 1
        slot = (1 - sx) * 4 + role
        n = ((sx + 1) * 2 + beside) * 2 + which
        return pltpu.make_async_remote_copy(
            part.at[(sx + 1) * 2 + beside], fold.at[slot], f_send.at[n], f_recv.at[slot],
            device_id=(tile + sx, 2 * to_pair + which), device_id_type=MESH,
        )

    def fold_valid(sx, beside, which):
        ok = (tile + sx >= 0) & (tile + sx < tiles)
        if beside:
            return ok & (beside_pair >= 0) & (beside_pair < pairs)
        return ok if sx else ok & (which != parity)

    fold_list = [(sx, b, w) for b in (1, 0) for sx in (-1, 1, 0) for w in (0, 1)]
    for item in fold_list:
        @pl.when(fold_valid(*item))
        def _():
            fold_copy(*item).start()

    for dt in (-1, 0, 1):
        for role in range(4):
            slot = (dt + 1) * 4 + role

            @pl.when(fold_from(dt, role))
            def _():
                pltpu.make_async_remote_copy(
                    part.at[0], fold.at[slot], f_send.at[0], f_recv.at[slot],
                    device_id=(tile, layer), device_id_type=MESH,
                ).wait_recv()

    terms = [part[2]] + [fold[slot] for slot in range(12)]
    while len(terms) > 1:
        terms = [sum(terms[n + 1 : n + 2], terms[n]) for n in range(0, len(terms), 2)]
    gsend[...] = terms[0]

    def gather_copy(k):
        other = lax.rem(tile * pairs + pair + k, tiles * pairs)
        return pltpu.make_async_remote_copy(
            gsend, gath.at[tile * pairs + pair], g_send.at[k], g_recv.at[tile * pairs + pair],
            device_id=(other // pairs, 2 * (other % pairs) + parity), device_id_type=MESH,
        )

    for k in range(1, tiles * pairs):
        gather_copy(k).start()
    gath[tile * pairs + pair] = gsend[...]

    cell_at = lax.broadcasted_iota(jnp.int32, (LANES, ny), 0)
    fine_at = lax.broadcasted_iota(jnp.int32, (LANES, ny), 1)
    parent = fine_at // EDGE
    spread = jnp.where(cell_at == parent, 1.0, 0.0).astype(jnp.bfloat16)
    beside_y = parent + 2 * (fine_at // HALF % 2) - 1
    spread_y = jnp.where(cell_at == beside_y, 1.0, 0.0).astype(jnp.bfloat16)

    for k in range(1, tiles * pairs):
        frm = lax.rem(tile * pairs + pair + tiles * pairs - k, tiles * pairs)
        pltpu.make_async_remote_copy(
            gsend, gath.at[frm], g_send.at[k], g_recv.at[frm],
            device_id=(tile, layer), device_id_type=MESH,
        ).wait_recv()

    for t in range(tiles):
        total = gath[t * pairs]
        for p in range(1, pairs):
            total = total + gath[t * pairs + p]
        gsum[pl.ds(t * rows, rows), :] = total
    lane_t = lax.broadcasted_iota(jnp.int32, (tiles, LANES), 1)

    def value(v):
        a = gsum[pl.ds(v % rows, tiles, stride=rows), :]
        if v >= rows:
            a = pltpu.roll(a, LANES - span, 1)
        return only(lane_t < span, a)

    def shifted(a, offset):
        ox, oz, oy = offset
        along = -(oz * cells + oy) % LANES
        if along:
            a = pltpu.roll(a, along, 1)
        if ox:
            a = pltpu.roll(a, -ox % tiles, 0)
        return a

    offsets = [((v + 13) // 9 - 1, (v + 13) // 3 % 3 - 1, (v + 13) % 3 - 1) for v in range(14)]
    forward = [value(v) for v in range(14)]
    backward = [
        shifted(forward[v], [-d for d in offsets[v]]) if v else None for v in range(14)
    ]
    rhs = value(RHS)
    scale = COARSE_DAMPING / jnp.where(lane_t < span, forward[0], 1.0)
    coarse = rhs * scale
    for _ in range(SWEEPS - 1):
        applied = forward[0] * coarse
        for v in range(1, 14):
            applied = applied + forward[v] * shifted(coarse, offsets[v])
            applied = applied + backward[v] * shifted(coarse, [-d for d in offsets[v]])
        coarse = coarse + (rhs - applied) * scale
    csc[...] = coarse

    def coarse_row(t, p):
        a = jnp.broadcast_to(csc[pl.ds(t, 1), :], (SUB, LANES))
        return pltpu.roll(a, (LANES - p * cells) % LANES, 1)

    center = coarse_row(tile, pair)
    four = jnp.concatenate(
        [
            center,
            coarse_row(tile, near_pair),
            coarse_row(jnp.maximum(tile - 1, 0), pair),
            coarse_row(jnp.minimum(tile + 1, tiles - 1), pair),
        ],
        axis=0,
    )
    wide = split_dot(spread, four, swap=True)
    c_own, c_z = wide[:SUB, :], wide[SUB : 2 * SUB, :]
    c_y = split_dot(spread_y, center, swap=True)
    ze[0] = ze[0] * jnp.concatenate([c_z] * (nx // SUB), axis=0)
    at_edge = sub == parity * (SUB - 1)
    for i in range(nx):
        at = plane(i + 1)
        result = own_s[at, :] * c_own + oy_s[at, :] * c_y
        result = result + only(at_edge, ze[0, pl.ds(i, 1), :])
        if i == 0:
            result = result + ox_s[plane(1), :] * wide[2 * SUB : 3 * SUB, :]
        if i == nx - 1:
            result = result + ox_s[plane(2), :] * wide[3 * SUB :, :]
        out_ref[plane(i), :] = result

    for sz in sides:
        @pl.when(has(0, sz))
        def _():
            layer_copy(sz).wait_send()
    for sx in sides:
        @pl.when(has(sx, 0))
        def _():
            for copy in halo_copies(sx):
                copy.wait_send()
    for sx, sz in diagonals:
        @pl.when(has(sx, sz))
        def _():
            corner_copy(sx, sz).wait_send()
    for item in fold_list:
        @pl.when(fold_valid(*item))
        def _():
            fold_copy(*item).wait_send()
    for k in range(1, tiles * pairs):
        gather_copy(k).wait_send()


def body(tiles, layers, classes, well_mask, source):
    nx, nz, ny = classes.shape
    assert nx == EDGE and nz == HALF == SUB and layers % 2 == 0
    cells, pairs = ny // EDGE, layers // 2
    assert 4 * cells <= LANES and pairs * cells <= LANES
    rows = VALUES // 2 if 2 * pairs * cells <= LANES else VALUES
    flat = lambda a: a.reshape(nx * nz, ny)
    f32 = lambda *shape: pltpu.VMEM(shape, jnp.float32)
    dma = pltpu.SemaphoreType.DMA
    block = (nx * SUB, ny)
    wide = ((nx + 2) * SUB, ny)
    scratch = [
        pltpu.VMEM(block, jnp.int32), pltpu.VMEM(block, jnp.int32), f32(*block),
        pltpu.VMEM((6 * VALUES, 4 * PADDED), jnp.bfloat16),
        f32((nx + 4) * SUB, ny), f32(*wide), f32(2, 3, nx, ny), f32(2, 3, nx, ny),
        f32(4, 1, ny), f32(4, 1, ny),
        f32(2, 2, nx, ny), f32(4, nx, ny),
        f32(*block), f32(*block), f32((nx + 1) * SUB, ny), f32(*block), f32(*block), f32(*block),
        f32(*wide), f32(*wide), f32(*wide), f32(4 * SUB, ny), f32(2, nx, ny), f32(2, 4, nx, ny),
        pltpu.VMEM((3, nx, ny), jnp.int32), f32(PADDED * SUB, ny), f32(6, rows, LANES), f32(12, rows, LANES), f32(rows, LANES),
        f32(tiles * pairs, rows, LANES), f32(tiles * rows, LANES), f32(tiles, LANES),
        dma((4,)), dma((2, 2)), dma((2, 2)), dma((2,)), dma((2,)), dma((4,)), dma((4,)),
        dma((12,)), dma((12,)), dma((tiles * pairs,)), dma((tiles * pairs,)),
    ]
    route = jnp.asarray(routing_table(), jnp.bfloat16)
    result = pl.pallas_call(
        functools.partial(kernel, tiles, layers, nx, ny),
        out_shape=jax.ShapeDtypeStruct(block, jnp.float32),
        in_specs=[pl.BlockSpec(memory_space=pltpu.HBM)] * 4,
        out_specs=pl.BlockSpec(memory_space=pltpu.VMEM),
        scratch_shapes=scratch,
        compiler_params=pltpu.CompilerParams(
            collective_id=0, has_side_effects=True, vmem_limit_bytes=107 * 2**19
        ),
    )(flat(classes), flat(well_mask), flat(source), route)
    return result.reshape(nx, nz, ny)


def solution(mesh):
    spec = P("tile", "layer", None)
    return jax.shard_map(
        functools.partial(body, mesh.shape["tile"], mesh.shape["layer"]),
        mesh=mesh, in_specs=(spec, spec, spec), out_specs=spec, check_vma=False,
    )
```

```python
import functools

import jax
import jax.numpy as jnp
import numpy as np
from jax import lax
from jax.experimental import pallas as pl
from jax.experimental.pallas import tpu as pltpu
from jax.sharding import PartitionSpec as P

EDGE = 16
HALF = EDGE // 2
CLASSES = 16
SWEEPS = 4
FINE_DAMPING = 0.67
COARSE_DAMPING = 0.5
SINK_RATE = 0.5
VERTICAL_RATIO = 0.25
LANES = 128
SUB = 8
VALUES = 16
RHS = 14
MESH = pl.DeviceIdType.MESH

OWN, OX, OZ, OY = range(4)
FULL_OFFSETS = ((0, 0, 0), (0, 0, 1), (0, 1, 0), (0, 1, 1), None)
EDGE_OFFSETS = ((1, 0, 0), (1, 0, 1), (1, 1, 0))
PRODUCTS = (
    [(w, b, 0) for w in (OWN, OZ, OY) for b in FULL_OFFSETS]
    + [(OX, b, -1) for b in FULL_OFFSETS]
    + [(OX, None, 1)]
    + [(w, b, 1) for w in (OWN, OZ, OY, OX) for b in EDGE_OFFSETS]
    + [(OX, b, -1) for b in EDGE_OFFSETS]
)
SLOT = {product: index for index, product in enumerate(PRODUCTS)}
PADDED = -(-len(PRODUCTS) // SUB) * SUB


def routing_table():
    table = np.zeros((2, 6 * VALUES, 4 * PADDED), np.float32)
    for parity, sign_z in ((0, -1), (1, 1)):
        for n, (weight, toggled, sign_x) in enumerate(PRODUCTS):
            for half, sign_y in ((0, -1), (1, 1)):
                row = ((weight == OX) * sign_x, (weight == OZ) * sign_z, (weight == OY) * sign_y)
                if toggled is None:
                    value = RHS
                else:
                    column = (toggled[0] * sign_x, toggled[1] * sign_z, toggled[2] * sign_y)
                    o = [column[d] - row[d] for d in range(3)]
                    value = 9 * (o[0] + 1) + 3 * (o[1] + 1) + (o[2] + 1) - 13
                    if value < 0:
                        continue
                group = 2 * (weight == OY) + half
                target = (row[0] + 1) * 2 + (weight == OZ)
                table[parity, target * VALUES + value, group * PADDED + n] = 1.0
    return table


def split_dot(table, values, swap=False):
    total = None
    rest = values
    for _ in range(2):
        part = rest.astype(jnp.bfloat16)
        rest = rest - part.astype(jnp.float32)
        pair = (part, table) if swap else (table, part)
        term = jnp.dot(*pair, preferred_element_type=jnp.float32)
        total = term if total is None else total + term
    return total


def inverse_of(a):
    guarded = jnp.maximum(a, 1e-30)
    guess = pl.reciprocal(guarded, approx=True)
    return guess * (2.0 - guarded * guess)


def harmonic(a, b):
    return 2.0 * a * b * inverse_of(a + b)


def perm_of(classes):
    step = 5.0 / (CLASSES - 1)
    return jnp.exp(classes.astype(jnp.float32) * step - 2.5)


def sink_of(well, perm):
    return SINK_RATE * well.astype(jnp.float32) * perm


def kernel(
    tiles, layers, nx, ny,
    cls_hbm, well_hbm, src_hbm, route_hbm, out_ref,
    cls, well, src, route,
    kx, sk, zs, zr, crs, crr, zq, ze,
    typ_s, tzi_s, txf, tzm_s, tzp_s, d_s, own_s, oy_s, oz_s, ox_s, tz_edge, zb,
    zi, half_table, acc, part, fold, gsend, gath, gsum, csc,
    in_sem, x_send, x_recv, z_send, z_recv, c_send, c_recv, f_send, f_recv, g_send, g_recv,
):
    tile = lax.axis_index("tile")
    layer = lax.axis_index("layer")
    pairs = layers // 2
    pair = layer // 2
    parity = layer % 2
    cells = ny // EDGE
    span = pairs * cells
    rows = part.shape[1]
    plane = lambda i: pl.ds(i * SUB, SUB)

    loads = [
        pltpu.make_async_copy(a, b, in_sem.at[n])
        for n, (a, b) in enumerate(
            ((cls_hbm, cls), (well_hbm, well), (src_hbm, src), (route_hbm.at[parity], route))
        )
    ]
    loads[0].start()
    loads[1].start()

    barrier = pltpu.get_barrier_semaphore()
    for a in range(tiles):
        for b in range(layers):
            if a or b:
                pl.semaphore_signal(
                    barrier, inc=1, device_id_type=MESH,
                    device_id=(lax.rem(tile + a, tiles), lax.rem(layer + b, layers)),
                )

    def fold_from(dt, role):
        from_layer = 2 * pair - 1 + role
        ok = (tile + dt >= 0) & (tile + dt < tiles)
        ok = ok & (from_layer >= 0) & (from_layer < layers)
        return ok & (from_layer != layer) if dt == 0 else ok

    for dt in (-1, 0, 1):
        for role in range(4):
            @pl.when(jnp.logical_not(fold_from(dt, role)))
            def _():
                fold[(dt + 1) * 4 + role] = jnp.zeros(fold.shape[1:], jnp.float32)

    loads[0].wait()
    loads[1].wait()
    loads[2].start()
    loads[3].start()

    for i in (0, 1, nx - 2, nx - 1):
        k = perm_of(cls[plane(i), :])
        kx[plane(i + 2), :] = k
        if i in (0, nx - 1):
            sk[plane(i + 1), :] = sink_of(well[plane(i), :], k)
    for side, (z1, z2) in enumerate(((0, 1), (SUB - 1, SUB - 2))):
        for i in range(nx):
            zi[0, pl.ds(i, 1), :] = cls[pl.ds(i * SUB + z1, 1), :]
            zi[1, pl.ds(i, 1), :] = cls[pl.ds(i * SUB + z2, 1), :]
            zi[2, pl.ds(i, 1), :] = well[pl.ds(i * SUB + z1, 1), :]
        k = perm_of(zi[0])
        zs[side, 0] = k
        zs[side, 1] = perm_of(zi[1])
        zs[side, 2] = sink_of(zi[2], k)
        crs[0 + side] = k[0:1, :]
        crs[2 + side] = k[nx - 1 : nx, :]

    pl.semaphore_wait(barrier, tiles * layers - 1)

    def halo_copies(sx):
        lo = sx < 0
        src_k = kx.at[pl.ds((2 if lo else nx) * SUB, 2 * SUB), :]
        dst_k = kx.at[pl.ds((nx + 2 if lo else 0) * SUB, 2 * SUB), :]
        src_s = sk.at[plane(1 if lo else nx), :]
        dst_s = sk.at[plane(nx + 1 if lo else 0), :]
        s = 0 if lo else 1
        return [
            pltpu.make_async_remote_copy(
                a, b, x_send.at[s, n], x_recv.at[s, n],
                device_id=(tile + sx, layer), device_id_type=MESH,
            )
            for n, (a, b) in enumerate(((src_k, dst_k), (src_s, dst_s)))
        ]

    def layer_copy(sz, n):
        s = 0 if sz < 0 else 1
        return pltpu.make_async_remote_copy(
            zs.at[s, n], zr.at[1 - s, n], z_send.at[s, n], z_recv.at[s, n],
            device_id=(tile, layer + sz), device_id_type=MESH,
        )

    def corner_copy(sx, sz):
        a, b = (0 if sx < 0 else 1), (0 if sz < 0 else 1)
        return pltpu.make_async_remote_copy(
            crs.at[2 * a + b], crr.at[2 * (1 - a) + (1 - b)],
            c_send.at[2 * a + b], c_recv.at[2 * a + b],
            device_id=(tile + sx, layer + sz), device_id_type=MESH,
        )

    def has(sx, sz):
        ok = None
        for s, at, count in ((sx, tile, tiles), (sz, layer, layers)):
            if s:
                test = at > 0 if s < 0 else at < count - 1
                ok = test if ok is None else ok & test
        return ok

    sides = (-1, 1)
    diagonals = [(sx, sz) for sx in sides for sz in sides]
    for sz in sides:
        @pl.when(has(0, sz))
        def _():
            layer_copy(sz, 0).start()

        @pl.when(jnp.logical_not(has(0, sz)))
        def _():
            zr[0 if sz < 0 else 1] = jnp.zeros(zr.shape[1:], jnp.float32)
    for sx in sides:
        @pl.when(has(sx, 0))
        def _():
            for copy in halo_copies(sx):
                copy.start()

        @pl.when(jnp.logical_not(has(sx, 0)))
        def _():
            first = 0 if sx < 0 else nx + 2
            kx[pl.ds(first * SUB, 2 * SUB), :] = jnp.zeros((2 * SUB, ny), jnp.float32)
            sk[plane(0 if sx < 0 else nx + 1), :] = jnp.zeros((SUB, ny), jnp.float32)
    for sx, sz in diagonals:
        @pl.when(has(sx, sz))
        def _():
            corner_copy(sx, sz).start()

        @pl.when(jnp.logical_not(has(sx, sz)))
        def _():
            crr[2 * (0 if sx < 0 else 1) + (0 if sz < 0 else 1)] = jnp.zeros((1, ny), jnp.float32)
    for sz in sides:
        @pl.when(has(0, sz))
        def _():
            layer_copy(sz, 1).start()
            layer_copy(sz, 2).start()

    sub = lax.broadcasted_iota(jnp.int32, (SUB, ny), 0)
    lane = lax.broadcasted_iota(jnp.int32, (SUB, ny), 1)
    even = parity == 0
    cross_ym = lane % EDGE == 0
    cross_yp = lane % EDGE == EDGE - 1
    cross_zm = (sub == 0) & even
    cross_zp = (sub == SUB - 1) & jnp.logical_not(even)

    def up(a, dim):
        return pltpu.roll(a, 1, dim)

    def down(a, dim):
        return pltpu.roll(a, a.shape[dim] - 1, dim)

    def y_face(k):
        at = lax.broadcasted_iota(jnp.int32, k.shape, 1)
        return jnp.where(at == ny - 1, 0.0, harmonic(k, down(k, 1)))

    def only(mask, a):
        return jnp.where(mask, a, 0.0)

    for i in range(2, nx - 2):
        k = perm_of(cls[plane(i), :])
        kx[plane(i + 2), :] = k
        sk[plane(i + 1), :] = sink_of(well[plane(i), :], k)
    for i in (1, nx - 2):
        sk[plane(i + 1), :] = sink_of(well[plane(i), :], kx[plane(i + 2), :])

    def faces(i):
        at = plane(i)
        k = kx[plane(i + 2), :]
        typ_s[at, :] = y_face(k)
        tzi_s[at, :] = VERTICAL_RATIO * harmonic(k, up(k, 0))

        if i > 0:
            txf[at, :] = harmonic(kx[plane(i + 1), :], k)

    for i in range(nx):
        faces(i)

    fine = lax.broadcasted_iota(jnp.int32, (ny, LANES), 0)
    spot = lax.broadcasted_iota(jnp.int32, (ny, LANES), 1)
    group = spot // cells
    upper = group % 2
    wanted = fine // EDGE + jnp.where(group >= 2, 2 * upper - 1, 0)
    hit = (fine // HALF % 2 == upper) & (wanted == spot % cells) & (group < 4)
    half_table[...] = jnp.where(hit, 1.0, 0.0).astype(jnp.bfloat16)

    def wait_layers(n):
        for sz in sides:
            @pl.when(has(0, sz))
            def _():
                layer_copy(-sz, n).wait_recv()

    wait_layers(0)
    for sx in sides:
        @pl.when(has(sx, 0))
        def _():
            halo_copies(-sx)[0].wait_recv()
    txf[plane(0), :] = harmonic(kx[plane(1), :], kx[plane(2), :])
    txf[plane(nx), :] = harmonic(kx[plane(nx + 1), :], kx[plane(nx + 2), :])
    for side in (0, 1):
        tz_edge[side] = VERTICAL_RATIO * harmonic(zs[side, 0], zr[side, 0])

    def basis(sink, faces, crossing):
        diagonal = sink
        for pair_of in faces:
            diagonal = diagonal + pair_of[0] + pair_of[1]
        inverse = FINE_DAMPING * inverse_of(diagonal)
        leaving = sink
        for term in crossing:
            if term is not None:
                leaving = leaving + term
        outer = [None if term is None else term * inverse for term in crossing]
        return diagonal, 1.0 - leaving * inverse, outer

    def block_basis(i, edge):
        at = plane(i)
        after = plane(i + 1)
        inner = tzi_s[at, :]
        tzm = jnp.where(sub == 0, tz_edge[0, pl.ds(i, 1), :], inner)
        tzp = jnp.where(sub == SUB - 1, tz_edge[1, pl.ds(i, 1), :], down(inner, 0))
        txm = txf[at, :]
        txp = txf[after, :]
        typ = typ_s[at, :]
        tym = up(typ, 1)
        crossing = (
            None if edge == 0 else (txm if edge < 0 else txp),
            only(cross_zm, tzm) + only(cross_zp, tzp),
            only(cross_ym, tym) + only(cross_yp, typ),
        )
        diagonal, own, outer = basis(
            sk[after, :], ((txm, txp), (tzm, tzp), (tym, typ)), crossing
        )
        tzm_s[at, :] = tzm
        tzp_s[at, :] = tzp
        d_s[at, :] = diagonal
        own_s[after, :] = own
        if i >= nx - 2:
            oz_s[after, :] = outer[1]
        oy_s[after, :] = outer[2]
        if edge:
            ox_s[plane(1 if edge < 0 else 2), :] = outer[0]

    for i in range(nx):
        block_basis(i, -1 if i == 0 else int(i == nx - 1))

    for sx in sides:
        @pl.when(has(sx, 0))
        def _():
            halo_copies(-sx)[1].wait_recv()
    for sx, sz in diagonals:
        @pl.when(has(sx, sz))
        def _():
            corner_copy(-sx, -sz).wait_recv()

    for side in (0, 1):
        k1 = kx[plane(1 if side == 0 else nx + 2), :]
        k2 = kx[plane(0 if side == 0 else nx + 3), :]
        toward = txf[plane(0 if side == 0 else nx), :]
        inner = VERTICAL_RATIO * harmonic(k1, up(k1, 0))
        tzm = jnp.where(sub == 0, VERTICAL_RATIO * harmonic(k1, crr[2 * side]), inner)
        tzp = jnp.where(
            sub == SUB - 1, VERTICAL_RATIO * harmonic(k1, crr[2 * side + 1]), down(inner, 0)
        )
        typ = y_face(k1)
        tym = up(typ, 1)
        crossing = (
            toward,
            only(cross_zm, tzm) + only(cross_zp, tzp),
            only(cross_ym, tym) + only(cross_yp, typ),
        )
        _, own, outer = basis(
            sk[plane(0 if side == 0 else nx + 1), :],
            ((toward, harmonic(k1, k2)), (tzm, tzp), (tym, typ)),
            crossing,
        )
        at = plane(0 if side == 0 else nx + 1)
        own_s[at, :] = own
        ox_s[plane(0 if side == 0 else 3), :] = outer[0]
        oz_s[at, :] = outer[1]
        oy_s[at, :] = outer[2]

    wait_layers(1)
    wait_layers(2)
    wide_row = lax.broadcasted_iota(jnp.int32, (nx, ny), 0)
    wide_lane = lax.broadcasted_iota(jnp.int32, (nx, ny), 1)
    for side in (0, 1):
        k1 = zr[side, 0]
        k2 = zr[side, 1]
        toward = tz_edge[side]
        inner = harmonic(k1, up(k1, 0))
        txm = jnp.where(wide_row == 0, harmonic(k1, crr[side]), inner)
        txp = jnp.where(wide_row == nx - 1, harmonic(k1, crr[2 + side]), down(inner, 0))
        typ = y_face(k1)
        tym = up(typ, 1)
        crosses = even if side == 0 else jnp.logical_not(even)
        crossing = (
            only(wide_row == 0, txm) + only(wide_row == nx - 1, txp),
            toward * crosses.astype(jnp.float32),
            only(wide_lane % EDGE == 0, tym) + only(wide_lane % EDGE == EDGE - 1, typ),
        )
        _, own, outer = basis(
            zr[side, 2],
            ((txm, txp), (toward, VERTICAL_RATIO * harmonic(k1, k2)), (tym, typ)),
            crossing,
        )
        zb[side, OWN] = own
        zb[side, OX] = outer[0]
        zb[side, OZ] = outer[1]
        zb[side, OY] = outer[2]
        zq[side, 0] = jnp.where(crosses, outer[1], own)
        zq[side, 1] = jnp.where(crosses, 0.0, outer[2])

    loads[2].wait()
    loads[3].wait()

    sums_of = {}

    def add(product, term):
        sums_of[product] = sums_of[product] + term if product in sums_of else term

    def products(i, edge):
        at, mid, after, row = plane(i), plane(i + 1), plane(i + 2), pl.ds(i, 1)
        diagonal, tzm, tzp, typ = d_s[at, :], tzm_s[at, :], tzp_s[at, :], typ_s[at, :]
        tym = up(typ, 1)
        txm, txp = txf[at, :], txf[mid, :]
        own, oy = own_s[mid, :], oy_s[mid, :]
        source = src[at, :]
        swap_m, swap_p = jnp.where(cross_yp, oy, own), jnp.where(cross_ym, oy, own)
        keep_m, keep_p = jnp.where(cross_yp, own, oy), jnp.where(cross_ym, own, oy)

        def z_pair(a, kind):
            return (
                jnp.where(sub == 0, zq[0, kind, row, :], up(a, 0)),
                jnp.where(sub == SUB - 1, zq[1, kind, row, :], down(a, 0)),
            )

        own_zm, own_zp = z_pair(own, 0)
        oy_zm, oy_zp = z_pair(oy, 1)
        before_own = ox_s[plane(0), :] if edge < 0 else own_s[at, :]
        after_own = ox_s[plane(3), :] if edge > 0 else own_s[after, :]
        q0 = (
            diagonal * own - txm * before_own - txp * after_own
            - tym * up(swap_m, 1) - typ * down(swap_p, 1) - tzm * own_zm - tzp * own_zp
        )
        qy = (
            diagonal * oy - tym * up(keep_m, 1) - typ * down(keep_p, 1)
            - tzm * oy_zm - tzp * oy_zp
        )
        if edge >= 0:
            qy = qy - txm * oy_s[at, :]
        if edge <= 0:
            qy = qy - txp * oy_s[after, :]
        fields = (((0, 0, 0), q0), ((0, 0, 1), qy), (None, source))
        for kind, weight in ((OWN, own), (OY, oy)):
            for offset, field in fields:
                add((kind, offset, 0), weight * field)
        if not edge:
            return
        ox = ox_s[plane(1 if edge < 0 else 2), :]
        if edge < 0:
            for offset, field in fields:
                add((OX, offset, -1), ox * field)
            across, t_across = plane(0), txm
        else:
            add((OX, None, 1), ox * source)
            across, t_across = plane(nx + 1), txp
        tymc, typc = only(cross_ym, tym), only(cross_yp, typ)
        tzmc, tzpc = only(cross_zm, tzm), only(cross_zp, tzp)
        ox_ym, ox_yp = up(ox, 1), down(ox, 1)
        ox_zm = jnp.where(sub == 0, zb[0, OX, row, :], up(ox, 0))
        ox_zp = jnp.where(sub == SUB - 1, zb[1, OX, row, :], down(ox, 0))
        qx = (
            diagonal * ox - t_across * own_s[across, :] - (tym - tymc) * ox_ym
            - (typ - typc) * ox_yp - (tzm - tzmc) * ox_zm - (tzp - tzpc) * ox_zp
        )
        qxy = -(t_across * oy_s[across, :] + tymc * ox_ym + typc * ox_yp)
        qxz = -(t_across * oz_s[across, :] + tzmc * ox_zm + tzpc * ox_zp)
        for offset, field in zip(EDGE_OFFSETS, (qx, qxy, qxz)):
            add((OX, offset, edge), ox * field)
            if edge > 0:
                for kind, weight in ((OWN, own), (OZ, oz_s[mid, :]), (OY, oy)):
                    add((kind, offset, 1), weight * field)
        if edge > 0:
            inward = -txm * ox
            for kind, ref in ((OWN, own_s), (OZ, oz_s), (OY, oy_s)):
                add((kind, EDGE_OFFSETS[0], 1), ref[at, :] * inward)

    for i in range(nx):
        products(i, -1 if i == 0 else int(i == nx - 1))

    z1 = parity * (SUB - 1)
    z2 = 1 + parity * (SUB - 3)
    for i in range(nx):
        ze[1, pl.ds(i, 1), :] = own_s[pl.ds((i + 1) * SUB + z2, 1), :]
        ze[2, pl.ds(i, 1), :] = oy_s[pl.ds((i + 1) * SUB + z2, 1), :]
        ze[3, pl.ds(i, 1), :] = src[pl.ds(i * SUB + z1, 1), :]
    first, last = wide_row == 0, wide_row == nx - 1
    wide_ym, wide_yp = wide_lane % EDGE == 0, wide_lane % EDGE == EDGE - 1
    k1 = zs[parity, 0]
    t_out = tz_edge[parity]
    t_in = VERTICAL_RATIO * harmonic(k1, zs[parity, 1])
    inner = harmonic(k1, up(k1, 0))
    txm = jnp.where(first, harmonic(k1, kx[pl.ds(SUB + z1, 1), :]), inner)
    txp = jnp.where(last, harmonic(k1, kx[pl.ds((nx + 2) * SUB + z1, 1), :]), down(inner, 0))
    typ = y_face(k1)
    tym = up(typ, 1)
    txmc, txpc = only(first, txm), only(last, txp)
    tymc, typc = only(wide_ym, tym), only(wide_yp, typ)
    diagonal, own, (ox, oz, oy) = basis(
        zs[parity, 2], ((txm, txp), (t_in, t_out), (tym, typ)),
        (txmc + txpc, t_out, tymc + typc),
    )
    ze[0] = oz
    txmn, txpn, tymn, typn = txm - txmc, txp - txpc, tym - tymc, typ - typc
    own_in, oy_in, source = ze[1], ze[2], ze[3]
    ox_before, ox_after = ox_s[pl.ds(z1, 1), :], ox_s[pl.ds(3 * SUB + z1, 1), :]
    oz_ym, oz_yp = up(oz, 1), down(oz, 1)
    q0 = (
        diagonal * own - t_out * zb[parity, OZ] - t_in * own_in
        - txm * jnp.where(first, ox_before, up(own, 0))
        - txp * jnp.where(last, ox_after, down(own, 0))
        - tym * up(jnp.where(wide_yp, oy, own), 1) - typ * down(jnp.where(wide_ym, oy, own), 1)
    )
    qy = (
        diagonal * oy - t_in * oy_in - txmn * up(oy, 0) - txpn * down(oy, 0)
        - tym * up(jnp.where(wide_yp, own, oy), 1) - typ * down(jnp.where(wide_ym, own, oy), 1)
    )
    qz = (
        diagonal * oz - t_out * zb[parity, OWN] - txmn * up(oz, 0) - txpn * down(oz, 0)
        - tymn * oz_ym - typn * oz_yp
    )
    qz_in = -t_in * oz
    qzy = -(tymc * oz_ym + typc * oz_yp + t_out * zb[parity, OY])

    def add_rows(product, term):
        add(product, term[:SUB, :] + term[SUB:, :])

    for offset, field in zip(FULL_OFFSETS, (q0, qy, qz, qzy, source)):
        add_rows((OZ, offset, 0), oz * field)
    add_rows((OWN, FULL_OFFSETS[2], 0), own * qz + own_in * qz_in)
    add_rows((OY, FULL_OFFSETS[2], 0), oy * qz + oy_in * qz_in)
    add_rows((OWN, FULL_OFFSETS[3], 0), own * qzy)
    add_rows((OY, FULL_OFFSETS[3], 0), oy * qzy)
    add_rows((OX, FULL_OFFSETS[3], -1), only(first, ox * qzy))
    ox_in = only(first, ox_s[pl.ds(SUB + z2, 1), :])
    add_rows((OX, FULL_OFFSETS[2], -1), only(first, ox * qz) + ox_in * qz_in)
    for n in range(PADDED):
        acc[plane(n), :] = (
            sums_of[PRODUCTS[n]] if n < len(PRODUCTS) else jnp.zeros((SUB, ny), jnp.float32)
        )

    halves = split_dot(half_table[...], acc[...], swap=True)
    sums = halves.reshape(PADDED, SUB, LANES).sum(axis=1)
    stacked = jnp.concatenate(
        [sums] + [pltpu.roll(sums, LANES - g * cells, 1) for g in (1, 2, 3)], axis=0
    )
    routed = split_dot(route[...], stacked)
    routed = jnp.where(
        lax.broadcasted_iota(jnp.int32, routed.shape, 1) < cells, routed, 0.0
    )
    beside_pair = pair + 2 * parity - 1
    near_pair = jnp.clip(beside_pair, 0, pairs - 1)
    for target in range(6):
        block = routed[target * VALUES : (target + 1) * VALUES, :]
        if rows < VALUES:
            block = block[:rows, :] + pltpu.roll(block[rows:, :], span, 1)
        to_pair = near_pair if target % 2 else pair
        part[target] = pltpu.roll(block, to_pair * cells, 1)

    def fold_copy(sx, beside, which):
        to_pair = beside_pair if beside else pair
        role = layer - 2 * to_pair + 1
        slot = (1 - sx) * 4 + role
        n = ((sx + 1) * 2 + beside) * 2 + which
        return pltpu.make_async_remote_copy(
            part.at[(sx + 1) * 2 + beside], fold.at[slot], f_send.at[n], f_recv.at[slot],
            device_id=(tile + sx, 2 * to_pair + which), device_id_type=MESH,
        )

    def fold_valid(sx, beside, which):
        ok = (tile + sx >= 0) & (tile + sx < tiles)
        if beside:
            return ok & (beside_pair >= 0) & (beside_pair < pairs)
        return ok if sx else ok & (which != parity)

    fold_list = [(sx, b, w) for b in (1, 0) for sx in (-1, 1, 0) for w in (0, 1)]
    for item in fold_list:
        @pl.when(fold_valid(*item))
        def _():
            fold_copy(*item).start()

    for dt in (-1, 0, 1):
        for role in range(4):
            slot = (dt + 1) * 4 + role

            @pl.when(fold_from(dt, role))
            def _():
                pltpu.make_async_remote_copy(
                    part.at[0], fold.at[slot], f_send.at[0], f_recv.at[slot],
                    device_id=(tile, layer), device_id_type=MESH,
                ).wait_recv()

    terms = [part[2]] + [fold[slot] for slot in range(12)]
    while len(terms) > 1:
        terms = [sum(terms[n + 1 : n + 2], terms[n]) for n in range(0, len(terms), 2)]
    gsend[...] = terms[0]

    def gather_copy(k):
        other = lax.rem(tile * pairs + pair + k, tiles * pairs)
        return pltpu.make_async_remote_copy(
            gsend, gath.at[tile * pairs + pair], g_send.at[k], g_recv.at[tile * pairs + pair],
            device_id=(other // pairs, 2 * (other % pairs) + parity), device_id_type=MESH,
        )

    for k in range(1, tiles * pairs):
        gather_copy(k).start()
    gath[tile * pairs + pair] = gsend[...]

    cell_at = lax.broadcasted_iota(jnp.int32, (LANES, ny), 0)
    fine_at = lax.broadcasted_iota(jnp.int32, (LANES, ny), 1)
    parent = fine_at // EDGE
    spread = jnp.where(cell_at == parent, 1.0, 0.0).astype(jnp.bfloat16)
    beside_y = parent + 2 * (fine_at // HALF % 2) - 1
    spread_y = jnp.where(cell_at == beside_y, 1.0, 0.0).astype(jnp.bfloat16)

    for k in range(1, tiles * pairs):
        frm = lax.rem(tile * pairs + pair + tiles * pairs - k, tiles * pairs)
        pltpu.make_async_remote_copy(
            gsend, gath.at[frm], g_send.at[k], g_recv.at[frm],
            device_id=(tile, layer), device_id_type=MESH,
        ).wait_recv()

    for t in range(tiles):
        total = gath[t * pairs]
        for p in range(1, pairs):
            total = total + gath[t * pairs + p]
        gsum[pl.ds(t * rows, rows), :] = total
    lane_t = lax.broadcasted_iota(jnp.int32, (tiles, LANES), 1)

    def value(v):
        a = gsum[pl.ds(v % rows, tiles, stride=rows), :]
        if v >= rows:
            a = pltpu.roll(a, LANES - span, 1)
        return only(lane_t < span, a)

    def shifted(a, offset):
        ox, oz, oy = offset
        along = -(oz * cells + oy) % LANES
        if along:
            a = pltpu.roll(a, along, 1)
        if ox:
            a = pltpu.roll(a, -ox % tiles, 0)
        return a

    offsets = [((v + 13) // 9 - 1, (v + 13) // 3 % 3 - 1, (v + 13) % 3 - 1) for v in range(14)]
    forward = [value(v) for v in range(14)]
    backward = [
        shifted(forward[v], [-d for d in offsets[v]]) if v else None for v in range(14)
    ]
    rhs = value(RHS)
    scale = COARSE_DAMPING / jnp.where(lane_t < span, forward[0], 1.0)
    coarse = rhs * scale
    for _ in range(SWEEPS - 1):
        applied = forward[0] * coarse
        for v in range(1, 14):
            applied = applied + forward[v] * shifted(coarse, offsets[v])
            applied = applied + backward[v] * shifted(coarse, [-d for d in offsets[v]])
        coarse = coarse + (rhs - applied) * scale
    csc[...] = coarse

    def coarse_row(t, p):
        a = jnp.broadcast_to(csc[pl.ds(t, 1), :], (SUB, LANES))
        return pltpu.roll(a, (LANES - p * cells) % LANES, 1)

    center = coarse_row(tile, pair)
    four = jnp.concatenate(
        [
            center,
            coarse_row(tile, near_pair),
            coarse_row(jnp.maximum(tile - 1, 0), pair),
            coarse_row(jnp.minimum(tile + 1, tiles - 1), pair),
        ],
        axis=0,
    )
    wide = split_dot(spread, four, swap=True)
    c_own, c_z = wide[:SUB, :], wide[SUB : 2 * SUB, :]
    c_y = split_dot(spread_y, center, swap=True)
    ze[0] = ze[0] * jnp.concatenate([c_z] * (nx // SUB), axis=0)
    at_edge = sub == parity * (SUB - 1)
    for i in range(nx):
        at = plane(i + 1)
        result = own_s[at, :] * c_own + oy_s[at, :] * c_y
        result = result + only(at_edge, ze[0, pl.ds(i, 1), :])
        if i == 0:
            result = result + ox_s[plane(1), :] * wide[2 * SUB : 3 * SUB, :]
        if i == nx - 1:
            result = result + ox_s[plane(2), :] * wide[3 * SUB :, :]
        out_ref[plane(i), :] = result

    for sz in sides:
        @pl.when(has(0, sz))
        def _():
            for n in range(3):
                layer_copy(sz, n).wait_send()
    for sx in sides:
        @pl.when(has(sx, 0))
        def _():
            for copy in halo_copies(sx):
                copy.wait_send()
    for sx, sz in diagonals:
        @pl.when(has(sx, sz))
        def _():
            corner_copy(sx, sz).wait_send()
    for item in fold_list:
        @pl.when(fold_valid(*item))
        def _():
            fold_copy(*item).wait_send()
    for k in range(1, tiles * pairs):
        gather_copy(k).wait_send()


def body(tiles, layers, classes, well_mask, source):
    nx, nz, ny = classes.shape
    assert nx == EDGE and nz == HALF == SUB and layers % 2 == 0
    cells, pairs = ny // EDGE, layers // 2
    assert 4 * cells <= LANES and pairs * cells <= LANES
    rows = VALUES // 2 if 2 * pairs * cells <= LANES else VALUES
    flat = lambda a: a.reshape(nx * nz, ny)
    f32 = lambda *shape: pltpu.VMEM(shape, jnp.float32)
    dma = pltpu.SemaphoreType.DMA
    block = (nx * SUB, ny)
    wide = ((nx + 2) * SUB, ny)
    scratch = [
        pltpu.VMEM(block, jnp.int32), pltpu.VMEM(block, jnp.int32), f32(*block),
        pltpu.VMEM((6 * VALUES, 4 * PADDED), jnp.bfloat16),
        f32((nx + 4) * SUB, ny), f32(*wide), f32(2, 3, nx, ny), f32(2, 3, nx, ny),
        f32(4, 1, ny), f32(4, 1, ny),
        f32(2, 2, nx, ny), f32(4, nx, ny),
        f32(*block), f32(*block), f32((nx + 1) * SUB, ny), f32(*block), f32(*block), f32(*block),
        f32(*wide), f32(*wide), f32(*wide), f32(4 * SUB, ny), f32(2, nx, ny), f32(2, 4, nx, ny),
        pltpu.VMEM((3, nx, ny), jnp.int32), pltpu.VMEM((ny, LANES), jnp.bfloat16), f32(PADDED * SUB, ny), f32(6, rows, LANES), f32(12, rows, LANES), f32(rows, LANES),
        f32(tiles * pairs, rows, LANES), f32(tiles * rows, LANES), f32(tiles, LANES),
        dma((4,)), dma((2, 2)), dma((2, 2)), dma((2, 3)), dma((2, 3)), dma((4,)), dma((4,)),
        dma((12,)), dma((12,)), dma((tiles * pairs,)), dma((tiles * pairs,)),
    ]
    route = jnp.asarray(routing_table(), jnp.bfloat16)
    result = pl.pallas_call(
        functools.partial(kernel, tiles, layers, nx, ny),
        out_shape=jax.ShapeDtypeStruct(block, jnp.float32),
        in_specs=[pl.BlockSpec(memory_space=pltpu.HBM)] * 4,
        out_specs=pl.BlockSpec(memory_space=pltpu.VMEM),
        scratch_shapes=scratch,
        compiler_params=pltpu.CompilerParams(
            collective_id=0, has_side_effects=True, vmem_limit_bytes=215 * 2**18
        ),
    )(flat(classes), flat(well_mask), flat(source), route)
    return result.reshape(nx, nz, ny)


def solution(mesh):
    spec = P("tile", "layer", None)
    return jax.shard_map(
        functools.partial(body, mesh.shape["tile"], mesh.shape["layer"]),
        mesh=mesh, in_specs=(spec, spec, spec), out_specs=spec, check_vma=False,
    )
```

```python
import functools

import jax
import jax.numpy as jnp
import numpy as np
from jax import lax
from jax.experimental import pallas as pl
from jax.experimental.pallas import tpu as pltpu
from jax.sharding import PartitionSpec as P

EDGE = 16
HALF = EDGE // 2
CLASSES = 16
SWEEPS = 4
FINE_DAMPING = 0.67
COARSE_DAMPING = 0.5
SINK_RATE = 0.5
VERTICAL_RATIO = 0.25
LANES = 128
SUB = 8
VALUES = 16
RHS = 14
MESH = pl.DeviceIdType.MESH

OWN, OX, OZ, OY = range(4)
FULL_OFFSETS = ((0, 0, 0), (0, 0, 1), (0, 1, 0), (0, 1, 1), None)
EDGE_OFFSETS = ((1, 0, 0), (1, 0, 1), (1, 1, 0))
PRODUCTS = (
    [(w, b, 0) for w in (OWN, OZ, OY) for b in FULL_OFFSETS]
    + [(OX, b, -1) for b in FULL_OFFSETS]
    + [(OX, None, 1)]
    + [(w, b, 1) for w in (OWN, OZ, OY, OX) for b in EDGE_OFFSETS]
    + [(OX, b, -1) for b in EDGE_OFFSETS]
)
SLOT = {product: index for index, product in enumerate(PRODUCTS)}
PADDED = -(-len(PRODUCTS) // SUB) * SUB


def routing_table():
    table = np.zeros((2, 6 * VALUES, 4 * PADDED), np.float32)
    for parity, sign_z in ((0, -1), (1, 1)):
        for n, (weight, toggled, sign_x) in enumerate(PRODUCTS):
            for half, sign_y in ((0, -1), (1, 1)):
                row = ((weight == OX) * sign_x, (weight == OZ) * sign_z, (weight == OY) * sign_y)
                if toggled is None:
                    value = RHS
                else:
                    column = (toggled[0] * sign_x, toggled[1] * sign_z, toggled[2] * sign_y)
                    o = [column[d] - row[d] for d in range(3)]
                    value = 9 * (o[0] + 1) + 3 * (o[1] + 1) + (o[2] + 1) - 13
                    if value < 0:
                        continue
                group = 2 * (weight == OY) + half
                target = (row[0] + 1) * 2 + (weight == OZ)
                table[parity, target * VALUES + value, group * PADDED + n] = 1.0
    return table


def split_dot(table, values, swap=False):
    total = None
    rest = values
    for _ in range(2):
        part = rest.astype(jnp.bfloat16)
        rest = rest - part.astype(jnp.float32)
        pair = (part, table) if swap else (table, part)
        term = jnp.dot(*pair, preferred_element_type=jnp.float32)
        total = term if total is None else total + term
    return total


def tree_sum(terms):
    while len(terms) > 1:
        terms = [sum(terms[n + 1 : n + 2], terms[n]) for n in range(0, len(terms), 2)]
    return terms[0]


def inverse_of(a):
    guarded = jnp.maximum(a, 1e-30)
    guess = pl.reciprocal(guarded, approx=True)
    return guess * (2.0 - guarded * guess)


def harmonic(a, b):
    return 2.0 * a * b * inverse_of(a + b)


def perm_of(classes):
    step = 5.0 / (CLASSES - 1)
    return jnp.exp(classes.astype(jnp.float32) * step - 2.5)


def sink_of(well, perm):
    return SINK_RATE * well.astype(jnp.float32) * perm


def kernel(
    tiles, layers, nx, ny,
    cls_hbm, well_hbm, src_hbm, route_hbm, out_ref,
    cls, well, src, route,
    kx, sk, zs, zr, crs, crr, zq, ze,
    typ_s, tzi_s, txf, tzm_s, tzp_s, d_s, own_s, oy_s, oz_s, ox_s, tz_edge, zb,
    zi, half_table, acc, part, fold, gsend, gath, gsum, csc,
    in_sem, x_send, x_recv, z_send, z_recv, c_send, c_recv, f_send, f_recv, g_send, g_recv,
):
    tile = lax.axis_index("tile")
    layer = lax.axis_index("layer")
    pairs = layers // 2
    pair = layer // 2
    parity = layer % 2
    cells = ny // EDGE
    span = pairs * cells
    rows = part.shape[1]
    plane = lambda i: pl.ds(i * SUB, SUB)

    loads = [
        pltpu.make_async_copy(a, b, in_sem.at[n])
        for n, (a, b) in enumerate(
            ((cls_hbm, cls), (well_hbm, well), (src_hbm, src), (route_hbm.at[parity], route))
        )
    ]
    loads[0].start()
    loads[1].start()

    barrier = pltpu.get_barrier_semaphore()
    for a in range(tiles):
        for b in range(layers):
            if a or b:
                pl.semaphore_signal(
                    barrier, inc=1, device_id_type=MESH,
                    device_id=(lax.rem(tile + a, tiles), lax.rem(layer + b, layers)),
                )

    def fold_from(dt, role):
        from_layer = 2 * pair - 1 + role
        ok = (tile + dt >= 0) & (tile + dt < tiles)
        ok = ok & (from_layer >= 0) & (from_layer < layers)
        return ok & (from_layer != layer) if dt == 0 else ok

    for dt in (-1, 0, 1):
        for role in range(4):
            @pl.when(jnp.logical_not(fold_from(dt, role)))
            def _():
                fold[(dt + 1) * 4 + role] = jnp.zeros(fold.shape[1:], jnp.float32)

    loads[0].wait()
    loads[1].wait()
    loads[2].start()
    loads[3].start()

    for i in (0, 1, nx - 2, nx - 1):
        k = perm_of(cls[plane(i), :])
        kx[plane(i + 2), :] = k
        if i in (0, nx - 1):
            sk[plane(i + 1), :] = sink_of(well[plane(i), :], k)
    for side, (z1, z2) in enumerate(((0, 1), (SUB - 1, SUB - 2))):
        for i in range(nx):
            zi[0, pl.ds(i, 1), :] = cls[pl.ds(i * SUB + z1, 1), :]
            zi[1, pl.ds(i, 1), :] = cls[pl.ds(i * SUB + z2, 1), :]
            zi[2, pl.ds(i, 1), :] = well[pl.ds(i * SUB + z1, 1), :]
        k = perm_of(zi[0])
        zs[side, 0] = k
        zs[side, 1] = perm_of(zi[1])
        zs[side, 2] = sink_of(zi[2], k)
        crs[0 + side] = k[0:1, :]
        crs[2 + side] = k[nx - 1 : nx, :]

    pl.semaphore_wait(barrier, tiles * layers - 1)

    def halo_copies(sx):
        lo = sx < 0
        src_k = kx.at[pl.ds((2 if lo else nx) * SUB, 2 * SUB), :]
        dst_k = kx.at[pl.ds((nx + 2 if lo else 0) * SUB, 2 * SUB), :]
        src_s = sk.at[plane(1 if lo else nx), :]
        dst_s = sk.at[plane(nx + 1 if lo else 0), :]
        s = 0 if lo else 1
        return [
            pltpu.make_async_remote_copy(
                a, b, x_send.at[s, n], x_recv.at[s, n],
                device_id=(tile + sx, layer), device_id_type=MESH,
            )
            for n, (a, b) in enumerate(((src_k, dst_k), (src_s, dst_s)))
        ]

    def layer_copy(sz, n):
        s = 0 if sz < 0 else 1
        return pltpu.make_async_remote_copy(
            zs.at[s, n], zr.at[1 - s, n], z_send.at[s, n], z_recv.at[s, n],
            device_id=(tile, layer + sz), device_id_type=MESH,
        )

    def corner_copy(sx, sz):
        a, b = (0 if sx < 0 else 1), (0 if sz < 0 else 1)
        return pltpu.make_async_remote_copy(
            crs.at[2 * a + b], crr.at[2 * (1 - a) + (1 - b)],
            c_send.at[2 * a + b], c_recv.at[2 * a + b],
            device_id=(tile + sx, layer + sz), device_id_type=MESH,
        )

    def has(sx, sz):
        ok = None
        for s, at, count in ((sx, tile, tiles), (sz, layer, layers)):
            if s:
                test = at > 0 if s < 0 else at < count - 1
                ok = test if ok is None else ok & test
        return ok

    sides = (-1, 1)
    diagonals = [(sx, sz) for sx in sides for sz in sides]
    for sz in sides:
        @pl.when(has(0, sz))
        def _():
            layer_copy(sz, 0).start()

        @pl.when(jnp.logical_not(has(0, sz)))
        def _():
            zr[0 if sz < 0 else 1] = jnp.zeros(zr.shape[1:], jnp.float32)
    for sx in sides:
        @pl.when(has(sx, 0))
        def _():
            for copy in halo_copies(sx):
                copy.start()

        @pl.when(jnp.logical_not(has(sx, 0)))
        def _():
            first = 0 if sx < 0 else nx + 2
            kx[pl.ds(first * SUB, 2 * SUB), :] = jnp.zeros((2 * SUB, ny), jnp.float32)
            sk[plane(0 if sx < 0 else nx + 1), :] = jnp.zeros((SUB, ny), jnp.float32)
    for sx, sz in diagonals:
        @pl.when(has(sx, sz))
        def _():
            corner_copy(sx, sz).start()

        @pl.when(jnp.logical_not(has(sx, sz)))
        def _():
            crr[2 * (0 if sx < 0 else 1) + (0 if sz < 0 else 1)] = jnp.zeros((1, ny), jnp.float32)
    for sz in sides:
        @pl.when(has(0, sz))
        def _():
            layer_copy(sz, 1).start()
            layer_copy(sz, 2).start()

    sub = lax.broadcasted_iota(jnp.int32, (SUB, ny), 0)
    lane = lax.broadcasted_iota(jnp.int32, (SUB, ny), 1)
    even = parity == 0
    cross_ym = lane % EDGE == 0
    cross_yp = lane % EDGE == EDGE - 1
    cross_zm = (sub == 0) & even
    cross_zp = (sub == SUB - 1) & jnp.logical_not(even)

    def up(a, dim):
        return pltpu.roll(a, 1, dim)

    def down(a, dim):
        return pltpu.roll(a, a.shape[dim] - 1, dim)

    def y_face(k):
        at = lax.broadcasted_iota(jnp.int32, k.shape, 1)
        return jnp.where(at == ny - 1, 0.0, harmonic(k, down(k, 1)))

    def only(mask, a):
        return jnp.where(mask, a, 0.0)

    for i in range(2, nx - 2):
        k = perm_of(cls[plane(i), :])
        kx[plane(i + 2), :] = k
        sk[plane(i + 1), :] = sink_of(well[plane(i), :], k)
    for i in (1, nx - 2):
        sk[plane(i + 1), :] = sink_of(well[plane(i), :], kx[plane(i + 2), :])

    def faces(i):
        at = plane(i)
        k = kx[plane(i + 2), :]
        typ_s[at, :] = y_face(k)
        tzi_s[at, :] = VERTICAL_RATIO * harmonic(k, up(k, 0))

        if i > 0:
            txf[at, :] = harmonic(kx[plane(i + 1), :], k)

    for i in range(nx):
        faces(i)

    fine = lax.broadcasted_iota(jnp.int32, (ny, LANES), 0)
    spot = lax.broadcasted_iota(jnp.int32, (ny, LANES), 1)
    group = spot // cells
    upper = group % 2
    wanted = fine // EDGE + jnp.where(group >= 2, 2 * upper - 1, 0)
    hit = (fine // HALF % 2 == upper) & (wanted == spot % cells) & (group < 4)
    half_table[...] = jnp.where(hit, 1.0, 0.0).astype(jnp.bfloat16)

    def wait_layers(n):
        for sz in sides:
            @pl.when(has(0, sz))
            def _():
                layer_copy(-sz, n).wait_recv()

    wait_layers(0)
    for sx in sides:
        @pl.when(has(sx, 0))
        def _():
            halo_copies(-sx)[0].wait_recv()
    txf[plane(0), :] = harmonic(kx[plane(1), :], kx[plane(2), :])
    txf[plane(nx), :] = harmonic(kx[plane(nx + 1), :], kx[plane(nx + 2), :])
    for side in (0, 1):
        tz_edge[side] = VERTICAL_RATIO * harmonic(zs[side, 0], zr[side, 0])

    def basis(sink, faces, crossing):
        diagonal = sink
        for pair_of in faces:
            diagonal = diagonal + pair_of[0] + pair_of[1]
        inverse = FINE_DAMPING * inverse_of(diagonal)
        leaving = sink
        for term in crossing:
            if term is not None:
                leaving = leaving + term
        outer = [None if term is None else term * inverse for term in crossing]
        return diagonal, 1.0 - leaving * inverse, outer

    def block_basis(i, edge):
        at = plane(i)
        after = plane(i + 1)
        inner = tzi_s[at, :]
        tzm = jnp.where(sub == 0, tz_edge[0, pl.ds(i, 1), :], inner)
        tzp = jnp.where(sub == SUB - 1, tz_edge[1, pl.ds(i, 1), :], down(inner, 0))
        txm = txf[at, :]
        txp = txf[after, :]
        typ = typ_s[at, :]
        tym = up(typ, 1)
        crossing = (
            None if edge == 0 else (txm if edge < 0 else txp),
            only(cross_zm, tzm) + only(cross_zp, tzp),
            only(cross_ym, tym) + only(cross_yp, typ),
        )
        diagonal, own, outer = basis(
            sk[after, :], ((txm, txp), (tzm, tzp), (tym, typ)), crossing
        )
        tzm_s[at, :] = tzm
        tzp_s[at, :] = tzp
        d_s[at, :] = diagonal
        own_s[after, :] = own
        if i >= nx - 2:
            oz_s[after, :] = outer[1]
        oy_s[after, :] = outer[2]
        if edge:
            ox_s[plane(1 if edge < 0 else 2), :] = outer[0]

    for i in range(nx):
        block_basis(i, -1 if i == 0 else int(i == nx - 1))

    for sx in sides:
        @pl.when(has(sx, 0))
        def _():
            halo_copies(-sx)[1].wait_recv()
    for sx, sz in diagonals:
        @pl.when(has(sx, sz))
        def _():
            corner_copy(-sx, -sz).wait_recv()

    for side in (0, 1):
        k1 = kx[plane(1 if side == 0 else nx + 2), :]
        k2 = kx[plane(0 if side == 0 else nx + 3), :]
        toward = txf[plane(0 if side == 0 else nx), :]
        inner = VERTICAL_RATIO * harmonic(k1, up(k1, 0))
        tzm = jnp.where(sub == 0, VERTICAL_RATIO * harmonic(k1, crr[2 * side]), inner)
        tzp = jnp.where(
            sub == SUB - 1, VERTICAL_RATIO * harmonic(k1, crr[2 * side + 1]), down(inner, 0)
        )
        typ = y_face(k1)
        tym = up(typ, 1)
        crossing = (
            toward,
            only(cross_zm, tzm) + only(cross_zp, tzp),
            only(cross_ym, tym) + only(cross_yp, typ),
        )
        _, own, outer = basis(
            sk[plane(0 if side == 0 else nx + 1), :],
            ((toward, harmonic(k1, k2)), (tzm, tzp), (tym, typ)),
            crossing,
        )
        at = plane(0 if side == 0 else nx + 1)
        own_s[at, :] = own
        ox_s[plane(0 if side == 0 else 3), :] = outer[0]
        oz_s[at, :] = outer[1]
        oy_s[at, :] = outer[2]

    wait_layers(1)
    wait_layers(2)
    wide_row = lax.broadcasted_iota(jnp.int32, (nx, ny), 0)
    wide_lane = lax.broadcasted_iota(jnp.int32, (nx, ny), 1)
    for side in (0, 1):
        k1 = zr[side, 0]
        k2 = zr[side, 1]
        toward = tz_edge[side]
        inner = harmonic(k1, up(k1, 0))
        txm = jnp.where(wide_row == 0, harmonic(k1, crr[side]), inner)
        txp = jnp.where(wide_row == nx - 1, harmonic(k1, crr[2 + side]), down(inner, 0))
        typ = y_face(k1)
        tym = up(typ, 1)
        crosses = even if side == 0 else jnp.logical_not(even)
        crossing = (
            only(wide_row == 0, txm) + only(wide_row == nx - 1, txp),
            toward * crosses.astype(jnp.float32),
            only(wide_lane % EDGE == 0, tym) + only(wide_lane % EDGE == EDGE - 1, typ),
        )
        _, own, outer = basis(
            zr[side, 2],
            ((txm, txp), (toward, VERTICAL_RATIO * harmonic(k1, k2)), (tym, typ)),
            crossing,
        )
        zb[side, OWN] = own
        zb[side, OX] = outer[0]
        zb[side, OZ] = outer[1]
        zb[side, OY] = outer[2]
        zq[side, 0] = jnp.where(crosses, outer[1], own)
        zq[side, 1] = jnp.where(crosses, 0.0, outer[2])

    loads[2].wait()
    loads[3].wait()

    sums_of = {}

    def add(product, term):
        sums_of[product] = sums_of[product] + term if product in sums_of else term

    def products(i, edge):
        at, mid, after, row = plane(i), plane(i + 1), plane(i + 2), pl.ds(i, 1)
        diagonal, tzm, tzp, typ = d_s[at, :], tzm_s[at, :], tzp_s[at, :], typ_s[at, :]
        tym = up(typ, 1)
        txm, txp = txf[at, :], txf[mid, :]
        own, oy = own_s[mid, :], oy_s[mid, :]
        source = src[at, :]
        swap_m, swap_p = jnp.where(cross_yp, oy, own), jnp.where(cross_ym, oy, own)
        keep_m, keep_p = jnp.where(cross_yp, own, oy), jnp.where(cross_ym, own, oy)

        def z_pair(a, kind):
            return (
                jnp.where(sub == 0, zq[0, kind, row, :], up(a, 0)),
                jnp.where(sub == SUB - 1, zq[1, kind, row, :], down(a, 0)),
            )

        own_zm, own_zp = z_pair(own, 0)
        oy_zm, oy_zp = z_pair(oy, 1)
        before_own = ox_s[plane(0), :] if edge < 0 else own_s[at, :]
        after_own = ox_s[plane(3), :] if edge > 0 else own_s[after, :]
        q0 = (
            diagonal * own - txm * before_own - txp * after_own
            - tym * up(swap_m, 1) - typ * down(swap_p, 1) - tzm * own_zm - tzp * own_zp
        )
        qy = (
            diagonal * oy - tym * up(keep_m, 1) - typ * down(keep_p, 1)
            - tzm * oy_zm - tzp * oy_zp
        )
        if edge >= 0:
            qy = qy - txm * oy_s[at, :]
        if edge <= 0:
            qy = qy - txp * oy_s[after, :]
        fields = (((0, 0, 0), q0), ((0, 0, 1), qy), (None, source))
        for kind, weight in ((OWN, own), (OY, oy)):
            for offset, field in fields:
                add((kind, offset, 0), weight * field)
        if not edge:
            return
        ox = ox_s[plane(1 if edge < 0 else 2), :]
        if edge < 0:
            for offset, field in fields:
                add((OX, offset, -1), ox * field)
            across, t_across = plane(0), txm
        else:
            add((OX, None, 1), ox * source)
            across, t_across = plane(nx + 1), txp
        tymc, typc = only(cross_ym, tym), only(cross_yp, typ)
        tzmc, tzpc = only(cross_zm, tzm), only(cross_zp, tzp)
        ox_ym, ox_yp = up(ox, 1), down(ox, 1)
        ox_zm = jnp.where(sub == 0, zb[0, OX, row, :], up(ox, 0))
        ox_zp = jnp.where(sub == SUB - 1, zb[1, OX, row, :], down(ox, 0))
        qx = (
            diagonal * ox - t_across * own_s[across, :] - (tym - tymc) * ox_ym
            - (typ - typc) * ox_yp - (tzm - tzmc) * ox_zm - (tzp - tzpc) * ox_zp
        )
        qxy = -(t_across * oy_s[across, :] + tymc * ox_ym + typc * ox_yp)
        qxz = -(t_across * oz_s[across, :] + tzmc * ox_zm + tzpc * ox_zp)
        for offset, field in zip(EDGE_OFFSETS, (qx, qxy, qxz)):
            add((OX, offset, edge), ox * field)
            if edge > 0:
                for kind, weight in ((OWN, own), (OZ, oz_s[mid, :]), (OY, oy)):
                    add((kind, offset, 1), weight * field)
        if edge > 0:
            inward = -txm * ox
            for kind, ref in ((OWN, own_s), (OZ, oz_s), (OY, oy_s)):
                add((kind, EDGE_OFFSETS[0], 1), ref[at, :] * inward)

    for i in range(nx):
        products(i, -1 if i == 0 else int(i == nx - 1))

    z1 = parity * (SUB - 1)
    z2 = 1 + parity * (SUB - 3)
    for i in range(nx):
        ze[1, pl.ds(i, 1), :] = own_s[pl.ds((i + 1) * SUB + z2, 1), :]
        ze[2, pl.ds(i, 1), :] = oy_s[pl.ds((i + 1) * SUB + z2, 1), :]
        ze[3, pl.ds(i, 1), :] = src[pl.ds(i * SUB + z1, 1), :]
    first, last = wide_row == 0, wide_row == nx - 1
    wide_ym, wide_yp = wide_lane % EDGE == 0, wide_lane % EDGE == EDGE - 1
    k1 = zs[parity, 0]
    t_out = tz_edge[parity]
    t_in = VERTICAL_RATIO * harmonic(k1, zs[parity, 1])
    inner = harmonic(k1, up(k1, 0))
    txm = jnp.where(first, harmonic(k1, kx[pl.ds(SUB + z1, 1), :]), inner)
    txp = jnp.where(last, harmonic(k1, kx[pl.ds((nx + 2) * SUB + z1, 1), :]), down(inner, 0))
    typ = y_face(k1)
    tym = up(typ, 1)
    txmc, txpc = only(first, txm), only(last, txp)
    tymc, typc = only(wide_ym, tym), only(wide_yp, typ)
    diagonal, own, (ox, oz, oy) = basis(
        zs[parity, 2], ((txm, txp), (t_in, t_out), (tym, typ)),
        (txmc + txpc, t_out, tymc + typc),
    )
    ze[0] = oz
    txmn, txpn, tymn, typn = txm - txmc, txp - txpc, tym - tymc, typ - typc
    own_in, oy_in, source = ze[1], ze[2], ze[3]
    ox_before, ox_after = ox_s[pl.ds(z1, 1), :], ox_s[pl.ds(3 * SUB + z1, 1), :]
    oz_ym, oz_yp = up(oz, 1), down(oz, 1)
    q0 = (
        diagonal * own - t_out * zb[parity, OZ] - t_in * own_in
        - txm * jnp.where(first, ox_before, up(own, 0))
        - txp * jnp.where(last, ox_after, down(own, 0))
        - tym * up(jnp.where(wide_yp, oy, own), 1) - typ * down(jnp.where(wide_ym, oy, own), 1)
    )
    qy = (
        diagonal * oy - t_in * oy_in - txmn * up(oy, 0) - txpn * down(oy, 0)
        - tym * up(jnp.where(wide_yp, own, oy), 1) - typ * down(jnp.where(wide_ym, own, oy), 1)
    )
    qz = (
        diagonal * oz - t_out * zb[parity, OWN] - txmn * up(oz, 0) - txpn * down(oz, 0)
        - tymn * oz_ym - typn * oz_yp
    )
    qz_in = -t_in * oz
    qzy = -(tymc * oz_ym + typc * oz_yp + t_out * zb[parity, OY])

    def add_rows(product, term):
        add(product, term[:SUB, :] + term[SUB:, :])

    for offset, field in zip(FULL_OFFSETS, (q0, qy, qz, qzy, source)):
        add_rows((OZ, offset, 0), oz * field)
    add_rows((OWN, FULL_OFFSETS[2], 0), own * qz + own_in * qz_in)
    add_rows((OY, FULL_OFFSETS[2], 0), oy * qz + oy_in * qz_in)
    add_rows((OWN, FULL_OFFSETS[3], 0), own * qzy)
    add_rows((OY, FULL_OFFSETS[3], 0), oy * qzy)
    add_rows((OX, FULL_OFFSETS[3], -1), only(first, ox * qzy))
    ox_in = only(first, ox_s[pl.ds(SUB + z2, 1), :])
    add_rows((OX, FULL_OFFSETS[2], -1), only(first, ox * qz) + ox_in * qz_in)
    for n in range(PADDED):
        acc[plane(n), :] = (
            sums_of[PRODUCTS[n]] if n < len(PRODUCTS) else jnp.zeros((SUB, ny), jnp.float32)
        )

    halves = split_dot(half_table[...], acc[...], swap=True)
    sums = halves.reshape(PADDED, SUB, LANES).sum(axis=1)
    stacked = jnp.concatenate(
        [sums] + [pltpu.roll(sums, LANES - g * cells, 1) for g in (1, 2, 3)], axis=0
    )
    routed = split_dot(route[...], stacked)
    routed = jnp.where(
        lax.broadcasted_iota(jnp.int32, routed.shape, 1) < cells, routed, 0.0
    )
    beside_pair = pair + 2 * parity - 1
    near_pair = jnp.clip(beside_pair, 0, pairs - 1)
    for target in range(6):
        block = routed[target * VALUES : (target + 1) * VALUES, :]
        if rows < VALUES:
            block = block[:rows, :] + pltpu.roll(block[rows:, :], span, 1)
        to_pair = near_pair if target % 2 else pair
        part[target] = pltpu.roll(block, to_pair * cells, 1)

    def fold_copy(sx, beside, which):
        to_pair = beside_pair if beside else pair
        role = layer - 2 * to_pair + 1
        slot = (1 - sx) * 4 + role
        n = ((sx + 1) * 2 + beside) * 2 + which
        return pltpu.make_async_remote_copy(
            part.at[(sx + 1) * 2 + beside], fold.at[slot], f_send.at[n], f_recv.at[slot],
            device_id=(tile + sx, 2 * to_pair + which), device_id_type=MESH,
        )

    def fold_valid(sx, beside, which):
        ok = (tile + sx >= 0) & (tile + sx < tiles)
        if beside:
            return ok & (beside_pair >= 0) & (beside_pair < pairs)
        return ok if sx else ok & (which != parity)

    fold_list = [(sx, b, w) for b in (1, 0) for sx in (-1, 1, 0) for w in (0, 1)]
    for item in fold_list:
        @pl.when(fold_valid(*item))
        def _():
            fold_copy(*item).start()

    for dt in (-1, 0, 1):
        for role in range(4):
            slot = (dt + 1) * 4 + role

            @pl.when(fold_from(dt, role))
            def _():
                pltpu.make_async_remote_copy(
                    part.at[0], fold.at[slot], f_send.at[0], f_recv.at[slot],
                    device_id=(tile, layer), device_id_type=MESH,
                ).wait_recv()

    terms = [part[2]] + [fold[slot] for slot in range(12)]
    gsend[...] = tree_sum(terms)

    def gather_copy(k):
        other = lax.rem(tile * pairs + pair + k, tiles * pairs)
        return pltpu.make_async_remote_copy(
            gsend, gath.at[tile * pairs + pair], g_send.at[k], g_recv.at[tile * pairs + pair],
            device_id=(other // pairs, 2 * (other % pairs) + parity), device_id_type=MESH,
        )

    for k in range(1, tiles * pairs):
        gather_copy(k).start()
    gath[tile * pairs + pair] = gsend[...]

    cell_at = lax.broadcasted_iota(jnp.int32, (LANES, ny), 0)
    fine_at = lax.broadcasted_iota(jnp.int32, (LANES, ny), 1)
    parent = fine_at // EDGE
    spread = jnp.where(cell_at == parent, 1.0, 0.0).astype(jnp.bfloat16)
    beside_y = parent + 2 * (fine_at // HALF % 2) - 1
    spread_y = jnp.where(cell_at == beside_y, 1.0, 0.0).astype(jnp.bfloat16)

    for sz in sides:
        @pl.when(has(0, sz))
        def _():
            for n in range(3):
                layer_copy(sz, n).wait_send()
    for sx in sides:
        @pl.when(has(sx, 0))
        def _():
            for copy in halo_copies(sx):
                copy.wait_send()
    for sx, sz in diagonals:
        @pl.when(has(sx, sz))
        def _():
            corner_copy(sx, sz).wait_send()
    for item in fold_list:
        @pl.when(fold_valid(*item))
        def _():
            fold_copy(*item).wait_send()
    for k in range(1, tiles * pairs):
        gather_copy(k).wait_send()

    for k in range(1, tiles * pairs):
        frm = lax.rem(tile * pairs + pair + tiles * pairs - k, tiles * pairs)
        pltpu.make_async_remote_copy(
            gsend, gath.at[frm], g_send.at[k], g_recv.at[frm],
            device_id=(tile, layer), device_id_type=MESH,
        ).wait_recv()

    for t in range(tiles):
        total = gath[t * pairs]
        for p in range(1, pairs):
            total = total + gath[t * pairs + p]
        gsum[pl.ds(t * rows, rows), :] = total
    lane_t = lax.broadcasted_iota(jnp.int32, (tiles, LANES), 1)

    def value(v):
        a = gsum[pl.ds(v % rows, tiles, stride=rows), :]
        if v >= rows:
            a = pltpu.roll(a, LANES - span, 1)
        return only(lane_t < span, a)

    def shifted(a, offset):
        ox, oz, oy = offset
        along = -(oz * cells + oy) % LANES
        if along:
            a = pltpu.roll(a, along, 1)
        if ox:
            a = pltpu.roll(a, -ox % tiles, 0)
        return a

    offsets = [((v + 13) // 9 - 1, (v + 13) // 3 % 3 - 1, (v + 13) % 3 - 1) for v in range(14)]
    forward = [value(v) for v in range(14)]
    backward = [
        shifted(forward[v], [-d for d in offsets[v]]) if v else None for v in range(14)
    ]
    rhs = value(RHS)
    scale = COARSE_DAMPING / jnp.where(lane_t < span, forward[0], 1.0)
    coarse = rhs * scale
    for _ in range(SWEEPS - 1):
        terms = [forward[0] * coarse]
        for v in range(1, 14):
            terms.append(forward[v] * shifted(coarse, offsets[v]))
            terms.append(backward[v] * shifted(coarse, [-d for d in offsets[v]]))
        coarse = coarse + (rhs - tree_sum(terms)) * scale
    csc[...] = coarse

    def coarse_row(t, p):
        a = jnp.broadcast_to(csc[pl.ds(t, 1), :], (SUB, LANES))
        return pltpu.roll(a, (LANES - p * cells) % LANES, 1)

    center = coarse_row(tile, pair)
    four = jnp.concatenate(
        [
            center,
            coarse_row(tile, near_pair),
            coarse_row(jnp.maximum(tile - 1, 0), pair),
            coarse_row(jnp.minimum(tile + 1, tiles - 1), pair),
        ],
        axis=0,
    )
    wide = split_dot(spread, four, swap=True)
    c_own, c_z = wide[:SUB, :], wide[SUB : 2 * SUB, :]
    c_y = split_dot(spread_y, center, swap=True)
    ze[0] = ze[0] * jnp.concatenate([c_z] * (nx // SUB), axis=0)
    at_edge = sub == parity * (SUB - 1)
    for i in range(nx):
        at = plane(i + 1)
        result = own_s[at, :] * c_own + oy_s[at, :] * c_y
        result = result + only(at_edge, ze[0, pl.ds(i, 1), :])
        if i == 0:
            result = result + ox_s[plane(1), :] * wide[2 * SUB : 3 * SUB, :]
        if i == nx - 1:
            result = result + ox_s[plane(2), :] * wide[3 * SUB :, :]
        out_ref[plane(i), :] = result


def body(tiles, layers, classes, well_mask, source):
    nx, nz, ny = classes.shape
    assert nx == EDGE and nz == HALF == SUB and layers % 2 == 0
    cells, pairs = ny // EDGE, layers // 2
    assert 4 * cells <= LANES and pairs * cells <= LANES
    rows = VALUES // 2 if 2 * pairs * cells <= LANES else VALUES
    flat = lambda a: a.reshape(nx * nz, ny)
    f32 = lambda *shape: pltpu.VMEM(shape, jnp.float32)
    dma = pltpu.SemaphoreType.DMA
    block = (nx * SUB, ny)
    wide = ((nx + 2) * SUB, ny)
    scratch = [
        pltpu.VMEM(block, jnp.int32), pltpu.VMEM(block, jnp.int32), f32(*block),
        pltpu.VMEM((6 * VALUES, 4 * PADDED), jnp.bfloat16),
        f32((nx + 4) * SUB, ny), f32(*wide), f32(2, 3, nx, ny), f32(2, 3, nx, ny),
        f32(4, 1, ny), f32(4, 1, ny),
        f32(2, 2, nx, ny), f32(4, nx, ny),
        f32(*block), f32(*block), f32((nx + 1) * SUB, ny), f32(*block), f32(*block), f32(*block),
        f32(*wide), f32(*wide), f32(*wide), f32(4 * SUB, ny), f32(2, nx, ny), f32(2, 4, nx, ny),
        pltpu.VMEM((3, nx, ny), jnp.int32), pltpu.VMEM((ny, LANES), jnp.bfloat16), f32(PADDED * SUB, ny), f32(6, rows, LANES), f32(12, rows, LANES), f32(rows, LANES),
        f32(tiles * pairs, rows, LANES), f32(tiles * rows, LANES), f32(tiles, LANES),
        dma((4,)), dma((2, 2)), dma((2, 2)), dma((2, 3)), dma((2, 3)), dma((4,)), dma((4,)),
        dma((12,)), dma((12,)), dma((tiles * pairs,)), dma((tiles * pairs,)),
    ]
    route = jnp.asarray(np.pad(routing_table(), ((0, 38), (0, 0), (0, 0))), jnp.bfloat16)
    result = pl.pallas_call(
        functools.partial(kernel, tiles, layers, nx, ny),
        out_shape=jax.ShapeDtypeStruct(block, jnp.float32),
        in_specs=[pl.BlockSpec(memory_space=pltpu.HBM)] * 4,
        out_specs=pl.BlockSpec(memory_space=pltpu.VMEM),
        scratch_shapes=scratch,
        compiler_params=pltpu.CompilerParams(
            collective_id=0, has_side_effects=True, vmem_limit_bytes=107 * 2**19
        ),
    )(flat(classes), flat(well_mask), flat(source), route)
    return result.reshape(nx, nz, ny)


def solution(mesh):
    spec = P("tile", "layer", None)
    return jax.shard_map(
        functools.partial(body, mesh.shape["tile"], mesh.shape["layer"]),
        mesh=mesh, in_specs=(spec, spec, spec), out_specs=spec, check_vma=False,
    )
```

```python
import functools

import jax
import jax.numpy as jnp
import numpy as np
from jax import lax
from jax.experimental import pallas as pl
from jax.experimental.pallas import tpu as pltpu
from jax.sharding import PartitionSpec as P

EDGE = 16
HALF = EDGE // 2
CLASSES = 16
SWEEPS = 4
FINE_DAMPING = 0.67
COARSE_DAMPING = 0.5
SINK_RATE = 0.5
VERTICAL_RATIO = 0.25
LANES = 128
SUB = 8
VALUES = 16
RHS = 14
MESH = pl.DeviceIdType.MESH

OWN, OX, OZ, OY = range(4)
FULL_OFFSETS = ((0, 0, 0), (0, 0, 1), (0, 1, 0), (0, 1, 1), None)
EDGE_OFFSETS = ((1, 0, 0), (1, 0, 1), (1, 1, 0))
PRODUCTS = (
    [(w, b, 0) for w in (OWN, OZ, OY) for b in FULL_OFFSETS]
    + [(OX, b, -1) for b in FULL_OFFSETS]
    + [(OX, None, 1)]
    + [(w, b, 1) for w in (OWN, OZ, OY, OX) for b in EDGE_OFFSETS]
    + [(OX, b, -1) for b in EDGE_OFFSETS]
)
SLOT = {product: index for index, product in enumerate(PRODUCTS)}
PADDED = -(-len(PRODUCTS) // SUB) * SUB


def routing_table():
    table = np.zeros((2, 6 * VALUES, 4 * PADDED), np.float32)
    for parity, sign_z in ((0, -1), (1, 1)):
        for n, (weight, toggled, sign_x) in enumerate(PRODUCTS):
            for half, sign_y in ((0, -1), (1, 1)):
                row = ((weight == OX) * sign_x, (weight == OZ) * sign_z, (weight == OY) * sign_y)
                if toggled is None:
                    value = RHS
                else:
                    column = (toggled[0] * sign_x, toggled[1] * sign_z, toggled[2] * sign_y)
                    o = [column[d] - row[d] for d in range(3)]
                    value = 9 * (o[0] + 1) + 3 * (o[1] + 1) + (o[2] + 1) - 13
                    if value < 0:
                        continue
                group = 2 * (weight == OY) + half
                target = (row[0] + 1) * 2 + (weight == OZ)
                table[parity, target * VALUES + value, group * PADDED + n] = 1.0
    return table


def split_dot(table, values, swap=False):
    total = None
    rest = values
    for _ in range(2):
        part = rest.astype(jnp.bfloat16)
        rest = rest - part.astype(jnp.float32)
        pair = (part, table) if swap else (table, part)
        term = jnp.dot(*pair, preferred_element_type=jnp.float32)
        total = term if total is None else total + term
    return total


def tree_sum(terms):
    while len(terms) > 1:
        terms = [sum(terms[n + 1 : n + 2], terms[n]) for n in range(0, len(terms), 2)]
    return terms[0]


def inverse_of(a):
    guarded = jnp.maximum(a, 1e-30)
    guess = pl.reciprocal(guarded, approx=True)
    return guess * (2.0 - guarded * guess)


def harmonic(a, b):
    return 2.0 * a * b * inverse_of(a + b)


def perm_of(classes):
    step = 5.0 / (CLASSES - 1)
    return jnp.exp(classes.astype(jnp.float32) * step - 2.5)


def sink_of(well, perm):
    return SINK_RATE * well.astype(jnp.float32) * perm


def kernel(
    tiles, layers, nx, ny,
    cls_hbm, well_hbm, src_hbm, route_hbm, out_ref,
    cls, well, src, route,
    kx, sk, zs, zr, crs, crr, zq, ze,
    typ_s, tzi_s, txf, tzm_s, tzp_s, d_s, own_s, oy_s, oz_s, ox_s, tz_edge, zb,
    zi, half_table, acc, part, fold, gsend, gath, gsum, csc,
    in_sem, x_send, x_recv, z_send, z_recv, c_send, c_recv, f_send, f_recv, g_send, g_recv,
):
    tile = lax.axis_index("tile")
    layer = lax.axis_index("layer")
    pairs = layers // 2
    pair = layer // 2
    parity = layer % 2
    cells = ny // EDGE
    span = pairs * cells
    rows = part.shape[1]
    plane = lambda i: pl.ds(i * SUB, SUB)

    loads = [
        pltpu.make_async_copy(a, b, in_sem.at[n])
        for n, (a, b) in enumerate(
            ((cls_hbm, cls), (well_hbm, well), (src_hbm, src), (route_hbm.at[parity], route))
        )
    ]
    loads[0].start()
    loads[1].start()

    barrier = pltpu.get_barrier_semaphore()
    for a in range(tiles):
        for b in range(layers):
            if a or b:
                pl.semaphore_signal(
                    barrier, inc=1, device_id_type=MESH,
                    device_id=(lax.rem(tile + a, tiles), lax.rem(layer + b, layers)),
                )

    def fold_from(dt, role):
        from_layer = 2 * pair - 1 + role
        ok = (tile + dt >= 0) & (tile + dt < tiles)
        ok = ok & (from_layer >= 0) & (from_layer < layers)
        return ok & (from_layer != layer) if dt == 0 else ok

    for dt in (-1, 0, 1):
        for role in range(4):
            @pl.when(jnp.logical_not(fold_from(dt, role)))
            def _():
                fold[(dt + 1) * 4 + role] = jnp.zeros(fold.shape[1:], jnp.float32)

    loads[0].wait()
    loads[1].wait()
    loads[2].start()
    loads[3].start()

    ends = ((0, 1), (SUB - 1, SUB - 2))
    for side, (z1, z2) in enumerate(ends):
        for i in range(nx):
            zi[side, pl.ds(i, 1), :] = cls[pl.ds(i * SUB + z1, 1), :]
        k = perm_of(zi[side])
        zs[side, 0] = k
        crs[0 + side] = k[0:1, :]
        crs[2 + side] = k[nx - 1 : nx, :]

    def pack_planes():
        for i in (0, 1, nx - 2, nx - 1):
            k = perm_of(cls[plane(i), :])
            kx[plane(i + 2), :] = k
            if i in (0, nx - 1):
                sk[plane(i + 1), :] = sink_of(well[plane(i), :], k)

    def pack_rows():
        for side, (z1, z2) in enumerate(ends):
            for i in range(nx):
                zi[2 + side, pl.ds(i, 1), :] = cls[pl.ds(i * SUB + z2, 1), :]
                zi[4 + side, pl.ds(i, 1), :] = well[pl.ds(i * SUB + z1, 1), :]
            zs[side, 1] = perm_of(zi[2 + side])
            zs[side, 2] = sink_of(zi[4 + side], zs[side, 0])

    pl.semaphore_wait(barrier, tiles * layers - 1)

    def halo_copies(sx):
        lo = sx < 0
        src_k = kx.at[pl.ds((2 if lo else nx) * SUB, 2 * SUB), :]
        dst_k = kx.at[pl.ds((nx + 2 if lo else 0) * SUB, 2 * SUB), :]
        src_s = sk.at[plane(1 if lo else nx), :]
        dst_s = sk.at[plane(nx + 1 if lo else 0), :]
        s = 0 if lo else 1
        return [
            pltpu.make_async_remote_copy(
                a, b, x_send.at[s, n], x_recv.at[s, n],
                device_id=(tile + sx, layer), device_id_type=MESH,
            )
            for n, (a, b) in enumerate(((src_k, dst_k), (src_s, dst_s)))
        ]

    def layer_copy(sz, n):
        s = 0 if sz < 0 else 1
        return pltpu.make_async_remote_copy(
            zs.at[s, n], zr.at[1 - s, n], z_send.at[s, n], z_recv.at[s, n],
            device_id=(tile, layer + sz), device_id_type=MESH,
        )

    def corner_copy(sx, sz):
        a, b = (0 if sx < 0 else 1), (0 if sz < 0 else 1)
        return pltpu.make_async_remote_copy(
            crs.at[2 * a + b], crr.at[2 * (1 - a) + (1 - b)],
            c_send.at[2 * a + b], c_recv.at[2 * a + b],
            device_id=(tile + sx, layer + sz), device_id_type=MESH,
        )

    def has(sx, sz):
        ok = None
        for s, at, count in ((sx, tile, tiles), (sz, layer, layers)):
            if s:
                test = at > 0 if s < 0 else at < count - 1
                ok = test if ok is None else ok & test
        return ok

    sides = (-1, 1)
    diagonals = [(sx, sz) for sx in sides for sz in sides]
    for sz in sides:
        @pl.when(has(0, sz))
        def _():
            layer_copy(sz, 0).start()

        @pl.when(jnp.logical_not(has(0, sz)))
        def _():
            zr[0 if sz < 0 else 1] = jnp.zeros(zr.shape[1:], jnp.float32)
    pack_planes()
    for sx in sides:
        @pl.when(has(sx, 0))
        def _():
            for copy in halo_copies(sx):
                copy.start()

        @pl.when(jnp.logical_not(has(sx, 0)))
        def _():
            first = 0 if sx < 0 else nx + 2
            kx[pl.ds(first * SUB, 2 * SUB), :] = jnp.zeros((2 * SUB, ny), jnp.float32)
            sk[plane(0 if sx < 0 else nx + 1), :] = jnp.zeros((SUB, ny), jnp.float32)
    for sx, sz in diagonals:
        @pl.when(has(sx, sz))
        def _():
            corner_copy(sx, sz).start()

        @pl.when(jnp.logical_not(has(sx, sz)))
        def _():
            crr[2 * (0 if sx < 0 else 1) + (0 if sz < 0 else 1)] = jnp.zeros((1, ny), jnp.float32)
    pack_rows()
    for sz in sides:
        @pl.when(has(0, sz))
        def _():
            layer_copy(sz, 1).start()
            layer_copy(sz, 2).start()

    sub = lax.broadcasted_iota(jnp.int32, (SUB, ny), 0)
    lane = lax.broadcasted_iota(jnp.int32, (SUB, ny), 1)
    even = parity == 0
    cross_ym = lane % EDGE == 0
    cross_yp = lane % EDGE == EDGE - 1
    cross_zm = (sub == 0) & even
    cross_zp = (sub == SUB - 1) & jnp.logical_not(even)

    def up(a, dim):
        return pltpu.roll(a, 1, dim)

    def down(a, dim):
        return pltpu.roll(a, a.shape[dim] - 1, dim)

    def y_face(k):
        at = lax.broadcasted_iota(jnp.int32, k.shape, 1)
        return jnp.where(at == ny - 1, 0.0, harmonic(k, down(k, 1)))

    def only(mask, a):
        return jnp.where(mask, a, 0.0)

    for i in range(2, nx - 2):
        k = perm_of(cls[plane(i), :])
        kx[plane(i + 2), :] = k
        sk[plane(i + 1), :] = sink_of(well[plane(i), :], k)
    for i in (1, nx - 2):
        sk[plane(i + 1), :] = sink_of(well[plane(i), :], kx[plane(i + 2), :])

    def faces(i):
        at = plane(i)
        k = kx[plane(i + 2), :]
        typ_s[at, :] = y_face(k)
        tzi_s[at, :] = VERTICAL_RATIO * harmonic(k, up(k, 0))

        if i > 0:
            txf[at, :] = harmonic(kx[plane(i + 1), :], k)

    for i in range(nx):
        faces(i)

    fine = lax.broadcasted_iota(jnp.int32, (ny, LANES), 0)
    spot = lax.broadcasted_iota(jnp.int32, (ny, LANES), 1)
    group = spot // cells
    upper = group % 2
    wanted = fine // EDGE + jnp.where(group >= 2, 2 * upper - 1, 0)
    hit = (fine // HALF % 2 == upper) & (wanted == spot % cells) & (group < 4)
    half_table[...] = jnp.where(hit, 1.0, 0.0).astype(jnp.bfloat16)

    def wait_layers(n):
        for sz in sides:
            @pl.when(has(0, sz))
            def _():
                layer_copy(-sz, n).wait_recv()

    wait_layers(0)
    for sx in sides:
        @pl.when(has(sx, 0))
        def _():
            halo_copies(-sx)[0].wait_recv()
    txf[plane(0), :] = harmonic(kx[plane(1), :], kx[plane(2), :])
    txf[plane(nx), :] = harmonic(kx[plane(nx + 1), :], kx[plane(nx + 2), :])
    for side in (0, 1):
        tz_edge[side] = VERTICAL_RATIO * harmonic(zs[side, 0], zr[side, 0])

    def basis(sink, faces, crossing):
        diagonal = sink
        for pair_of in faces:
            diagonal = diagonal + pair_of[0] + pair_of[1]
        inverse = FINE_DAMPING * inverse_of(diagonal)
        leaving = sink
        for term in crossing:
            if term is not None:
                leaving = leaving + term
        outer = [None if term is None else term * inverse for term in crossing]
        return diagonal, 1.0 - leaving * inverse, outer

    def block_basis(i, edge):
        at = plane(i)
        after = plane(i + 1)
        inner = tzi_s[at, :]
        tzm = jnp.where(sub == 0, tz_edge[0, pl.ds(i, 1), :], inner)
        tzp = jnp.where(sub == SUB - 1, tz_edge[1, pl.ds(i, 1), :], down(inner, 0))
        txm = txf[at, :]
        txp = txf[after, :]
        typ = typ_s[at, :]
        tym = up(typ, 1)
        crossing = (
            None if edge == 0 else (txm if edge < 0 else txp),
            only(cross_zm, tzm) + only(cross_zp, tzp),
            only(cross_ym, tym) + only(cross_yp, typ),
        )
        diagonal, own, outer = basis(
            sk[after, :], ((txm, txp), (tzm, tzp), (tym, typ)), crossing
        )
        tzm_s[at, :] = tzm
        tzp_s[at, :] = tzp
        d_s[at, :] = diagonal
        own_s[after, :] = own
        if i >= nx - 2:
            oz_s[after, :] = outer[1]
        oy_s[after, :] = outer[2]
        if edge:
            ox_s[plane(1 if edge < 0 else 2), :] = outer[0]

    for i in range(nx):
        block_basis(i, -1 if i == 0 else int(i == nx - 1))

    for sx in sides:
        @pl.when(has(sx, 0))
        def _():
            halo_copies(-sx)[1].wait_recv()
    for sx, sz in diagonals:
        @pl.when(has(sx, sz))
        def _():
            corner_copy(-sx, -sz).wait_recv()

    for side in (0, 1):
        k1 = kx[plane(1 if side == 0 else nx + 2), :]
        k2 = kx[plane(0 if side == 0 else nx + 3), :]
        toward = txf[plane(0 if side == 0 else nx), :]
        inner = VERTICAL_RATIO * harmonic(k1, up(k1, 0))
        tzm = jnp.where(sub == 0, VERTICAL_RATIO * harmonic(k1, crr[2 * side]), inner)
        tzp = jnp.where(
            sub == SUB - 1, VERTICAL_RATIO * harmonic(k1, crr[2 * side + 1]), down(inner, 0)
        )
        typ = y_face(k1)
        tym = up(typ, 1)
        crossing = (
            toward,
            only(cross_zm, tzm) + only(cross_zp, tzp),
            only(cross_ym, tym) + only(cross_yp, typ),
        )
        _, own, outer = basis(
            sk[plane(0 if side == 0 else nx + 1), :],
            ((toward, harmonic(k1, k2)), (tzm, tzp), (tym, typ)),
            crossing,
        )
        at = plane(0 if side == 0 else nx + 1)
        own_s[at, :] = own
        ox_s[plane(0 if side == 0 else 3), :] = outer[0]
        oz_s[at, :] = outer[1]
        oy_s[at, :] = outer[2]

    wait_layers(1)
    wait_layers(2)
    wide_row = lax.broadcasted_iota(jnp.int32, (nx, ny), 0)
    wide_lane = lax.broadcasted_iota(jnp.int32, (nx, ny), 1)
    for side in (0, 1):
        k1 = zr[side, 0]
        k2 = zr[side, 1]
        toward = tz_edge[side]
        inner = harmonic(k1, up(k1, 0))
        txm = jnp.where(wide_row == 0, harmonic(k1, crr[side]), inner)
        txp = jnp.where(wide_row == nx - 1, harmonic(k1, crr[2 + side]), down(inner, 0))
        typ = y_face(k1)
        tym = up(typ, 1)
        crosses = even if side == 0 else jnp.logical_not(even)
        crossing = (
            only(wide_row == 0, txm) + only(wide_row == nx - 1, txp),
            toward * crosses.astype(jnp.float32),
            only(wide_lane % EDGE == 0, tym) + only(wide_lane % EDGE == EDGE - 1, typ),
        )
        _, own, outer = basis(
            zr[side, 2],
            ((txm, txp), (toward, VERTICAL_RATIO * harmonic(k1, k2)), (tym, typ)),
            crossing,
        )
        zb[side, OWN] = own
        zb[side, OX] = outer[0]
        zb[side, OZ] = outer[1]
        zb[side, OY] = outer[2]
        zq[side, 0] = jnp.where(crosses, outer[1], own)
        zq[side, 1] = jnp.where(crosses, 0.0, outer[2])

    loads[2].wait()
    loads[3].wait()

    sums_of = {}

    def add(product, term):
        sums_of[product] = sums_of[product] + term if product in sums_of else term

    def products(i, edge):
        at, mid, after, row = plane(i), plane(i + 1), plane(i + 2), pl.ds(i, 1)
        diagonal, tzm, tzp, typ = d_s[at, :], tzm_s[at, :], tzp_s[at, :], typ_s[at, :]
        tym = up(typ, 1)
        txm, txp = txf[at, :], txf[mid, :]
        own, oy = own_s[mid, :], oy_s[mid, :]
        source = src[at, :]
        swap_m, swap_p = jnp.where(cross_yp, oy, own), jnp.where(cross_ym, oy, own)
        keep_m, keep_p = jnp.where(cross_yp, own, oy), jnp.where(cross_ym, own, oy)

        def z_pair(a, kind):
            return (
                jnp.where(sub == 0, zq[0, kind, row, :], up(a, 0)),
                jnp.where(sub == SUB - 1, zq[1, kind, row, :], down(a, 0)),
            )

        own_zm, own_zp = z_pair(own, 0)
        oy_zm, oy_zp = z_pair(oy, 1)
        before_own = ox_s[plane(0), :] if edge < 0 else own_s[at, :]
        after_own = ox_s[plane(3), :] if edge > 0 else own_s[after, :]
        q0 = (
            diagonal * own - txm * before_own - txp * after_own
            - tym * up(swap_m, 1) - typ * down(swap_p, 1) - tzm * own_zm - tzp * own_zp
        )
        qy = (
            diagonal * oy - tym * up(keep_m, 1) - typ * down(keep_p, 1)
            - tzm * oy_zm - tzp * oy_zp
        )
        if edge >= 0:
            qy = qy - txm * oy_s[at, :]
        if edge <= 0:
            qy = qy - txp * oy_s[after, :]
        fields = (((0, 0, 0), q0), ((0, 0, 1), qy), (None, source))
        for kind, weight in ((OWN, own), (OY, oy)):
            for offset, field in fields:
                add((kind, offset, 0), weight * field)
        if not edge:
            return
        ox = ox_s[plane(1 if edge < 0 else 2), :]
        if edge < 0:
            for offset, field in fields:
                add((OX, offset, -1), ox * field)
            across, t_across = plane(0), txm
        else:
            add((OX, None, 1), ox * source)
            across, t_across = plane(nx + 1), txp
        tymc, typc = only(cross_ym, tym), only(cross_yp, typ)
        tzmc, tzpc = only(cross_zm, tzm), only(cross_zp, tzp)
        ox_ym, ox_yp = up(ox, 1), down(ox, 1)
        ox_zm = jnp.where(sub == 0, zb[0, OX, row, :], up(ox, 0))
        ox_zp = jnp.where(sub == SUB - 1, zb[1, OX, row, :], down(ox, 0))
        qx = (
            diagonal * ox - t_across * own_s[across, :] - (tym - tymc) * ox_ym
            - (typ - typc) * ox_yp - (tzm - tzmc) * ox_zm - (tzp - tzpc) * ox_zp
        )
        qxy = -(t_across * oy_s[across, :] + tymc * ox_ym + typc * ox_yp)
        qxz = -(t_across * oz_s[across, :] + tzmc * ox_zm + tzpc * ox_zp)
        for offset, field in zip(EDGE_OFFSETS, (qx, qxy, qxz)):
            add((OX, offset, edge), ox * field)
            if edge > 0:
                for kind, weight in ((OWN, own), (OZ, oz_s[mid, :]), (OY, oy)):
                    add((kind, offset, 1), weight * field)
        if edge > 0:
            inward = -txm * ox
            for kind, ref in ((OWN, own_s), (OZ, oz_s), (OY, oy_s)):
                add((kind, EDGE_OFFSETS[0], 1), ref[at, :] * inward)

    for i in range(nx):
        products(i, -1 if i == 0 else int(i == nx - 1))

    z1 = parity * (SUB - 1)
    z2 = 1 + parity * (SUB - 3)
    for i in range(nx):
        ze[1, pl.ds(i, 1), :] = own_s[pl.ds((i + 1) * SUB + z2, 1), :]
        ze[2, pl.ds(i, 1), :] = oy_s[pl.ds((i + 1) * SUB + z2, 1), :]
        ze[3, pl.ds(i, 1), :] = src[pl.ds(i * SUB + z1, 1), :]
    first, last = wide_row == 0, wide_row == nx - 1
    wide_ym, wide_yp = wide_lane % EDGE == 0, wide_lane % EDGE == EDGE - 1
    k1 = zs[parity, 0]
    t_out = tz_edge[parity]
    t_in = VERTICAL_RATIO * harmonic(k1, zs[parity, 1])
    inner = harmonic(k1, up(k1, 0))
    txm = jnp.where(first, harmonic(k1, kx[pl.ds(SUB + z1, 1), :]), inner)
    txp = jnp.where(last, harmonic(k1, kx[pl.ds((nx + 2) * SUB + z1, 1), :]), down(inner, 0))
    typ = y_face(k1)
    tym = up(typ, 1)
    txmc, txpc = only(first, txm), only(last, txp)
    tymc, typc = only(wide_ym, tym), only(wide_yp, typ)
    diagonal, own, (ox, oz, oy) = basis(
        zs[parity, 2], ((txm, txp), (t_in, t_out), (tym, typ)),
        (txmc + txpc, t_out, tymc + typc),
    )
    ze[0] = oz
    txmn, txpn, tymn, typn = txm - txmc, txp - txpc, tym - tymc, typ - typc
    own_in, oy_in, source = ze[1], ze[2], ze[3]
    ox_before, ox_after = ox_s[pl.ds(z1, 1), :], ox_s[pl.ds(3 * SUB + z1, 1), :]
    oz_ym, oz_yp = up(oz, 1), down(oz, 1)
    q0 = (
        diagonal * own - t_out * zb[parity, OZ] - t_in * own_in
        - txm * jnp.where(first, ox_before, up(own, 0))
        - txp * jnp.where(last, ox_after, down(own, 0))
        - tym * up(jnp.where(wide_yp, oy, own), 1) - typ * down(jnp.where(wide_ym, oy, own), 1)
    )
    qy = (
        diagonal * oy - t_in * oy_in - txmn * up(oy, 0) - txpn * down(oy, 0)
        - tym * up(jnp.where(wide_yp, own, oy), 1) - typ * down(jnp.where(wide_ym, own, oy), 1)
    )
    qz = (
        diagonal * oz - t_out * zb[parity, OWN] - txmn * up(oz, 0) - txpn * down(oz, 0)
        - tymn * oz_ym - typn * oz_yp
    )
    qz_in = -t_in * oz
    qzy = -(tymc * oz_ym + typc * oz_yp + t_out * zb[parity, OY])

    def add_rows(product, term):
        add(product, term[:SUB, :] + term[SUB:, :])

    for offset, field in zip(FULL_OFFSETS, (q0, qy, qz, qzy, source)):
        add_rows((OZ, offset, 0), oz * field)
    add_rows((OWN, FULL_OFFSETS[2], 0), own * qz + own_in * qz_in)
    add_rows((OY, FULL_OFFSETS[2], 0), oy * qz + oy_in * qz_in)
    add_rows((OWN, FULL_OFFSETS[3], 0), own * qzy)
    add_rows((OY, FULL_OFFSETS[3], 0), oy * qzy)
    add_rows((OX, FULL_OFFSETS[3], -1), only(first, ox * qzy))
    ox_in = only(first, ox_s[pl.ds(SUB + z2, 1), :])
    add_rows((OX, FULL_OFFSETS[2], -1), only(first, ox * qz) + ox_in * qz_in)
    def merge(a, b, distance):
        lower = sub // distance % 2 == 0
        if 2 * distance == SUB:
            return jnp.where(lower, a, b) + pltpu.roll(jnp.where(lower, b, a), distance, 0)
        return jnp.where(
            lower, a + pltpu.roll(a, SUB - distance, 0), b + pltpu.roll(b, distance, 0)
        )

    nothing = jnp.zeros((SUB, ny), jnp.float32)
    for first_row in range(0, PADDED, SUB):
        group_of = [
            sums_of[PRODUCTS[n]] if n < len(PRODUCTS) else nothing
            for n in range(first_row, first_row + SUB)
        ]
        while len(group_of) > 1:
            distance = len(group_of) // 2
            group_of = [
                merge(group_of[j], group_of[j + distance], distance) for j in range(distance)
            ]
        acc[pl.ds(first_row, SUB), :] = group_of[0]

    sums = split_dot(half_table[...], acc[...], swap=True)
    stacked = jnp.concatenate(
        [sums] + [pltpu.roll(sums, LANES - g * cells, 1) for g in (1, 2, 3)], axis=0
    )
    routed = split_dot(route[...], stacked)
    routed = jnp.where(
        lax.broadcasted_iota(jnp.int32, routed.shape, 1) < cells, routed, 0.0
    )
    beside_pair = pair + 2 * parity - 1
    near_pair = jnp.clip(beside_pair, 0, pairs - 1)
    for target in range(6):
        block = routed[target * VALUES : (target + 1) * VALUES, :]
        if rows < VALUES:
            block = block[:rows, :] + pltpu.roll(block[rows:, :], span, 1)
        to_pair = near_pair if target % 2 else pair
        part[target] = pltpu.roll(block, to_pair * cells, 1)

    def fold_copy(sx, beside, which):
        to_pair = beside_pair if beside else pair
        role = layer - 2 * to_pair + 1
        slot = (1 - sx) * 4 + role
        n = ((sx + 1) * 2 + beside) * 2 + which
        return pltpu.make_async_remote_copy(
            part.at[(sx + 1) * 2 + beside], fold.at[slot], f_send.at[n], f_recv.at[slot],
            device_id=(tile + sx, 2 * to_pair + which), device_id_type=MESH,
        )

    def fold_valid(sx, beside, which):
        ok = (tile + sx >= 0) & (tile + sx < tiles)
        if beside:
            return ok & (beside_pair >= 0) & (beside_pair < pairs)
        return ok if sx else ok & (which != parity)

    fold_list = [(sx, b, w) for b in (1, 0) for sx in (-1, 1, 0) for w in (0, 1)]
    for item in fold_list:
        @pl.when(fold_valid(*item))
        def _():
            fold_copy(*item).start()

    for dt in (-1, 0, 1):
        for role in range(4):
            slot = (dt + 1) * 4 + role

            @pl.when(fold_from(dt, role))
            def _():
                pltpu.make_async_remote_copy(
                    part.at[0], fold.at[slot], f_send.at[0], f_recv.at[slot],
                    device_id=(tile, layer), device_id_type=MESH,
                ).wait_recv()

    terms = [part[2]] + [fold[slot] for slot in range(12)]
    gsend[...] = tree_sum(terms)

    def gather_copy(k):
        other = lax.rem(tile * pairs + pair + k, tiles * pairs)
        return pltpu.make_async_remote_copy(
            gsend, gath.at[tile * pairs + pair], g_send.at[k], g_recv.at[tile * pairs + pair],
            device_id=(other // pairs, 2 * (other % pairs) + parity), device_id_type=MESH,
        )

    far_first = sorted(
        range(1, tiles * pairs), key=lambda k: (k % pairs == 0, abs(k - tiles * pairs // 2))
    )
    for k in far_first:
        gather_copy(k).start()
    gath[tile * pairs + pair] = gsend[...]

    cell_at = lax.broadcasted_iota(jnp.int32, (LANES, ny), 0)
    fine_at = lax.broadcasted_iota(jnp.int32, (LANES, ny), 1)
    parent = fine_at // EDGE
    spread = jnp.where(cell_at == parent, 1.0, 0.0).astype(jnp.bfloat16)
    beside_y = parent + 2 * (fine_at // HALF % 2) - 1
    spread_y = jnp.where(cell_at == beside_y, 1.0, 0.0).astype(jnp.bfloat16)

    for sz in sides:
        @pl.when(has(0, sz))
        def _():
            for n in range(3):
                layer_copy(sz, n).wait_send()
    for sx in sides:
        @pl.when(has(sx, 0))
        def _():
            for copy in halo_copies(sx):
                copy.wait_send()
    for sx, sz in diagonals:
        @pl.when(has(sx, sz))
        def _():
            corner_copy(sx, sz).wait_send()
    for item in fold_list:
        @pl.when(fold_valid(*item))
        def _():
            fold_copy(*item).wait_send()
    for k in range(1, tiles * pairs):
        gather_copy(k).wait_send()

    for k in range(1, tiles * pairs):
        frm = lax.rem(tile * pairs + pair + tiles * pairs - k, tiles * pairs)
        pltpu.make_async_remote_copy(
            gsend, gath.at[frm], g_send.at[k], g_recv.at[frm],
            device_id=(tile, layer), device_id_type=MESH,
        ).wait_recv()

    for t in range(tiles):
        total = gath[t * pairs]
        for p in range(1, pairs):
            total = total + gath[t * pairs + p]
        gsum[pl.ds(t * rows, rows), :] = total
    lane_t = lax.broadcasted_iota(jnp.int32, (tiles, LANES), 1)

    def value(v):
        a = gsum[pl.ds(v % rows, tiles, stride=rows), :]
        if v >= rows:
            a = pltpu.roll(a, LANES - span, 1)
        return only(lane_t < span, a)

    def shifted(a, offset):
        ox, oz, oy = offset
        along = -(oz * cells + oy) % LANES
        if along:
            a = pltpu.roll(a, along, 1)
        if ox:
            a = pltpu.roll(a, -ox % tiles, 0)
        return a

    offsets = [((v + 13) // 9 - 1, (v + 13) // 3 % 3 - 1, (v + 13) % 3 - 1) for v in range(14)]
    forward = [value(v) for v in range(14)]
    backward = [
        shifted(forward[v], [-d for d in offsets[v]]) if v else None for v in range(14)
    ]
    rhs = value(RHS)
    scale = COARSE_DAMPING / jnp.where(lane_t < span, forward[0], 1.0)
    coarse = rhs * scale
    for _ in range(SWEEPS - 1):
        terms = [forward[0] * coarse]
        for v in range(1, 14):
            terms.append(forward[v] * shifted(coarse, offsets[v]))
            terms.append(backward[v] * shifted(coarse, [-d for d in offsets[v]]))
        coarse = coarse + (rhs - tree_sum(terms)) * scale
    csc[...] = coarse

    def coarse_row(t, p):
        a = jnp.broadcast_to(csc[pl.ds(t, 1), :], (SUB, LANES))
        return pltpu.roll(a, (LANES - p * cells) % LANES, 1)

    center = coarse_row(tile, pair)
    four = jnp.concatenate(
        [
            center,
            coarse_row(tile, near_pair),
            coarse_row(jnp.maximum(tile - 1, 0), pair),
            coarse_row(jnp.minimum(tile + 1, tiles - 1), pair),
        ],
        axis=0,
    )
    wide = split_dot(spread, four, swap=True)
    c_own, c_z = wide[:SUB, :], wide[SUB : 2 * SUB, :]
    c_y = split_dot(spread_y, center, swap=True)
    ze[0] = ze[0] * jnp.concatenate([c_z] * (nx // SUB), axis=0)
    at_edge = sub == parity * (SUB - 1)
    for i in range(nx):
        at = plane(i + 1)
        result = own_s[at, :] * c_own + oy_s[at, :] * c_y
        result = result + only(at_edge, ze[0, pl.ds(i, 1), :])
        if i == 0:
            result = result + ox_s[plane(1), :] * wide[2 * SUB : 3 * SUB, :]
        if i == nx - 1:
            result = result + ox_s[plane(2), :] * wide[3 * SUB :, :]
        out_ref[plane(i), :] = result


def body(tiles, layers, classes, well_mask, source):
    nx, nz, ny = classes.shape
    assert nx == EDGE and nz == HALF == SUB and layers % 2 == 0
    cells, pairs = ny // EDGE, layers // 2
    assert 4 * cells <= LANES and pairs * cells <= LANES
    rows = VALUES // 2 if 2 * pairs * cells <= LANES else VALUES
    flat = lambda a: a.reshape(nx * nz, ny)
    f32 = lambda *shape: pltpu.VMEM(shape, jnp.float32)
    dma = pltpu.SemaphoreType.DMA
    block = (nx * SUB, ny)
    wide = ((nx + 2) * SUB, ny)
    scratch = [
        pltpu.VMEM(block, jnp.int32), pltpu.VMEM(block, jnp.int32), f32(*block),
        pltpu.VMEM((6 * VALUES, 4 * PADDED), jnp.bfloat16),
        f32((nx + 4) * SUB, ny), f32(*wide), f32(2, 3, nx, ny), f32(2, 3, nx, ny),
        f32(4, 1, ny), f32(4, 1, ny),
        f32(2, 2, nx, ny), f32(4, nx, ny),
        f32(*block), f32(*block), f32((nx + 1) * SUB, ny), f32(*block), f32(*block), f32(*block),
        f32(*wide), f32(*wide), f32(*wide), f32(4 * SUB, ny), f32(2, nx, ny), f32(2, 4, nx, ny),
        pltpu.VMEM((6, nx, ny), jnp.int32), pltpu.VMEM((ny, LANES), jnp.bfloat16), f32(PADDED, ny), f32(6, rows, LANES), f32(12, rows, LANES), f32(rows, LANES),
        f32(tiles * pairs, rows, LANES), f32(tiles * rows, LANES), f32(tiles, LANES),
        dma((4,)), dma((2, 2)), dma((2, 2)), dma((2, 3)), dma((2, 3)), dma((4,)), dma((4,)),
        dma((12,)), dma((12,)), dma((tiles * pairs,)), dma((tiles * pairs,)),
    ]
    route = jnp.asarray(np.pad(routing_table(), ((0, 38), (0, 0), (0, 0))), jnp.bfloat16)
    result = pl.pallas_call(
        functools.partial(kernel, tiles, layers, nx, ny),
        out_shape=jax.ShapeDtypeStruct(block, jnp.float32),
        in_specs=[pl.BlockSpec(memory_space=pltpu.HBM)] * 4,
        out_specs=pl.BlockSpec(memory_space=pltpu.VMEM),
        scratch_shapes=scratch,
        compiler_params=pltpu.CompilerParams(
            collective_id=0, has_side_effects=True, vmem_limit_bytes=107 * 2**19
        ),
    )(flat(classes), flat(well_mask), flat(source), route)
    return result.reshape(nx, nz, ny)


def solution(mesh):
    spec = P("tile", "layer", None)
    return jax.shard_map(
        functools.partial(body, mesh.shape["tile"], mesh.shape["layer"]),
        mesh=mesh, in_specs=(spec, spec, spec), out_specs=spec, check_vma=False,
    )
```

```python
import functools

import jax
import jax.numpy as jnp
import numpy as np
from jax import lax
from jax.experimental import pallas as pl
from jax.experimental.pallas import tpu as pltpu
from jax.sharding import PartitionSpec as P

EDGE = 16
HALF = EDGE // 2
CLASSES = 16
SWEEPS = 4
FINE_DAMPING = 0.67
COARSE_DAMPING = 0.5
SINK_RATE = 0.5
VERTICAL_RATIO = 0.25
LANES = 128
SUB = 8
VALUES = 16
RHS = 14
MESH = pl.DeviceIdType.MESH

OWN, OX, OZ, OY = range(4)
FULL_OFFSETS = ((0, 0, 0), (0, 0, 1), (0, 1, 0), (0, 1, 1), None)
EDGE_OFFSETS = ((1, 0, 0), (1, 0, 1), (1, 1, 0))
PRODUCTS = (
    [(w, b, 0) for w in (OWN, OZ, OY) for b in FULL_OFFSETS]
    + [(OX, b, -1) for b in FULL_OFFSETS]
    + [(OX, None, 1)]
    + [(w, b, 1) for w in (OWN, OZ, OY, OX) for b in EDGE_OFFSETS]
    + [(OX, b, -1) for b in EDGE_OFFSETS]
)
SLOT = {product: index for index, product in enumerate(PRODUCTS)}
PADDED = -(-len(PRODUCTS) // SUB) * SUB


def routing_table():
    table = np.zeros((2, 6 * VALUES, 4 * PADDED), np.float32)
    for parity, sign_z in ((0, -1), (1, 1)):
        for n, (weight, toggled, sign_x) in enumerate(PRODUCTS):
            for half, sign_y in ((0, -1), (1, 1)):
                row = ((weight == OX) * sign_x, (weight == OZ) * sign_z, (weight == OY) * sign_y)
                if toggled is None:
                    value = RHS
                else:
                    column = (toggled[0] * sign_x, toggled[1] * sign_z, toggled[2] * sign_y)
                    o = [column[d] - row[d] for d in range(3)]
                    value = 9 * (o[0] + 1) + 3 * (o[1] + 1) + (o[2] + 1) - 13
                    if value < 0:
                        continue
                group = 2 * (weight == OY) + half
                target = (row[0] + 1) * 2 + (weight == OZ)
                table[parity, target * VALUES + value, group * PADDED + n] = 1.0
    return table


def split_dot(table, values, swap=False):
    total = None
    rest = values
    for _ in range(2):
        part = rest.astype(jnp.bfloat16)
        rest = rest - part.astype(jnp.float32)
        pair = (part, table) if swap else (table, part)
        term = jnp.dot(*pair, preferred_element_type=jnp.float32)
        total = term if total is None else total + term
    return total


def tree_sum(terms):
    while len(terms) > 1:
        terms = [sum(terms[n + 1 : n + 2], terms[n]) for n in range(0, len(terms), 2)]
    return terms[0]


def inverse_of(a):
    guarded = jnp.maximum(a, 1e-30)
    guess = pl.reciprocal(guarded, approx=True)
    return guess * (2.0 - guarded * guess)


def harmonic(a, b):
    return 2.0 * a * b * inverse_of(a + b)


def perm_of(classes):
    step = 5.0 / (CLASSES - 1)
    return jnp.exp(classes.astype(jnp.float32) * step - 2.5)


def sink_of(well, perm):
    return SINK_RATE * well.astype(jnp.float32) * perm


def kernel(
    tiles, layers, nx, ny,
    cls_hbm, well_hbm, src_hbm, route_hbm, out_ref,
    cls, well, src, route,
    kx, sk, zs, zr, crs, crr, zq, zw, ze,
    typ_s, tzi_s, txf, tzm_s, tzp_s, d_s, own_s, oy_s, oz_s, ox_s, tz_edge, zb,
    zi, half_table, acc, part, fold, gsend, gath, gsum, csc,
    in_sem, x_send, x_recv, z_send, z_recv, c_send, c_recv, f_send, f_recv, g_send, g_recv,
):
    tile = lax.axis_index("tile")
    layer = lax.axis_index("layer")
    pairs = layers // 2
    pair = layer // 2
    parity = layer % 2
    cells = ny // EDGE
    span = pairs * cells
    rows = part.shape[1]
    plane = lambda i: pl.ds(i * SUB, SUB)

    loads = [
        pltpu.make_async_copy(a, b, in_sem.at[n])
        for n, (a, b) in enumerate(
            ((cls_hbm, cls), (well_hbm, well), (src_hbm, src), (route_hbm.at[parity], route))
        )
    ]
    loads[0].start()
    loads[1].start()

    barrier = pltpu.get_barrier_semaphore()
    for a in range(tiles):
        for b in range(layers):
            if a or b:
                pl.semaphore_signal(
                    barrier, inc=1, device_id_type=MESH,
                    device_id=(lax.rem(tile + a, tiles), lax.rem(layer + b, layers)),
                )

    def fold_from(dt, role):
        from_layer = 2 * pair - 1 + role
        ok = (tile + dt >= 0) & (tile + dt < tiles)
        ok = ok & (from_layer >= 0) & (from_layer < layers)
        return ok & (from_layer != layer) if dt == 0 else ok

    for dt in (-1, 0, 1):
        for role in range(4):
            @pl.when(jnp.logical_not(fold_from(dt, role)))
            def _():
                fold[(dt + 1) * 4 + role] = jnp.zeros(fold.shape[1:], jnp.float32)

    loads[0].wait()
    loads[1].wait()
    loads[2].start()
    loads[3].start()

    ends = ((0, 1), (SUB - 1, SUB - 2))
    for side, (z1, z2) in enumerate(ends):
        for i in range(nx):
            zi[side, pl.ds(i, 1), :] = cls[pl.ds(i * SUB + z1, 1), :]
        k = perm_of(zi[side])
        zs[side, 0] = k
        crs[0 + side] = k[0:1, :]
        crs[2 + side] = k[nx - 1 : nx, :]

    def pack_planes():
        for i in (0, 1, nx - 2, nx - 1):
            k = perm_of(cls[plane(i), :])
            kx[plane(i + 2), :] = k
            if i in (0, nx - 1):
                sk[plane(i + 1), :] = sink_of(well[plane(i), :], k)

    def pack_rows():
        for side, (z1, z2) in enumerate(ends):
            for i in range(nx):
                zi[2 + side, pl.ds(i, 1), :] = cls[pl.ds(i * SUB + z2, 1), :]
                zi[4 + side, pl.ds(i, 1), :] = well[pl.ds(i * SUB + z1, 1), :]
            zs[side, 1] = perm_of(zi[2 + side])
            zs[side, 2] = sink_of(zi[4 + side], zs[side, 0])

    pl.semaphore_wait(barrier, tiles * layers - 1)

    def halo_copies(sx):
        lo = sx < 0
        src_k = kx.at[pl.ds((2 if lo else nx) * SUB, 2 * SUB), :]
        dst_k = kx.at[pl.ds((nx + 2 if lo else 0) * SUB, 2 * SUB), :]
        src_s = sk.at[plane(1 if lo else nx), :]
        dst_s = sk.at[plane(nx + 1 if lo else 0), :]
        s = 0 if lo else 1
        return [
            pltpu.make_async_remote_copy(
                a, b, x_send.at[s, n], x_recv.at[s, n],
                device_id=(tile + sx, layer), device_id_type=MESH,
            )
            for n, (a, b) in enumerate(((src_k, dst_k), (src_s, dst_s)))
        ]

    def layer_copy(sz, n):
        s = 0 if sz < 0 else 1
        return pltpu.make_async_remote_copy(
            zs.at[s, n], zr.at[1 - s, n], z_send.at[s, n], z_recv.at[s, n],
            device_id=(tile, layer + sz), device_id_type=MESH,
        )

    def corner_copy(sx, sz):
        a, b = (0 if sx < 0 else 1), (0 if sz < 0 else 1)
        return pltpu.make_async_remote_copy(
            crs.at[2 * a + b], crr.at[2 * (1 - a) + (1 - b)],
            c_send.at[2 * a + b], c_recv.at[2 * a + b],
            device_id=(tile + sx, layer + sz), device_id_type=MESH,
        )

    def has(sx, sz):
        ok = None
        for s, at, count in ((sx, tile, tiles), (sz, layer, layers)):
            if s:
                test = at > 0 if s < 0 else at < count - 1
                ok = test if ok is None else ok & test
        return ok

    sides = (-1, 1)
    diagonals = [(sx, sz) for sx in sides for sz in sides]
    for sz in sides:
        @pl.when(has(0, sz))
        def _():
            layer_copy(sz, 0).start()

        @pl.when(jnp.logical_not(has(0, sz)))
        def _():
            zr[0 if sz < 0 else 1] = jnp.zeros(zr.shape[1:], jnp.float32)
    pack_planes()
    for sx in sides:
        @pl.when(has(sx, 0))
        def _():
            for copy in halo_copies(sx):
                copy.start()

        @pl.when(jnp.logical_not(has(sx, 0)))
        def _():
            first = 0 if sx < 0 else nx + 2
            kx[pl.ds(first * SUB, 2 * SUB), :] = jnp.zeros((2 * SUB, ny), jnp.float32)
            sk[plane(0 if sx < 0 else nx + 1), :] = jnp.zeros((SUB, ny), jnp.float32)
    for sx, sz in diagonals:
        @pl.when(has(sx, sz))
        def _():
            corner_copy(sx, sz).start()

        @pl.when(jnp.logical_not(has(sx, sz)))
        def _():
            crr[2 * (0 if sx < 0 else 1) + (0 if sz < 0 else 1)] = jnp.zeros((1, ny), jnp.float32)
    pack_rows()
    for sz in sides:
        @pl.when(has(0, sz))
        def _():
            layer_copy(sz, 1).start()
            layer_copy(sz, 2).start()

    sub = lax.broadcasted_iota(jnp.int32, (SUB, ny), 0)
    lane = lax.broadcasted_iota(jnp.int32, (SUB, ny), 1)
    even = parity == 0
    cross_ym = lane % EDGE == 0
    cross_yp = lane % EDGE == EDGE - 1
    cross_zm = (sub == 0) & even
    cross_zp = (sub == SUB - 1) & jnp.logical_not(even)

    def up(a, dim):
        return pltpu.roll(a, 1, dim)

    def down(a, dim):
        return pltpu.roll(a, a.shape[dim] - 1, dim)

    def y_face(k):
        at = lax.broadcasted_iota(jnp.int32, k.shape, 1)
        return jnp.where(at == ny - 1, 0.0, harmonic(k, down(k, 1)))

    def only(mask, a):
        return jnp.where(mask, a, 0.0)

    for i in range(2, nx - 2):
        k = perm_of(cls[plane(i), :])
        kx[plane(i + 2), :] = k
        sk[plane(i + 1), :] = sink_of(well[plane(i), :], k)
    for i in (1, nx - 2):
        sk[plane(i + 1), :] = sink_of(well[plane(i), :], kx[plane(i + 2), :])

    def faces(i):
        at = plane(i)
        k = kx[plane(i + 2), :]
        typ_s[at, :] = y_face(k)
        tzi_s[at, :] = VERTICAL_RATIO * harmonic(k, up(k, 0))

        if i > 0:
            txf[at, :] = harmonic(kx[plane(i + 1), :], k)

    for i in range(nx):
        faces(i)

    fine = lax.broadcasted_iota(jnp.int32, (ny, LANES), 0)
    spot = lax.broadcasted_iota(jnp.int32, (ny, LANES), 1)
    group = spot // cells
    upper = group % 2
    wanted = fine // EDGE + jnp.where(group >= 2, 2 * upper - 1, 0)
    hit = (fine // HALF % 2 == upper) & (wanted == spot % cells) & (group < 4)
    half_table[...] = jnp.where(hit, 1.0, 0.0).astype(jnp.bfloat16)

    def wait_layers(n):
        for sz in sides:
            @pl.when(has(0, sz))
            def _():
                layer_copy(-sz, n).wait_recv()

    wait_layers(0)
    for sx in sides:
        @pl.when(has(sx, 0))
        def _():
            halo_copies(-sx)[0].wait_recv()
    txf[plane(0), :] = harmonic(kx[plane(1), :], kx[plane(2), :])
    txf[plane(nx), :] = harmonic(kx[plane(nx + 1), :], kx[plane(nx + 2), :])
    for side in (0, 1):
        tz_edge[side] = VERTICAL_RATIO * harmonic(zs[side, 0], zr[side, 0])

    def basis(sink, faces, crossing):
        diagonal = sink
        for pair_of in faces:
            diagonal = diagonal + pair_of[0] + pair_of[1]
        inverse = FINE_DAMPING * inverse_of(diagonal)
        leaving = sink
        for term in crossing:
            if term is not None:
                leaving = leaving + term
        outer = [None if term is None else term * inverse for term in crossing]
        return diagonal, 1.0 - leaving * inverse, outer

    def block_basis(i, edge):
        at = plane(i)
        after = plane(i + 1)
        inner = tzi_s[at, :]
        tzm = jnp.where(sub == 0, tz_edge[0, pl.ds(i, 1), :], inner)
        tzp = jnp.where(sub == SUB - 1, tz_edge[1, pl.ds(i, 1), :], down(inner, 0))
        txm = txf[at, :]
        txp = txf[after, :]
        typ = typ_s[at, :]
        tym = up(typ, 1)
        crossing = (
            None if edge == 0 else (txm if edge < 0 else txp),
            only(cross_zm, tzm) + only(cross_zp, tzp),
            only(cross_ym, tym) + only(cross_yp, typ),
        )
        diagonal, own, outer = basis(
            sk[after, :], ((txm, txp), (tzm, tzp), (tym, typ)), crossing
        )
        tzm_s[at, :] = tzm
        tzp_s[at, :] = tzp
        d_s[at, :] = diagonal
        own_s[after, :] = own
        if i >= nx - 2:
            oz_s[after, :] = outer[1]
        oy_s[after, :] = outer[2]
        if edge:
            ox_s[plane(1 if edge < 0 else 2), :] = outer[0]

    for i in range(nx):
        block_basis(i, -1 if i == 0 else int(i == nx - 1))

    for sx in sides:
        @pl.when(has(sx, 0))
        def _():
            halo_copies(-sx)[1].wait_recv()
    for sx, sz in diagonals:
        @pl.when(has(sx, sz))
        def _():
            corner_copy(-sx, -sz).wait_recv()

    for side in (0, 1):
        k1 = kx[plane(1 if side == 0 else nx + 2), :]
        k2 = kx[plane(0 if side == 0 else nx + 3), :]
        toward = txf[plane(0 if side == 0 else nx), :]
        inner = VERTICAL_RATIO * harmonic(k1, up(k1, 0))
        tzm = jnp.where(sub == 0, VERTICAL_RATIO * harmonic(k1, crr[2 * side]), inner)
        tzp = jnp.where(
            sub == SUB - 1, VERTICAL_RATIO * harmonic(k1, crr[2 * side + 1]), down(inner, 0)
        )
        typ = y_face(k1)
        tym = up(typ, 1)
        crossing = (
            toward,
            only(cross_zm, tzm) + only(cross_zp, tzp),
            only(cross_ym, tym) + only(cross_yp, typ),
        )
        _, own, outer = basis(
            sk[plane(0 if side == 0 else nx + 1), :],
            ((toward, harmonic(k1, k2)), (tzm, tzp), (tym, typ)),
            crossing,
        )
        at = plane(0 if side == 0 else nx + 1)
        own_s[at, :] = own
        ox_s[plane(0 if side == 0 else 3), :] = outer[0]
        oz_s[at, :] = outer[1]
        oy_s[at, :] = outer[2]

    loads[2].wait()
    loads[3].wait()

    sums_of = {}

    def add(product, term):
        sums_of[product] = sums_of[product] + term if product in sums_of else term

    def products(i, edge):
        at, mid, after = plane(i), plane(i + 1), plane(i + 2)
        diagonal, tzm, tzp, typ = d_s[at, :], tzm_s[at, :], tzp_s[at, :], typ_s[at, :]
        tym = up(typ, 1)
        txm, txp = txf[at, :], txf[mid, :]
        own, oy = own_s[mid, :], oy_s[mid, :]
        source = src[at, :]
        swap_m, swap_p = jnp.where(cross_yp, oy, own), jnp.where(cross_ym, oy, own)
        keep_m, keep_p = jnp.where(cross_yp, own, oy), jnp.where(cross_ym, own, oy)

        def z_pair(a):
            return (
                only(sub != 0, up(a, 0)),
                only(sub != SUB - 1, down(a, 0)),
            )

        own_zm, own_zp = z_pair(own)
        oy_zm, oy_zp = z_pair(oy)
        before_own = ox_s[plane(0), :] if edge < 0 else own_s[at, :]
        after_own = ox_s[plane(3), :] if edge > 0 else own_s[after, :]
        q0 = (
            diagonal * own - txm * before_own - txp * after_own
            - tym * up(swap_m, 1) - typ * down(swap_p, 1) - tzm * own_zm - tzp * own_zp
        )
        qy = (
            diagonal * oy - tym * up(keep_m, 1) - typ * down(keep_p, 1)
            - tzm * oy_zm - tzp * oy_zp
        )
        if edge >= 0:
            qy = qy - txm * oy_s[at, :]
        if edge <= 0:
            qy = qy - txp * oy_s[after, :]
        fields = (((0, 0, 0), q0), ((0, 0, 1), qy), (None, source))
        for kind, weight in ((OWN, own), (OY, oy)):
            for offset, field in fields:
                add((kind, offset, 0), weight * field)
        if edge < 0:
            ox = ox_s[plane(1), :]
            for offset, field in fields:
                add((OX, offset, -1), ox * field)
        if edge > 0:
            add((OX, None, 1), ox_s[plane(2), :] * source)

    def edge_products(i, edge):
        at, mid, row = plane(i), plane(i + 1), pl.ds(i, 1)
        diagonal, tzm, tzp, typ = d_s[at, :], tzm_s[at, :], tzp_s[at, :], typ_s[at, :]
        tym = up(typ, 1)
        txm, txp = txf[at, :], txf[mid, :]
        own, oy = own_s[mid, :], oy_s[mid, :]
        ox = ox_s[plane(1 if edge < 0 else 2), :]
        across, t_across = (plane(0), txm) if edge < 0 else (plane(nx + 1), txp)
        tymc, typc = only(cross_ym, tym), only(cross_yp, typ)
        tzmc, tzpc = only(cross_zm, tzm), only(cross_zp, tzp)
        ox_ym, ox_yp = up(ox, 1), down(ox, 1)
        ox_zm = jnp.where(sub == 0, zb[0, OX, row, :], up(ox, 0))
        ox_zp = jnp.where(sub == SUB - 1, zb[1, OX, row, :], down(ox, 0))
        qx = (
            diagonal * ox - t_across * own_s[across, :] - (tym - tymc) * ox_ym
            - (typ - typc) * ox_yp - (tzm - tzmc) * ox_zm - (tzp - tzpc) * ox_zp
        )
        qxy = -(t_across * oy_s[across, :] + tymc * ox_ym + typc * ox_yp)
        qxz = -(t_across * oz_s[across, :] + tzmc * ox_zm + tzpc * ox_zp)
        for offset, field in zip(EDGE_OFFSETS, (qx, qxy, qxz)):
            add((OX, offset, edge), ox * field)
            if edge > 0:
                for kind, weight in ((OWN, own), (OZ, oz_s[mid, :]), (OY, oy)):
                    add((kind, offset, 1), weight * field)
        if edge > 0:
            inward = -txm * ox
            for kind, ref in ((OWN, own_s), (OZ, oz_s), (OY, oy_s)):
                add((kind, EDGE_OFFSETS[0], 1), ref[at, :] * inward)

    for i in range(nx):
        products(i, -1 if i == 0 else int(i == nx - 1))

    wide_row = lax.broadcasted_iota(jnp.int32, (nx, ny), 0)
    wide_lane = lax.broadcasted_iota(jnp.int32, (nx, ny), 1)
    z1 = parity * (SUB - 1)
    z2 = 1 + parity * (SUB - 3)
    for i in range(nx):
        ze[1, pl.ds(i, 1), :] = own_s[pl.ds((i + 1) * SUB + z2, 1), :]
        ze[2, pl.ds(i, 1), :] = oy_s[pl.ds((i + 1) * SUB + z2, 1), :]
        ze[3, pl.ds(i, 1), :] = src[pl.ds(i * SUB + z1, 1), :]
        for side in (0, 1):
            at = pl.ds((i + 1) * SUB + side * (SUB - 1), 1)
            zw[side, 0, pl.ds(i, 1), :] = own_s[at, :]
            zw[side, 1, pl.ds(i, 1), :] = oy_s[at, :]
    first, last = wide_row == 0, wide_row == nx - 1
    wide_ym, wide_yp = wide_lane % EDGE == 0, wide_lane % EDGE == EDGE - 1
    k1 = zs[parity, 0]
    t_out = tz_edge[parity]
    t_in = VERTICAL_RATIO * harmonic(k1, zs[parity, 1])
    inner = harmonic(k1, up(k1, 0))
    txm = jnp.where(first, harmonic(k1, kx[pl.ds(SUB + z1, 1), :]), inner)
    txp = jnp.where(last, harmonic(k1, kx[pl.ds((nx + 2) * SUB + z1, 1), :]), down(inner, 0))
    typ = y_face(k1)
    tym = up(typ, 1)
    txmc, txpc = only(first, txm), only(last, txp)
    tymc, typc = only(wide_ym, tym), only(wide_yp, typ)
    diagonal, own, (ox, oz, oy) = basis(
        zs[parity, 2], ((txm, txp), (t_in, t_out), (tym, typ)),
        (txmc + txpc, t_out, tymc + typc),
    )
    ze[0] = oz
    txmn, txpn, tymn, typn = txm - txmc, txp - txpc, tym - tymc, typ - typc
    def rows_beside():
        wait_layers(1)
        wait_layers(2)
        for side in (0, 1):
            k1 = zr[side, 0]
            k2 = zr[side, 1]
            toward = tz_edge[side]
            inner = harmonic(k1, up(k1, 0))
            txm = jnp.where(wide_row == 0, harmonic(k1, crr[side]), inner)
            txp = jnp.where(wide_row == nx - 1, harmonic(k1, crr[2 + side]), down(inner, 0))
            typ = y_face(k1)
            tym = up(typ, 1)
            crosses = even if side == 0 else jnp.logical_not(even)
            crossing = (
                only(wide_row == 0, txm) + only(wide_row == nx - 1, txp),
                toward * crosses.astype(jnp.float32),
                only(wide_lane % EDGE == 0, tym) + only(wide_lane % EDGE == EDGE - 1, typ),
            )
            _, own, outer = basis(
                zr[side, 2],
                ((txm, txp), (toward, VERTICAL_RATIO * harmonic(k1, k2)), (tym, typ)),
                crossing,
            )
            zb[side, OWN] = own
            zb[side, OX] = outer[0]
            zb[side, OZ] = outer[1]
            zb[side, OY] = outer[2]
            zq[side, 0] = jnp.where(crosses, outer[1], own)
            zq[side, 1] = jnp.where(crosses, 0.0, outer[2])

    rows_beside()
    def add_rows(product, term):
        add(product, term[:SUB, :] + term[SUB:, :])

    for i, edge in ((0, -1), (nx - 1, 1)):
        edge_products(i, edge)
    for side in (0, 1):
        weights = (
            (OWN, 0, zw[side, 0]), (OY, 0, zw[side, 1]),
            (OX, -1, only(first, ox_s[pl.ds(SUB + side * (SUB - 1), 1), :])),
        )
        for n, offset in enumerate(FULL_OFFSETS[:2]):
            field = -tz_edge[side] * zq[side, n]
            for kind, at_side, weight in weights:
                add_rows((kind, offset, at_side), weight * field)

    own_in, oy_in, source = ze[1], ze[2], ze[3]
    ox_before, ox_after = ox_s[pl.ds(z1, 1), :], ox_s[pl.ds(3 * SUB + z1, 1), :]
    oz_ym, oz_yp = up(oz, 1), down(oz, 1)
    q0 = (
        diagonal * own - t_out * zb[parity, OZ] - t_in * own_in
        - txm * jnp.where(first, ox_before, up(own, 0))
        - txp * jnp.where(last, ox_after, down(own, 0))
        - tym * up(jnp.where(wide_yp, oy, own), 1) - typ * down(jnp.where(wide_ym, oy, own), 1)
    )
    qy = (
        diagonal * oy - t_in * oy_in - txmn * up(oy, 0) - txpn * down(oy, 0)
        - tym * up(jnp.where(wide_yp, own, oy), 1) - typ * down(jnp.where(wide_ym, own, oy), 1)
    )
    qz = (
        diagonal * oz - t_out * zb[parity, OWN] - txmn * up(oz, 0) - txpn * down(oz, 0)
        - tymn * oz_ym - typn * oz_yp
    )
    qz_in = -t_in * oz
    qzy = -(tymc * oz_ym + typc * oz_yp + t_out * zb[parity, OY])

    for offset, field in zip(FULL_OFFSETS, (q0, qy, qz, qzy, source)):
        add_rows((OZ, offset, 0), oz * field)
    add_rows((OWN, FULL_OFFSETS[2], 0), own * qz + own_in * qz_in)
    add_rows((OY, FULL_OFFSETS[2], 0), oy * qz + oy_in * qz_in)
    add_rows((OWN, FULL_OFFSETS[3], 0), own * qzy)
    add_rows((OY, FULL_OFFSETS[3], 0), oy * qzy)
    add_rows((OX, FULL_OFFSETS[3], -1), only(first, ox * qzy))
    ox_in = only(first, ox_s[pl.ds(SUB + z2, 1), :])
    add_rows((OX, FULL_OFFSETS[2], -1), only(first, ox * qz) + ox_in * qz_in)
    def merge(a, b, distance):
        lower = sub // distance % 2 == 0
        if 2 * distance == SUB:
            return jnp.where(lower, a, b) + pltpu.roll(jnp.where(lower, b, a), distance, 0)
        return jnp.where(
            lower, a + pltpu.roll(a, SUB - distance, 0), b + pltpu.roll(b, distance, 0)
        )

    nothing = jnp.zeros((SUB, ny), jnp.float32)
    for first_row in range(0, PADDED, SUB):
        group_of = [
            sums_of[PRODUCTS[n]] if n < len(PRODUCTS) else nothing
            for n in range(first_row, first_row + SUB)
        ]
        while len(group_of) > 1:
            distance = len(group_of) // 2
            group_of = [
                merge(group_of[j], group_of[j + distance], distance) for j in range(distance)
            ]
        acc[pl.ds(first_row, SUB), :] = group_of[0]

    sums = split_dot(half_table[...], acc[...], swap=True)
    stacked = jnp.concatenate(
        [sums] + [pltpu.roll(sums, LANES - g * cells, 1) for g in (1, 2, 3)], axis=0
    )
    routed = split_dot(route[...], stacked)
    routed = jnp.where(
        lax.broadcasted_iota(jnp.int32, routed.shape, 1) < cells, routed, 0.0
    )
    beside_pair = pair + 2 * parity - 1
    near_pair = jnp.clip(beside_pair, 0, pairs - 1)
    for target in range(6):
        block = routed[target * VALUES : (target + 1) * VALUES, :]
        if rows < VALUES:
            block = block[:rows, :] + pltpu.roll(block[rows:, :], span, 1)
        to_pair = near_pair if target % 2 else pair
        part[target] = pltpu.roll(block, to_pair * cells, 1)

    def fold_copy(sx, beside, which):
        to_pair = beside_pair if beside else pair
        role = layer - 2 * to_pair + 1
        slot = (1 - sx) * 4 + role
        n = ((sx + 1) * 2 + beside) * 2 + which
        return pltpu.make_async_remote_copy(
            part.at[(sx + 1) * 2 + beside], fold.at[slot], f_send.at[n], f_recv.at[slot],
            device_id=(tile + sx, 2 * to_pair + which), device_id_type=MESH,
        )

    def fold_valid(sx, beside, which):
        ok = (tile + sx >= 0) & (tile + sx < tiles)
        if beside:
            return ok & (beside_pair >= 0) & (beside_pair < pairs)
        return ok if sx else ok & (which != parity)

    fold_list = [(sx, b, w) for b in (1, 0) for sx in (-1, 1, 0) for w in (0, 1)]
    for item in fold_list:
        @pl.when(fold_valid(*item))
        def _():
            fold_copy(*item).start()

    for dt in (-1, 0, 1):
        for role in range(4):
            slot = (dt + 1) * 4 + role

            @pl.when(fold_from(dt, role))
            def _():
                pltpu.make_async_remote_copy(
                    part.at[0], fold.at[slot], f_send.at[0], f_recv.at[slot],
                    device_id=(tile, layer), device_id_type=MESH,
                ).wait_recv()

    terms = [part[2]] + [fold[slot] for slot in range(12)]
    gsend[...] = tree_sum(terms)

    def gather_copy(k):
        other = lax.rem(tile * pairs + pair + k, tiles * pairs)
        return pltpu.make_async_remote_copy(
            gsend, gath.at[tile * pairs + pair], g_send.at[k], g_recv.at[tile * pairs + pair],
            device_id=(other // pairs, 2 * (other % pairs) + parity), device_id_type=MESH,
        )

    far_first = sorted(
        range(1, tiles * pairs), key=lambda k: (k % pairs == 0, abs(k - tiles * pairs // 2))
    )
    for k in far_first:
        gather_copy(k).start()
    gath[tile * pairs + pair] = gsend[...]

    cell_at = lax.broadcasted_iota(jnp.int32, (LANES, ny), 0)
    fine_at = lax.broadcasted_iota(jnp.int32, (LANES, ny), 1)
    parent = fine_at // EDGE
    spread = jnp.where(cell_at == parent, 1.0, 0.0).astype(jnp.bfloat16)
    beside_y = parent + 2 * (fine_at // HALF % 2) - 1
    spread_y = jnp.where(cell_at == beside_y, 1.0, 0.0).astype(jnp.bfloat16)

    for sz in sides:
        @pl.when(has(0, sz))
        def _():
            for n in range(3):
                layer_copy(sz, n).wait_send()
    for sx in sides:
        @pl.when(has(sx, 0))
        def _():
            for copy in halo_copies(sx):
                copy.wait_send()
    for sx, sz in diagonals:
        @pl.when(has(sx, sz))
        def _():
            corner_copy(sx, sz).wait_send()
    for item in fold_list:
        @pl.when(fold_valid(*item))
        def _():
            fold_copy(*item).wait_send()
    for k in range(1, tiles * pairs):
        gather_copy(k).wait_send()

    for k in range(1, tiles * pairs):
        frm = lax.rem(tile * pairs + pair + tiles * pairs - k, tiles * pairs)
        pltpu.make_async_remote_copy(
            gsend, gath.at[frm], g_send.at[k], g_recv.at[frm],
            device_id=(tile, layer), device_id_type=MESH,
        ).wait_recv()

    for t in range(tiles):
        total = gath[t * pairs]
        for p in range(1, pairs):
            total = total + gath[t * pairs + p]
        gsum[pl.ds(t * rows, rows), :] = total
    lane_t = lax.broadcasted_iota(jnp.int32, (tiles, LANES), 1)

    def value(v):
        a = gsum[pl.ds(v % rows, tiles, stride=rows), :]
        if v >= rows:
            a = pltpu.roll(a, LANES - span, 1)
        return only(lane_t < span, a)

    def shifted(a, offset):
        ox, oz, oy = offset
        along = -(oz * cells + oy) % LANES
        if along:
            a = pltpu.roll(a, along, 1)
        if ox:
            a = pltpu.roll(a, -ox % tiles, 0)
        return a

    offsets = [((v + 13) // 9 - 1, (v + 13) // 3 % 3 - 1, (v + 13) % 3 - 1) for v in range(14)]
    forward = [value(v) for v in range(14)]
    backward = [
        shifted(forward[v], [-d for d in offsets[v]]) if v else None for v in range(14)
    ]
    rhs = value(RHS)
    scale = COARSE_DAMPING / jnp.where(lane_t < span, forward[0], 1.0)
    coarse = rhs * scale
    for _ in range(SWEEPS - 1):
        terms = [forward[0] * coarse]
        for v in range(1, 14):
            terms.append(forward[v] * shifted(coarse, offsets[v]))
            terms.append(backward[v] * shifted(coarse, [-d for d in offsets[v]]))
        coarse = coarse + (rhs - tree_sum(terms)) * scale
    csc[...] = coarse

    def coarse_row(t, p):
        a = jnp.broadcast_to(csc[pl.ds(t, 1), :], (SUB, LANES))
        return pltpu.roll(a, (LANES - p * cells) % LANES, 1)

    center = coarse_row(tile, pair)
    four = jnp.concatenate(
        [
            center,
            coarse_row(tile, near_pair),
            coarse_row(jnp.maximum(tile - 1, 0), pair),
            coarse_row(jnp.minimum(tile + 1, tiles - 1), pair),
        ],
        axis=0,
    )
    wide = split_dot(spread, four, swap=True)
    c_own, c_z = wide[:SUB, :], wide[SUB : 2 * SUB, :]
    c_y = split_dot(spread_y, center, swap=True)
    ze[0] = ze[0] * jnp.concatenate([c_z] * (nx // SUB), axis=0)
    at_edge = sub == parity * (SUB - 1)
    for i in range(nx):
        at = plane(i + 1)
        result = own_s[at, :] * c_own + oy_s[at, :] * c_y
        result = result + only(at_edge, ze[0, pl.ds(i, 1), :])
        if i == 0:
            result = result + ox_s[plane(1), :] * wide[2 * SUB : 3 * SUB, :]
        if i == nx - 1:
            result = result + ox_s[plane(2), :] * wide[3 * SUB :, :]
        out_ref[plane(i), :] = result


def body(tiles, layers, classes, well_mask, source):
    nx, nz, ny = classes.shape
    assert nx == EDGE and nz == HALF == SUB and layers % 2 == 0
    cells, pairs = ny // EDGE, layers // 2
    assert 4 * cells <= LANES and pairs * cells <= LANES
    rows = VALUES // 2 if 2 * pairs * cells <= LANES else VALUES
    flat = lambda a: a.reshape(nx * nz, ny)
    f32 = lambda *shape: pltpu.VMEM(shape, jnp.float32)
    dma = pltpu.SemaphoreType.DMA
    block = (nx * SUB, ny)
    wide = ((nx + 2) * SUB, ny)
    scratch = [
        pltpu.VMEM(block, jnp.int32), pltpu.VMEM(block, jnp.int32), f32(*block),
        pltpu.VMEM((6 * VALUES, 4 * PADDED), jnp.bfloat16),
        f32((nx + 4) * SUB, ny), f32(*wide), f32(2, 3, nx, ny), f32(2, 3, nx, ny),
        f32(4, 1, ny), f32(4, 1, ny),
        f32(2, 2, nx, ny), f32(2, 2, nx, ny), f32(4, nx, ny),
        f32(*block), f32(*block), f32((nx + 1) * SUB, ny), f32(*block), f32(*block), f32(*block),
        f32(*wide), f32(*wide), f32(*wide), f32(4 * SUB, ny), f32(2, nx, ny), f32(2, 4, nx, ny),
        pltpu.VMEM((6, nx, ny), jnp.int32), pltpu.VMEM((ny, LANES), jnp.bfloat16), f32(PADDED, ny), f32(6, rows, LANES), f32(12, rows, LANES), f32(rows, LANES),
        f32(tiles * pairs, rows, LANES), f32(tiles * rows, LANES), f32(tiles, LANES),
        dma((4,)), dma((2, 2)), dma((2, 2)), dma((2, 3)), dma((2, 3)), dma((4,)), dma((4,)),
        dma((12,)), dma((12,)), dma((tiles * pairs,)), dma((tiles * pairs,)),
    ]
    route = jnp.asarray(np.pad(routing_table(), ((0, 38), (0, 0), (0, 0))), jnp.bfloat16)
    result = pl.pallas_call(
        functools.partial(kernel, tiles, layers, nx, ny),
        out_shape=jax.ShapeDtypeStruct(block, jnp.float32),
        in_specs=[pl.BlockSpec(memory_space=pltpu.HBM)] * 4,
        out_specs=pl.BlockSpec(memory_space=pltpu.VMEM),
        scratch_shapes=scratch,
        compiler_params=pltpu.CompilerParams(
            collective_id=0, has_side_effects=True, vmem_limit_bytes=107 * 2**19
        ),
    )(flat(classes), flat(well_mask), flat(source), route)
    return result.reshape(nx, nz, ny)


def solution(mesh):
    spec = P("tile", "layer", None)
    return jax.shard_map(
        functools.partial(body, mesh.shape["tile"], mesh.shape["layer"]),
        mesh=mesh, in_specs=(spec, spec, spec), out_specs=spec, check_vma=False,
    )
```

```python
import functools

import jax
import jax.numpy as jnp
import numpy as np
from jax import lax
from jax.experimental import pallas as pl
from jax.experimental.pallas import tpu as pltpu
from jax.sharding import PartitionSpec as P

EDGE = 16
HALF = EDGE // 2
CLASSES = 16
SWEEPS = 4
FINE_DAMPING = 0.67
COARSE_DAMPING = 0.5
SINK_RATE = 0.5
VERTICAL_RATIO = 0.25
LANES = 128
SUB = 8
VALUES = 16
RHS = 14
MESH = pl.DeviceIdType.MESH

OWN, OX, OZ, OY = range(4)
FULL_OFFSETS = ((0, 0, 0), (0, 0, 1), (0, 1, 0), (0, 1, 1), None)
EDGE_OFFSETS = ((1, 0, 0), (1, 0, 1), (1, 1, 0))
PRODUCTS = (
    [(w, b, 0) for w in (OWN, OZ, OY) for b in FULL_OFFSETS]
    + [(OX, b, -1) for b in FULL_OFFSETS]
    + [(OX, None, 1)]
    + [(w, b, 1) for w in (OWN, OZ, OY, OX) for b in EDGE_OFFSETS]
    + [(OX, b, -1) for b in EDGE_OFFSETS]
)
SLOT = {product: index for index, product in enumerate(PRODUCTS)}
PADDED = -(-len(PRODUCTS) // SUB) * SUB


def routing_table():
    table = np.zeros((2, 6 * VALUES, 4 * PADDED), np.float32)
    for parity, sign_z in ((0, -1), (1, 1)):
        for n, (weight, toggled, sign_x) in enumerate(PRODUCTS):
            for half, sign_y in ((0, -1), (1, 1)):
                row = ((weight == OX) * sign_x, (weight == OZ) * sign_z, (weight == OY) * sign_y)
                if toggled is None:
                    value = RHS
                else:
                    column = (toggled[0] * sign_x, toggled[1] * sign_z, toggled[2] * sign_y)
                    o = [column[d] - row[d] for d in range(3)]
                    value = 9 * (o[0] + 1) + 3 * (o[1] + 1) + (o[2] + 1) - 13
                    if value < 0:
                        continue
                group = 2 * (weight == OY) + half
                target = (row[0] + 1) * 2 + (weight == OZ)
                table[parity, target * VALUES + value, group * PADDED + n] = 1.0
    return table


def split_dot(table, values, swap=False):
    total = None
    rest = values
    for _ in range(2):
        part = rest.astype(jnp.bfloat16)
        rest = rest - part.astype(jnp.float32)
        pair = (part, table) if swap else (table, part)
        term = jnp.dot(*pair, preferred_element_type=jnp.float32)
        total = term if total is None else total + term
    return total


def tree_sum(terms):
    while len(terms) > 1:
        terms = [sum(terms[n + 1 : n + 2], terms[n]) for n in range(0, len(terms), 2)]
    return terms[0]


def inverse_of(a):
    guarded = jnp.maximum(a, 1e-30)
    guess = pl.reciprocal(guarded, approx=True)
    return guess * (2.0 - guarded * guess)


def harmonic(a, b):
    return 2.0 * a * b * inverse_of(a + b)


def perm_of(classes):
    step = 5.0 / (CLASSES - 1)
    return jnp.exp(classes.astype(jnp.float32) * step - 2.5)


def sink_of(well, perm):
    return SINK_RATE * well.astype(jnp.float32) * perm


def kernel(
    tiles, layers, nx, ny,
    cls_hbm, well_hbm, src_hbm, route_hbm, out_ref,
    cls, well, src, route,
    kx, sk, zs, zr, crs, crr, zq, zw, ze,
    typ_s, tzi_s, txf, tzm_s, tzp_s, d_s, own_s, oy_s, oz_s, ox_s, tz_edge, zb,
    zi, half_table, acc, part, fold, gsend, gath, gsum, csc,
    in_sem, x_send, x_recv, z_send, z_recv, c_send, c_recv, f_send, f_recv, g_send, g_recv,
):
    tile = lax.axis_index("tile")
    layer = lax.axis_index("layer")
    pairs = layers // 2
    pair = layer // 2
    parity = layer % 2
    cells = ny // EDGE
    span = pairs * cells
    rows = part.shape[1]
    plane = lambda i: pl.ds(i * SUB, SUB)

    loads = [
        pltpu.make_async_copy(a, b, in_sem.at[n])
        for n, (a, b) in enumerate(
            ((cls_hbm, cls), (well_hbm, well), (src_hbm, src), (route_hbm.at[parity], route))
        )
    ]
    loads[0].start()
    loads[1].start()

    barrier = pltpu.get_barrier_semaphore()
    for a in range(tiles):
        for b in range(layers):
            if a or b:
                pl.semaphore_signal(
                    barrier, inc=1, device_id_type=MESH,
                    device_id=(lax.rem(tile + a, tiles), lax.rem(layer + b, layers)),
                )

    def fold_from(dt, role):
        from_layer = 2 * pair - 1 + role
        ok = (tile + dt >= 0) & (tile + dt < tiles)
        ok = ok & (from_layer >= 0) & (from_layer < layers)
        return ok & (from_layer != layer) if dt == 0 else ok

    for dt in (-1, 0, 1):
        for role in range(4):
            @pl.when(jnp.logical_not(fold_from(dt, role)))
            def _():
                fold[(dt + 1) * 4 + role] = jnp.zeros(fold.shape[1:], jnp.float32)

    loads[0].wait()
    loads[1].wait()
    loads[2].start()
    loads[3].start()

    ends = ((0, 1), (SUB - 1, SUB - 2))
    for side, (z1, z2) in enumerate(ends):
        for i in range(nx):
            zi[side, pl.ds(i, 1), :] = cls[pl.ds(i * SUB + z1, 1), :]
        k = perm_of(zi[side])
        zs[side, 0] = k
        crs[0 + side] = k[0:1, :]
        crs[2 + side] = k[nx - 1 : nx, :]

    def pack_planes():
        for i in (0, 1, nx - 2, nx - 1):
            k = perm_of(cls[plane(i), :])
            kx[plane(i + 2), :] = k
            if i in (0, nx - 1):
                sk[plane(i + 1), :] = sink_of(well[plane(i), :], k)

    def pack_rows():
        for side, (z1, z2) in enumerate(ends):
            for i in range(nx):
                zi[2 + side, pl.ds(i, 1), :] = cls[pl.ds(i * SUB + z2, 1), :]
                zi[4 + side, pl.ds(i, 1), :] = well[pl.ds(i * SUB + z1, 1), :]
            zs[side, 1] = perm_of(zi[2 + side])
            zs[side, 2] = sink_of(zi[4 + side], zs[side, 0])

    pl.semaphore_wait(barrier, tiles * layers - 1)

    def halo_copies(sx):
        lo = sx < 0
        src_k = kx.at[pl.ds((2 if lo else nx) * SUB, 2 * SUB), :]
        dst_k = kx.at[pl.ds((nx + 2 if lo else 0) * SUB, 2 * SUB), :]
        src_s = sk.at[plane(1 if lo else nx), :]
        dst_s = sk.at[plane(nx + 1 if lo else 0), :]
        s = 0 if lo else 1
        return [
            pltpu.make_async_remote_copy(
                a, b, x_send.at[s, n], x_recv.at[s, n],
                device_id=(tile + sx, layer), device_id_type=MESH,
            )
            for n, (a, b) in enumerate(((src_k, dst_k), (src_s, dst_s)))
        ]

    def layer_copy(sz, n):
        s = 0 if sz < 0 else 1
        return pltpu.make_async_remote_copy(
            zs.at[s, n], zr.at[1 - s, n], z_send.at[s, n], z_recv.at[s, n],
            device_id=(tile, layer + sz), device_id_type=MESH,
        )

    def corner_copy(sx, sz):
        a, b = (0 if sx < 0 else 1), (0 if sz < 0 else 1)
        return pltpu.make_async_remote_copy(
            crs.at[2 * a + b], crr.at[2 * (1 - a) + (1 - b)],
            c_send.at[2 * a + b], c_recv.at[2 * a + b],
            device_id=(tile + sx, layer + sz), device_id_type=MESH,
        )

    def has(sx, sz):
        ok = None
        for s, at, count in ((sx, tile, tiles), (sz, layer, layers)):
            if s:
                test = at > 0 if s < 0 else at < count - 1
                ok = test if ok is None else ok & test
        return ok

    sides = (-1, 1)
    diagonals = [(sx, sz) for sx in sides for sz in sides]
    for sz in sides:
        @pl.when(has(0, sz))
        def _():
            layer_copy(sz, 0).start()

        @pl.when(jnp.logical_not(has(0, sz)))
        def _():
            zr[0 if sz < 0 else 1] = jnp.zeros(zr.shape[1:], jnp.float32)
    pack_planes()
    for sx in sides:
        @pl.when(has(sx, 0))
        def _():
            for copy in halo_copies(sx):
                copy.start()

        @pl.when(jnp.logical_not(has(sx, 0)))
        def _():
            first = 0 if sx < 0 else nx + 2
            kx[pl.ds(first * SUB, 2 * SUB), :] = jnp.zeros((2 * SUB, ny), jnp.float32)
            sk[plane(0 if sx < 0 else nx + 1), :] = jnp.zeros((SUB, ny), jnp.float32)
    for sx, sz in diagonals:
        @pl.when(has(sx, sz))
        def _():
            corner_copy(sx, sz).start()

        @pl.when(jnp.logical_not(has(sx, sz)))
        def _():
            crr[2 * (0 if sx < 0 else 1) + (0 if sz < 0 else 1)] = jnp.zeros((1, ny), jnp.float32)
    pack_rows()
    for sz in sides:
        @pl.when(has(0, sz))
        def _():
            layer_copy(sz, 1).start()
            layer_copy(sz, 2).start()

    sub = lax.broadcasted_iota(jnp.int32, (SUB, ny), 0)
    lane = lax.broadcasted_iota(jnp.int32, (SUB, ny), 1)
    even = parity == 0
    cross_ym = lane % EDGE == 0
    cross_yp = lane % EDGE == EDGE - 1
    cross_zm = (sub == 0) & even
    cross_zp = (sub == SUB - 1) & jnp.logical_not(even)

    def up(a, dim):
        return pltpu.roll(a, 1, dim)

    def down(a, dim):
        return pltpu.roll(a, a.shape[dim] - 1, dim)

    def y_face(k):
        at = lax.broadcasted_iota(jnp.int32, k.shape, 1)
        return jnp.where(at == ny - 1, 0.0, harmonic(k, down(k, 1)))

    def only(mask, a):
        return jnp.where(mask, a, 0.0)

    for i in range(2, nx - 2):
        k = perm_of(cls[plane(i), :])
        kx[plane(i + 2), :] = k
        sk[plane(i + 1), :] = sink_of(well[plane(i), :], k)
    for i in (1, nx - 2):
        sk[plane(i + 1), :] = sink_of(well[plane(i), :], kx[plane(i + 2), :])

    def faces(i):
        at = plane(i)
        k = kx[plane(i + 2), :]
        typ_s[at, :] = y_face(k)
        tzi_s[at, :] = VERTICAL_RATIO * harmonic(k, up(k, 0))

        if i > 0:
            txf[at, :] = harmonic(kx[plane(i + 1), :], k)

    for i in range(nx):
        faces(i)

    fine = lax.broadcasted_iota(jnp.int32, (ny, LANES), 0)
    spot = lax.broadcasted_iota(jnp.int32, (ny, LANES), 1)
    group = spot // cells
    upper = group % 2
    wanted = fine // EDGE + jnp.where(group >= 2, 2 * upper - 1, 0)
    hit = (fine // HALF % 2 == upper) & (wanted == spot % cells) & (group < 4)
    half_table[...] = jnp.where(hit, 1.0, 0.0).astype(jnp.bfloat16)

    def wait_layers(n):
        for sz in sides:
            @pl.when(has(0, sz))
            def _():
                layer_copy(-sz, n).wait_recv()

    wait_layers(0)
    for sx in sides:
        @pl.when(has(sx, 0))
        def _():
            halo_copies(-sx)[0].wait_recv()
    txf[plane(0), :] = harmonic(kx[plane(1), :], kx[plane(2), :])
    txf[plane(nx), :] = harmonic(kx[plane(nx + 1), :], kx[plane(nx + 2), :])
    for side in (0, 1):
        tz_edge[side] = VERTICAL_RATIO * harmonic(zs[side, 0], zr[side, 0])

    def basis(sink, faces, crossing):
        diagonal = sink
        for pair_of in faces:
            diagonal = diagonal + pair_of[0] + pair_of[1]
        inverse = FINE_DAMPING * inverse_of(diagonal)
        leaving = sink
        for term in crossing:
            if term is not None:
                leaving = leaving + term
        outer = [None if term is None else term * inverse for term in crossing]
        return diagonal, 1.0 - leaving * inverse, outer

    def block_basis(i, edge):
        at = plane(i)
        after = plane(i + 1)
        inner = tzi_s[at, :]
        tzm = jnp.where(sub == 0, tz_edge[0, pl.ds(i, 1), :], inner)
        tzp = jnp.where(sub == SUB - 1, tz_edge[1, pl.ds(i, 1), :], down(inner, 0))
        txm = txf[at, :]
        txp = txf[after, :]
        typ = typ_s[at, :]
        tym = up(typ, 1)
        crossing = (
            None if edge == 0 else (txm if edge < 0 else txp),
            only(cross_zm, tzm) + only(cross_zp, tzp),
            only(cross_ym, tym) + only(cross_yp, typ),
        )
        diagonal, own, outer = basis(
            sk[after, :], ((txm, txp), (tzm, tzp), (tym, typ)), crossing
        )
        tzm_s[at, :] = tzm
        tzp_s[at, :] = tzp
        d_s[at, :] = diagonal
        own_s[after, :] = own
        if i >= nx - 2:
            oz_s[after, :] = outer[1]
        oy_s[after, :] = outer[2]
        if edge:
            ox_s[plane(1 if edge < 0 else 2), :] = outer[0]

    for i in range(nx):
        block_basis(i, -1 if i == 0 else int(i == nx - 1))

    for sx in sides:
        @pl.when(has(sx, 0))
        def _():
            halo_copies(-sx)[1].wait_recv()
    for sx, sz in diagonals:
        @pl.when(has(sx, sz))
        def _():
            corner_copy(-sx, -sz).wait_recv()

    for side in (0, 1):
        k1 = kx[plane(1 if side == 0 else nx + 2), :]
        k2 = kx[plane(0 if side == 0 else nx + 3), :]
        toward = txf[plane(0 if side == 0 else nx), :]
        inner = VERTICAL_RATIO * harmonic(k1, up(k1, 0))
        tzm = jnp.where(sub == 0, VERTICAL_RATIO * harmonic(k1, crr[2 * side]), inner)
        tzp = jnp.where(
            sub == SUB - 1, VERTICAL_RATIO * harmonic(k1, crr[2 * side + 1]), down(inner, 0)
        )
        typ = y_face(k1)
        tym = up(typ, 1)
        crossing = (
            toward,
            only(cross_zm, tzm) + only(cross_zp, tzp),
            only(cross_ym, tym) + only(cross_yp, typ),
        )
        _, own, outer = basis(
            sk[plane(0 if side == 0 else nx + 1), :],
            ((toward, harmonic(k1, k2)), (tzm, tzp), (tym, typ)),
            crossing,
        )
        at = plane(0 if side == 0 else nx + 1)
        own_s[at, :] = own
        ox_s[plane(0 if side == 0 else 3), :] = outer[0]
        oz_s[at, :] = outer[1]
        oy_s[at, :] = outer[2]

    loads[2].wait()
    loads[3].wait()

    sums_of = {}

    def add(product, term):
        sums_of[product] = sums_of[product] + term if product in sums_of else term

    def products(i, edge):
        at, mid, after = plane(i), plane(i + 1), plane(i + 2)
        diagonal, tzm, tzp, typ = d_s[at, :], tzm_s[at, :], tzp_s[at, :], typ_s[at, :]
        tym = up(typ, 1)
        txm, txp = txf[at, :], txf[mid, :]
        own, oy = own_s[mid, :], oy_s[mid, :]
        source = src[at, :]
        swap_m, swap_p = jnp.where(cross_yp, oy, own), jnp.where(cross_ym, oy, own)
        keep_m, keep_p = jnp.where(cross_yp, own, oy), jnp.where(cross_ym, own, oy)

        def z_pair(a):
            return (
                only(sub != 0, up(a, 0)),
                only(sub != SUB - 1, down(a, 0)),
            )

        own_zm, own_zp = z_pair(own)
        oy_zm, oy_zp = z_pair(oy)
        before_own = ox_s[plane(0), :] if edge < 0 else own_s[at, :]
        after_own = ox_s[plane(3), :] if edge > 0 else own_s[after, :]
        q0 = (
            diagonal * own - txm * before_own - txp * after_own
            - tym * up(swap_m, 1) - typ * down(swap_p, 1) - tzm * own_zm - tzp * own_zp
        )
        qy = (
            diagonal * oy - tym * up(keep_m, 1) - typ * down(keep_p, 1)
            - tzm * oy_zm - tzp * oy_zp
        )
        if edge >= 0:
            qy = qy - txm * oy_s[at, :]
        if edge <= 0:
            qy = qy - txp * oy_s[after, :]
        fields = (((0, 0, 0), q0), ((0, 0, 1), qy), (None, source))
        for kind, weight in ((OWN, own), (OY, oy)):
            for offset, field in fields:
                add((kind, offset, 0), weight * field)
        if edge < 0:
            ox = ox_s[plane(1), :]
            for offset, field in fields:
                add((OX, offset, -1), ox * field)
        if edge > 0:
            add((OX, None, 1), ox_s[plane(2), :] * source)

    def edge_products(i, edge):
        at, mid, row = plane(i), plane(i + 1), pl.ds(i, 1)
        diagonal, tzm, tzp, typ = d_s[at, :], tzm_s[at, :], tzp_s[at, :], typ_s[at, :]
        tym = up(typ, 1)
        txm, txp = txf[at, :], txf[mid, :]
        own, oy = own_s[mid, :], oy_s[mid, :]
        ox = ox_s[plane(1 if edge < 0 else 2), :]
        across, t_across = (plane(0), txm) if edge < 0 else (plane(nx + 1), txp)
        tymc, typc = only(cross_ym, tym), only(cross_yp, typ)
        tzmc, tzpc = only(cross_zm, tzm), only(cross_zp, tzp)
        ox_ym, ox_yp = up(ox, 1), down(ox, 1)
        ox_zm = jnp.where(sub == 0, zb[0, OX, row, :], up(ox, 0))
        ox_zp = jnp.where(sub == SUB - 1, zb[1, OX, row, :], down(ox, 0))
        qx = (
            diagonal * ox - t_across * own_s[across, :] - (tym - tymc) * ox_ym
            - (typ - typc) * ox_yp - (tzm - tzmc) * ox_zm - (tzp - tzpc) * ox_zp
        )
        qxy = -(t_across * oy_s[across, :] + tymc * ox_ym + typc * ox_yp)
        qxz = -(t_across * oz_s[across, :] + tzmc * ox_zm + tzpc * ox_zp)
        for offset, field in zip(EDGE_OFFSETS, (qx, qxy, qxz)):
            add((OX, offset, edge), ox * field)
            if edge > 0:
                for kind, weight in ((OWN, own), (OZ, oz_s[mid, :]), (OY, oy)):
                    add((kind, offset, 1), weight * field)
        if edge > 0:
            inward = -txm * ox
            for kind, ref in ((OWN, own_s), (OZ, oz_s), (OY, oy_s)):
                add((kind, EDGE_OFFSETS[0], 1), ref[at, :] * inward)

    for i in range(nx):
        products(i, -1 if i == 0 else int(i == nx - 1))

    wide_row = lax.broadcasted_iota(jnp.int32, (nx, ny), 0)
    wide_lane = lax.broadcasted_iota(jnp.int32, (nx, ny), 1)
    z1 = parity * (SUB - 1)
    z2 = 1 + parity * (SUB - 3)
    for i in range(nx):
        ze[1, pl.ds(i, 1), :] = own_s[pl.ds((i + 1) * SUB + z2, 1), :]
        ze[2, pl.ds(i, 1), :] = oy_s[pl.ds((i + 1) * SUB + z2, 1), :]
        ze[3, pl.ds(i, 1), :] = src[pl.ds(i * SUB + z1, 1), :]
        for side in (0, 1):
            at = pl.ds((i + 1) * SUB + side * (SUB - 1), 1)
            zw[side, 0, pl.ds(i, 1), :] = own_s[at, :]
            zw[side, 1, pl.ds(i, 1), :] = oy_s[at, :]
    first, last = wide_row == 0, wide_row == nx - 1
    wide_ym, wide_yp = wide_lane % EDGE == 0, wide_lane % EDGE == EDGE - 1
    k1 = zs[parity, 0]
    t_out = tz_edge[parity]
    t_in = VERTICAL_RATIO * harmonic(k1, zs[parity, 1])
    inner = harmonic(k1, up(k1, 0))
    txm = jnp.where(first, harmonic(k1, kx[pl.ds(SUB + z1, 1), :]), inner)
    txp = jnp.where(last, harmonic(k1, kx[pl.ds((nx + 2) * SUB + z1, 1), :]), down(inner, 0))
    typ = y_face(k1)
    tym = up(typ, 1)
    txmc, txpc = only(first, txm), only(last, txp)
    tymc, typc = only(wide_ym, tym), only(wide_yp, typ)
    diagonal, own, (ox, oz, oy) = basis(
        zs[parity, 2], ((txm, txp), (t_in, t_out), (tym, typ)),
        (txmc + txpc, t_out, tymc + typc),
    )
    ze[0] = oz
    txmn, txpn, tymn, typn = txm - txmc, txp - txpc, tym - tymc, typ - typc
    def rows_beside():
        wait_layers(1)
        wait_layers(2)
        for side in (0, 1):
            k1 = zr[side, 0]
            k2 = zr[side, 1]
            toward = tz_edge[side]
            inner = harmonic(k1, up(k1, 0))
            txm = jnp.where(wide_row == 0, harmonic(k1, crr[side]), inner)
            txp = jnp.where(wide_row == nx - 1, harmonic(k1, crr[2 + side]), down(inner, 0))
            typ = y_face(k1)
            tym = up(typ, 1)
            crosses = even if side == 0 else jnp.logical_not(even)
            crossing = (
                only(wide_row == 0, txm) + only(wide_row == nx - 1, txp),
                toward * crosses.astype(jnp.float32),
                only(wide_lane % EDGE == 0, tym) + only(wide_lane % EDGE == EDGE - 1, typ),
            )
            _, own, outer = basis(
                zr[side, 2],
                ((txm, txp), (toward, VERTICAL_RATIO * harmonic(k1, k2)), (tym, typ)),
                crossing,
            )
            zb[side, OWN] = own
            zb[side, OX] = outer[0]
            zb[side, OZ] = outer[1]
            zb[side, OY] = outer[2]
            zq[side, 0] = jnp.where(crosses, outer[1], own)
            zq[side, 1] = jnp.where(crosses, 0.0, outer[2])

    rows_beside()
    def add_rows(product, term):
        add(product, term[:SUB, :] + term[SUB:, :])

    for i, edge in ((0, -1), (nx - 1, 1)):
        edge_products(i, edge)
    for side in (0, 1):
        weights = (
            (OWN, 0, zw[side, 0]), (OY, 0, zw[side, 1]),
            (OX, -1, only(first, ox_s[pl.ds(SUB + side * (SUB - 1), 1), :])),
        )
        for n, offset in enumerate(FULL_OFFSETS[:2]):
            field = -tz_edge[side] * zq[side, n]
            for kind, at_side, weight in weights:
                add_rows((kind, offset, at_side), weight * field)

    own_in, oy_in, source = ze[1], ze[2], ze[3]
    ox_before, ox_after = ox_s[pl.ds(z1, 1), :], ox_s[pl.ds(3 * SUB + z1, 1), :]
    oz_ym, oz_yp = up(oz, 1), down(oz, 1)
    q0 = (
        diagonal * own - t_out * zb[parity, OZ] - t_in * own_in
        - txm * jnp.where(first, ox_before, up(own, 0))
        - txp * jnp.where(last, ox_after, down(own, 0))
        - tym * up(jnp.where(wide_yp, oy, own), 1) - typ * down(jnp.where(wide_ym, oy, own), 1)
    )
    qy = (
        diagonal * oy - t_in * oy_in - txmn * up(oy, 0) - txpn * down(oy, 0)
        - tym * up(jnp.where(wide_yp, own, oy), 1) - typ * down(jnp.where(wide_ym, own, oy), 1)
    )
    qz = (
        diagonal * oz - t_out * zb[parity, OWN] - txmn * up(oz, 0) - txpn * down(oz, 0)
        - tymn * oz_ym - typn * oz_yp
    )
    qz_in = -t_in * oz
    qzy = -(tymc * oz_ym + typc * oz_yp + t_out * zb[parity, OY])

    for offset, field in zip(FULL_OFFSETS, (q0, qy, qz, qzy, source)):
        add_rows((OZ, offset, 0), oz * field)
    add_rows((OWN, FULL_OFFSETS[2], 0), own * qz + own_in * qz_in)
    add_rows((OY, FULL_OFFSETS[2], 0), oy * qz + oy_in * qz_in)
    add_rows((OWN, FULL_OFFSETS[3], 0), own * qzy)
    add_rows((OY, FULL_OFFSETS[3], 0), oy * qzy)
    add_rows((OX, FULL_OFFSETS[3], -1), only(first, ox * qzy))
    ox_in = only(first, ox_s[pl.ds(SUB + z2, 1), :])
    add_rows((OX, FULL_OFFSETS[2], -1), only(first, ox * qz) + ox_in * qz_in)
    def merge(a, b, distance):
        lower = sub // distance % 2 == 0
        if 2 * distance == SUB:
            return jnp.where(lower, a, b) + pltpu.roll(jnp.where(lower, b, a), distance, 0)
        return jnp.where(
            lower, a + pltpu.roll(a, SUB - distance, 0), b + pltpu.roll(b, distance, 0)
        )

    nothing = jnp.zeros((SUB, ny), jnp.float32)
    for first_row in range(0, PADDED, SUB):
        group_of = [
            sums_of[PRODUCTS[n]] if n < len(PRODUCTS) else nothing
            for n in range(first_row, first_row + SUB)
        ]
        while len(group_of) > 1:
            distance = len(group_of) // 2
            group_of = [
                merge(group_of[j], group_of[j + distance], distance) for j in range(distance)
            ]
        acc[pl.ds(first_row, SUB), :] = group_of[0]

    sums = split_dot(half_table[...], acc[...], swap=True)
    stacked = jnp.concatenate(
        [sums] + [pltpu.roll(sums, LANES - g * cells, 1) for g in (1, 2, 3)], axis=0
    )
    routed = split_dot(route[...], stacked)
    routed = jnp.where(
        lax.broadcasted_iota(jnp.int32, routed.shape, 1) < cells, routed, 0.0
    )
    beside_pair = pair + 2 * parity - 1
    near_pair = jnp.clip(beside_pair, 0, pairs - 1)
    for target in range(6):
        block = routed[target * VALUES : (target + 1) * VALUES, :]
        part[target] = tree_sum(
            [
                pltpu.roll(block[g * rows : (g + 1) * rows, :], g * cells, 1) if g else block[:rows, :]
                for g in range(VALUES // rows)
            ]
        )

    def fold_copy(sx, beside, which):
        to_pair = beside_pair if beside else pair
        role = layer - 2 * to_pair + 1
        slot = (1 - sx) * 4 + role
        n = ((sx + 1) * 2 + beside) * 2 + which
        return pltpu.make_async_remote_copy(
            part.at[(sx + 1) * 2 + beside], fold.at[slot], f_send.at[n], f_recv.at[slot],
            device_id=(tile + sx, 2 * to_pair + which), device_id_type=MESH,
        )

    def fold_valid(sx, beside, which):
        ok = (tile + sx >= 0) & (tile + sx < tiles)
        if beside:
            return ok & (beside_pair >= 0) & (beside_pair < pairs)
        return ok if sx else ok & (which != parity)

    fold_list = [(sx, b, w) for b in (1, 0) for sx in (-1, 1, 0) for w in (0, 1)]
    for item in fold_list:
        @pl.when(fold_valid(*item))
        def _():
            fold_copy(*item).start()

    for dt in (-1, 0, 1):
        for role in range(4):
            slot = (dt + 1) * 4 + role

            @pl.when(fold_from(dt, role))
            def _():
                pltpu.make_async_remote_copy(
                    part.at[0], fold.at[slot], f_send.at[0], f_recv.at[slot],
                    device_id=(tile, layer), device_id_type=MESH,
                ).wait_recv()

    terms = [part[2]] + [fold[slot] for slot in range(12)]
    gsend[...] = tree_sum(terms)

    def gather_copy(k):
        other = lax.rem(tile * pairs + pair + k, tiles * pairs)
        return pltpu.make_async_remote_copy(
            gsend, gath.at[tile * pairs + pair], g_send.at[k], g_recv.at[tile * pairs + pair],
            device_id=(other // pairs, 2 * (other % pairs) + parity), device_id_type=MESH,
        )

    far_first = sorted(
        range(1, tiles * pairs), key=lambda k: (k % pairs == 0, abs(k - tiles * pairs // 2))
    )
    for k in far_first:
        gather_copy(k).start()
    gath[tile * pairs + pair] = gsend[...]

    cell_at = lax.broadcasted_iota(jnp.int32, (LANES, ny), 0)
    fine_at = lax.broadcasted_iota(jnp.int32, (LANES, ny), 1)
    parent = fine_at // EDGE
    spread = jnp.where(cell_at == parent, 1.0, 0.0).astype(jnp.bfloat16)
    beside_y = parent + 2 * (fine_at // HALF % 2) - 1
    spread_y = jnp.where(cell_at == beside_y, 1.0, 0.0).astype(jnp.bfloat16)

    for sz in sides:
        @pl.when(has(0, sz))
        def _():
            for n in range(3):
                layer_copy(sz, n).wait_send()
    for sx in sides:
        @pl.when(has(sx, 0))
        def _():
            for copy in halo_copies(sx):
                copy.wait_send()
    for sx, sz in diagonals:
        @pl.when(has(sx, sz))
        def _():
            corner_copy(sx, sz).wait_send()
    for item in fold_list:
        @pl.when(fold_valid(*item))
        def _():
            fold_copy(*item).wait_send()
    for k in range(1, tiles * pairs):
        gather_copy(k).wait_send()

    for k in range(1, tiles * pairs):
        frm = lax.rem(tile * pairs + pair + tiles * pairs - k, tiles * pairs)
        pltpu.make_async_remote_copy(
            gsend, gath.at[frm], g_send.at[k], g_recv.at[frm],
            device_id=(tile, layer), device_id_type=MESH,
        ).wait_recv()

    for p in range(pairs):
        for t in range(tiles):
            gsum[pl.ds((p * tiles + t) * rows, rows), :] = gath[t * pairs + p]
    lane_t = lax.broadcasted_iota(jnp.int32, (tiles, LANES), 1)

    def value(v):
        total = None
        for p in range(pairs):
            a = gsum[pl.ds(p * tiles * rows + v % rows, tiles, stride=rows), :]
            shift = (p - v // rows) * cells % LANES
            a = only(lane_t // cells == p, pltpu.roll(a, shift, 1) if shift else a)
            total = a if total is None else total + a
        return total

    def shifted(a, offset):
        ox, oz, oy = offset
        along = -(oz * cells + oy) % LANES
        if along:
            a = pltpu.roll(a, along, 1)
        if ox:
            a = pltpu.roll(a, -ox % tiles, 0)
        return a

    offsets = [((v + 13) // 9 - 1, (v + 13) // 3 % 3 - 1, (v + 13) % 3 - 1) for v in range(14)]
    forward = [value(v) for v in range(14)]
    backward = [
        shifted(forward[v], [-d for d in offsets[v]]) if v else None for v in range(14)
    ]
    rhs = value(RHS)
    scale = COARSE_DAMPING / jnp.where(lane_t < span, forward[0], 1.0)
    coarse = rhs * scale
    for _ in range(SWEEPS - 1):
        terms = [forward[0] * coarse]
        for v in range(1, 14):
            terms.append(forward[v] * shifted(coarse, offsets[v]))
            terms.append(backward[v] * shifted(coarse, [-d for d in offsets[v]]))
        coarse = coarse + (rhs - tree_sum(terms)) * scale
    csc[...] = coarse

    def coarse_row(t, p):
        a = jnp.broadcast_to(csc[pl.ds(t, 1), :], (SUB, LANES))
        return pltpu.roll(a, (LANES - p * cells) % LANES, 1)

    center = coarse_row(tile, pair)
    four = jnp.concatenate(
        [
            center,
            coarse_row(tile, near_pair),
            coarse_row(jnp.maximum(tile - 1, 0), pair),
            coarse_row(jnp.minimum(tile + 1, tiles - 1), pair),
        ],
        axis=0,
    )
    wide = split_dot(spread, four, swap=True)
    c_own, c_z = wide[:SUB, :], wide[SUB : 2 * SUB, :]
    c_y = split_dot(spread_y, center, swap=True)
    ze[0] = ze[0] * jnp.concatenate([c_z] * (nx // SUB), axis=0)
    at_edge = sub == parity * (SUB - 1)
    for i in range(nx):
        at = plane(i + 1)
        result = own_s[at, :] * c_own + oy_s[at, :] * c_y
        result = result + only(at_edge, ze[0, pl.ds(i, 1), :])
        if i == 0:
            result = result + ox_s[plane(1), :] * wide[2 * SUB : 3 * SUB, :]
        if i == nx - 1:
            result = result + ox_s[plane(2), :] * wide[3 * SUB :, :]
        out_ref[plane(i), :] = result


def body(tiles, layers, classes, well_mask, source):
    nx, nz, ny = classes.shape
    assert nx == EDGE and nz == HALF == SUB and layers % 2 == 0
    cells, pairs = ny // EDGE, layers // 2
    assert 4 * cells == LANES and pairs * cells <= LANES
    rows = VALUES * cells // LANES
    flat = lambda a: a.reshape(nx * nz, ny)
    f32 = lambda *shape: pltpu.VMEM(shape, jnp.float32)
    dma = pltpu.SemaphoreType.DMA
    block = (nx * SUB, ny)
    wide = ((nx + 2) * SUB, ny)
    scratch = [
        pltpu.VMEM(block, jnp.int32), pltpu.VMEM(block, jnp.int32), f32(*block),
        pltpu.VMEM((6 * VALUES, 4 * PADDED), jnp.bfloat16),
        f32((nx + 4) * SUB, ny), f32(*wide), f32(2, 3, nx, ny), f32(2, 3, nx, ny),
        f32(4, 1, ny), f32(4, 1, ny),
        f32(2, 2, nx, ny), f32(2, 2, nx, ny), f32(4, nx, ny),
        f32(*block), f32(*block), f32((nx + 1) * SUB, ny), f32(*block), f32(*block), f32(*block),
        f32(*wide), f32(*wide), f32(*wide), f32(4 * SUB, ny), f32(2, nx, ny), f32(2, 4, nx, ny),
        pltpu.VMEM((6, nx, ny), jnp.int32), pltpu.VMEM((ny, LANES), jnp.bfloat16), f32(PADDED, ny), f32(6, rows, LANES), f32(12, rows, LANES), f32(rows, LANES),
        f32(tiles * pairs, rows, LANES), f32(pairs * tiles * rows, LANES), f32(tiles, LANES),
        dma((4,)), dma((2, 2)), dma((2, 2)), dma((2, 3)), dma((2, 3)), dma((4,)), dma((4,)),
        dma((12,)), dma((12,)), dma((tiles * pairs,)), dma((tiles * pairs,)),
    ]
    route = jnp.asarray(np.pad(routing_table(), ((0, 38), (0, 0), (0, 0))), jnp.bfloat16)
    result = pl.pallas_call(
        functools.partial(kernel, tiles, layers, nx, ny),
        out_shape=jax.ShapeDtypeStruct(block, jnp.float32),
        in_specs=[pl.BlockSpec(memory_space=pltpu.HBM)] * 4,
        out_specs=pl.BlockSpec(memory_space=pltpu.VMEM),
        scratch_shapes=scratch,
        compiler_params=pltpu.CompilerParams(
            collective_id=0, has_side_effects=True, vmem_limit_bytes=107 * 2**19
        ),
    )(flat(classes), flat(well_mask), flat(source), route)
    return result.reshape(nx, nz, ny)


def solution(mesh):
    spec = P("tile", "layer", None)
    return jax.shard_map(
        functools.partial(body, mesh.shape["tile"], mesh.shape["layer"]),
        mesh=mesh, in_specs=(spec, spec, spec), out_specs=spec, check_vma=False,
    )
```

```python
import functools

import jax
import jax.numpy as jnp
import numpy as np
from jax import lax
from jax.experimental import pallas as pl
from jax.experimental.pallas import tpu as pltpu
from jax.sharding import PartitionSpec as P

EDGE = 16
HALF = EDGE // 2
CLASSES = 16
SWEEPS = 4
FINE_DAMPING = 0.67
COARSE_DAMPING = 0.5
SINK_RATE = 0.5
VERTICAL_RATIO = 0.25
LANES = 128
SUB = 8
VALUES = 16
RHS = 14
MESH = pl.DeviceIdType.MESH

OWN, OX, OZ, OY = range(4)
FULL_OFFSETS = ((0, 0, 0), (0, 0, 1), (0, 1, 0), (0, 1, 1), None)
EDGE_OFFSETS = ((1, 0, 0), (1, 0, 1), (1, 1, 0))
PRODUCTS = (
    [(w, b, 0) for w in (OWN, OZ, OY) for b in FULL_OFFSETS]
    + [(OX, b, -1) for b in FULL_OFFSETS]
    + [(OX, None, 1)]
    + [(w, b, 1) for w in (OWN, OZ, OY, OX) for b in EDGE_OFFSETS]
    + [(OX, b, -1) for b in EDGE_OFFSETS]
)
SLOT = {product: index for index, product in enumerate(PRODUCTS)}
PADDED = -(-len(PRODUCTS) // SUB) * SUB


def routing_table():
    table = np.zeros((2, 6 * VALUES, 4 * PADDED), np.float32)
    for parity, sign_z in ((0, -1), (1, 1)):
        for n, (weight, toggled, sign_x) in enumerate(PRODUCTS):
            for half, sign_y in ((0, -1), (1, 1)):
                row = ((weight == OX) * sign_x, (weight == OZ) * sign_z, (weight == OY) * sign_y)
                if toggled is None:
                    value = RHS
                else:
                    column = (toggled[0] * sign_x, toggled[1] * sign_z, toggled[2] * sign_y)
                    o = [column[d] - row[d] for d in range(3)]
                    value = 9 * (o[0] + 1) + 3 * (o[1] + 1) + (o[2] + 1) - 13
                    if value < 0:
                        continue
                group = 2 * (weight == OY) + half
                target = (row[0] + 1) * 2 + (weight == OZ)
                table[parity, target * VALUES + value, group * PADDED + n] = 1.0
    return table


def split_dot(table, values, swap=False):
    total = None
    rest = values
    for _ in range(2):
        part = rest.astype(jnp.bfloat16)
        rest = rest - part.astype(jnp.float32)
        pair = (part, table) if swap else (table, part)
        term = jnp.dot(*pair, preferred_element_type=jnp.float32)
        total = term if total is None else total + term
    return total


def tree_sum(terms):
    while len(terms) > 1:
        terms = [sum(terms[n + 1 : n + 2], terms[n]) for n in range(0, len(terms), 2)]
    return terms[0]


def inverse_of(a):
    guarded = jnp.maximum(a, 1e-30)
    guess = pl.reciprocal(guarded, approx=True)
    return guess * (2.0 - guarded * guess)


def harmonic(a, b):
    return 2.0 * a * b * inverse_of(a + b)


def perm_of(classes):
    step = 5.0 / (CLASSES - 1)
    return jnp.exp(classes.astype(jnp.float32) * step - 2.5)


def sink_of(well, perm):
    return SINK_RATE * well.astype(jnp.float32) * perm


def kernel(
    tiles, layers, nx, ny,
    cls_hbm, well_hbm, src_hbm, route_hbm, out_ref,
    cls, well, src, route,
    kx, sk, zs, zr, crs, crr, zq, zw, ze,
    typ_s, tzi_s, txf, tzm_s, tzp_s, d_s, own_s, oy_s, oz_s, ox_s, tz_edge, zb,
    zi, half_table, acc, part, fold, gsend, gath, gsum, csc,
    in_sem, x_send, x_recv, z_send, z_recv, c_send, c_recv, f_send, f_recv, g_send, g_recv,
):
    tile = lax.axis_index("tile")
    layer = lax.axis_index("layer")
    pairs = layers // 2
    pair = layer // 2
    parity = layer % 2
    cells = ny // EDGE
    span = pairs * cells
    rows = part.shape[1]
    plane = lambda i: pl.ds(i * SUB, SUB)

    loads = [
        pltpu.make_async_copy(a, b, in_sem.at[n])
        for n, (a, b) in enumerate(
            ((cls_hbm, cls), (well_hbm, well), (src_hbm, src), (route_hbm.at[parity], route))
        )
    ]
    loads[0].start()
    loads[1].start()

    barrier = pltpu.get_barrier_semaphore()
    for a in range(tiles):
        for b in range(layers):
            if a or b:
                pl.semaphore_signal(
                    barrier, inc=1, device_id_type=MESH,
                    device_id=(lax.rem(tile + a, tiles), lax.rem(layer + b, layers)),
                )

    def fold_from(dt, role):
        from_layer = 2 * pair - 1 + role
        ok = (tile + dt >= 0) & (tile + dt < tiles)
        ok = ok & (from_layer >= 0) & (from_layer < layers)
        return ok & (from_layer != layer) if dt == 0 else ok

    for dt in (-1, 0, 1):
        for role in range(4):
            @pl.when(jnp.logical_not(fold_from(dt, role)))
            def _():
                fold[(dt + 1) * 4 + role] = jnp.zeros(fold.shape[1:], jnp.float32)

    loads[0].wait()

    ends = ((0, 1), (SUB - 1, SUB - 2))
    for side, (z1, z2) in enumerate(ends):
        for i in range(nx):
            zi[side, pl.ds(i, 1), :] = cls[pl.ds(i * SUB + z1, 1), :]
        k = perm_of(zi[side])
        zs[side, 0] = k
        crs[0 + side] = k[0:1, :]
        crs[2 + side] = k[nx - 1 : nx, :]

    def pack_planes():
        for i in (0, 1, nx - 2, nx - 1):
            k = perm_of(cls[plane(i), :])
            kx[plane(i + 2), :] = k

    def pack_sinks():
        loads[1].wait()
        loads[2].start()
        loads[3].start()
        for i in (0, nx - 1):
            sk[plane(i + 1), :] = sink_of(well[plane(i), :], kx[plane(i + 2), :])

    def pack_rows():
        for side, (z1, z2) in enumerate(ends):
            for i in range(nx):
                zi[2 + side, pl.ds(i, 1), :] = cls[pl.ds(i * SUB + z2, 1), :]
                zi[4 + side, pl.ds(i, 1), :] = well[pl.ds(i * SUB + z1, 1), :]
            zs[side, 1] = perm_of(zi[2 + side])
            zs[side, 2] = sink_of(zi[4 + side], zs[side, 0])

    pl.semaphore_wait(barrier, tiles * layers - 1)

    def halo_copies(sx):
        lo = sx < 0
        src_k = kx.at[pl.ds((2 if lo else nx) * SUB, 2 * SUB), :]
        dst_k = kx.at[pl.ds((nx + 2 if lo else 0) * SUB, 2 * SUB), :]
        src_s = sk.at[plane(1 if lo else nx), :]
        dst_s = sk.at[plane(nx + 1 if lo else 0), :]
        s = 0 if lo else 1
        return [
            pltpu.make_async_remote_copy(
                a, b, x_send.at[s, n], x_recv.at[s, n],
                device_id=(tile + sx, layer), device_id_type=MESH,
            )
            for n, (a, b) in enumerate(((src_k, dst_k), (src_s, dst_s)))
        ]

    def layer_copy(sz, n):
        s = 0 if sz < 0 else 1
        return pltpu.make_async_remote_copy(
            zs.at[s, n], zr.at[1 - s, n], z_send.at[s, n], z_recv.at[s, n],
            device_id=(tile, layer + sz), device_id_type=MESH,
        )

    def corner_copy(sx, sz):
        a, b = (0 if sx < 0 else 1), (0 if sz < 0 else 1)
        return pltpu.make_async_remote_copy(
            crs.at[2 * a + b], crr.at[2 * (1 - a) + (1 - b)],
            c_send.at[2 * a + b], c_recv.at[2 * a + b],
            device_id=(tile + sx, layer + sz), device_id_type=MESH,
        )

    def has(sx, sz):
        ok = None
        for s, at, count in ((sx, tile, tiles), (sz, layer, layers)):
            if s:
                test = at > 0 if s < 0 else at < count - 1
                ok = test if ok is None else ok & test
        return ok

    sides = (-1, 1)
    diagonals = [(sx, sz) for sx in sides for sz in sides]
    for sz in sides:
        @pl.when(has(0, sz))
        def _():
            layer_copy(sz, 0).start()

        @pl.when(jnp.logical_not(has(0, sz)))
        def _():
            zr[0 if sz < 0 else 1] = jnp.zeros(zr.shape[1:], jnp.float32)
    pack_planes()
    for sx in sides:
        @pl.when(has(sx, 0))
        def _():
            halo_copies(sx)[0].start()

        @pl.when(jnp.logical_not(has(sx, 0)))
        def _():
            first = 0 if sx < 0 else nx + 2
            kx[pl.ds(first * SUB, 2 * SUB), :] = jnp.zeros((2 * SUB, ny), jnp.float32)
            sk[plane(0 if sx < 0 else nx + 1), :] = jnp.zeros((SUB, ny), jnp.float32)
    for sx, sz in diagonals:
        @pl.when(has(sx, sz))
        def _():
            corner_copy(sx, sz).start()

        @pl.when(jnp.logical_not(has(sx, sz)))
        def _():
            crr[2 * (0 if sx < 0 else 1) + (0 if sz < 0 else 1)] = jnp.zeros((1, ny), jnp.float32)
    pack_sinks()
    for sx in sides:
        @pl.when(has(sx, 0))
        def _():
            halo_copies(sx)[1].start()

    pack_rows()
    for sz in sides:
        @pl.when(has(0, sz))
        def _():
            layer_copy(sz, 1).start()
            layer_copy(sz, 2).start()

    sub = lax.broadcasted_iota(jnp.int32, (SUB, ny), 0)
    lane = lax.broadcasted_iota(jnp.int32, (SUB, ny), 1)
    even = parity == 0
    cross_ym = lane % EDGE == 0
    cross_yp = lane % EDGE == EDGE - 1
    cross_zm = (sub == 0) & even
    cross_zp = (sub == SUB - 1) & jnp.logical_not(even)

    def up(a, dim):
        return pltpu.roll(a, 1, dim)

    def down(a, dim):
        return pltpu.roll(a, a.shape[dim] - 1, dim)

    def y_face(k):
        at = lax.broadcasted_iota(jnp.int32, k.shape, 1)
        return jnp.where(at == ny - 1, 0.0, harmonic(k, down(k, 1)))

    def only(mask, a):
        return jnp.where(mask, a, 0.0)

    for i in range(2, nx - 2):
        k = perm_of(cls[plane(i), :])
        kx[plane(i + 2), :] = k
        sk[plane(i + 1), :] = sink_of(well[plane(i), :], k)
    for i in (1, nx - 2):
        sk[plane(i + 1), :] = sink_of(well[plane(i), :], kx[plane(i + 2), :])

    def faces(i):
        at = plane(i)
        k = kx[plane(i + 2), :]
        typ_s[at, :] = y_face(k)
        tzi_s[at, :] = VERTICAL_RATIO * harmonic(k, up(k, 0))

        if i > 0:
            txf[at, :] = harmonic(kx[plane(i + 1), :], k)

    for i in range(nx):
        faces(i)

    fine = lax.broadcasted_iota(jnp.int32, (ny, LANES), 0)
    spot = lax.broadcasted_iota(jnp.int32, (ny, LANES), 1)
    group = spot // cells
    upper = group % 2
    wanted = fine // EDGE + jnp.where(group >= 2, 2 * upper - 1, 0)
    hit = (fine // HALF % 2 == upper) & (wanted == spot % cells) & (group < 4)
    half_table[...] = jnp.where(hit, 1.0, 0.0).astype(jnp.bfloat16)

    def wait_layers(n):
        for sz in sides:
            @pl.when(has(0, sz))
            def _():
                layer_copy(-sz, n).wait_recv()

    wait_layers(0)
    for sx in sides:
        @pl.when(has(sx, 0))
        def _():
            halo_copies(-sx)[0].wait_recv()
    txf[plane(0), :] = harmonic(kx[plane(1), :], kx[plane(2), :])
    txf[plane(nx), :] = harmonic(kx[plane(nx + 1), :], kx[plane(nx + 2), :])
    for side in (0, 1):
        tz_edge[side] = VERTICAL_RATIO * harmonic(zs[side, 0], zr[side, 0])

    def basis(sink, faces, crossing):
        diagonal = sink
        for pair_of in faces:
            diagonal = diagonal + pair_of[0] + pair_of[1]
        inverse = FINE_DAMPING * inverse_of(diagonal)
        leaving = sink
        for term in crossing:
            if term is not None:
                leaving = leaving + term
        outer = [None if term is None else term * inverse for term in crossing]
        return diagonal, 1.0 - leaving * inverse, outer

    def block_basis(i, edge):
        at = plane(i)
        after = plane(i + 1)
        inner = tzi_s[at, :]
        tzm = jnp.where(sub == 0, tz_edge[0, pl.ds(i, 1), :], inner)
        tzp = jnp.where(sub == SUB - 1, tz_edge[1, pl.ds(i, 1), :], down(inner, 0))
        txm = txf[at, :]
        txp = txf[after, :]
        typ = typ_s[at, :]
        tym = up(typ, 1)
        crossing = (
            None if edge == 0 else (txm if edge < 0 else txp),
            only(cross_zm, tzm) + only(cross_zp, tzp),
            only(cross_ym, tym) + only(cross_yp, typ),
        )
        diagonal, own, outer = basis(
            sk[after, :], ((txm, txp), (tzm, tzp), (tym, typ)), crossing
        )
        tzm_s[at, :] = tzm
        tzp_s[at, :] = tzp
        d_s[at, :] = diagonal
        own_s[after, :] = own
        if i >= nx - 2:
            oz_s[after, :] = outer[1]
        oy_s[after, :] = outer[2]
        if edge:
            ox_s[plane(1 if edge < 0 else 2), :] = outer[0]

    for i in range(nx):
        block_basis(i, -1 if i == 0 else int(i == nx - 1))

    for sx in sides:
        @pl.when(has(sx, 0))
        def _():
            halo_copies(-sx)[1].wait_recv()
    for sx, sz in diagonals:
        @pl.when(has(sx, sz))
        def _():
            corner_copy(-sx, -sz).wait_recv()

    for side in (0, 1):
        k1 = kx[plane(1 if side == 0 else nx + 2), :]
        k2 = kx[plane(0 if side == 0 else nx + 3), :]
        toward = txf[plane(0 if side == 0 else nx), :]
        inner = VERTICAL_RATIO * harmonic(k1, up(k1, 0))
        tzm = jnp.where(sub == 0, VERTICAL_RATIO * harmonic(k1, crr[2 * side]), inner)
        tzp = jnp.where(
            sub == SUB - 1, VERTICAL_RATIO * harmonic(k1, crr[2 * side + 1]), down(inner, 0)
        )
        typ = y_face(k1)
        tym = up(typ, 1)
        crossing = (
            toward,
            only(cross_zm, tzm) + only(cross_zp, tzp),
            only(cross_ym, tym) + only(cross_yp, typ),
        )
        _, own, outer = basis(
            sk[plane(0 if side == 0 else nx + 1), :],
            ((toward, harmonic(k1, k2)), (tzm, tzp), (tym, typ)),
            crossing,
        )
        at = plane(0 if side == 0 else nx + 1)
        own_s[at, :] = own
        ox_s[plane(0 if side == 0 else 3), :] = outer[0]
        oz_s[at, :] = outer[1]
        oy_s[at, :] = outer[2]

    loads[2].wait()
    loads[3].wait()

    sums_of = {}

    def add(product, term):
        sums_of[product] = sums_of[product] + term if product in sums_of else term

    def products(i, edge):
        at, mid, after = plane(i), plane(i + 1), plane(i + 2)
        diagonal, tzm, tzp, typ = d_s[at, :], tzm_s[at, :], tzp_s[at, :], typ_s[at, :]
        tym = up(typ, 1)
        txm, txp = txf[at, :], txf[mid, :]
        own, oy = own_s[mid, :], oy_s[mid, :]
        source = src[at, :]
        swap_m, swap_p = jnp.where(cross_yp, oy, own), jnp.where(cross_ym, oy, own)
        keep_m, keep_p = jnp.where(cross_yp, own, oy), jnp.where(cross_ym, own, oy)

        def z_pair(a):
            return (
                only(sub != 0, up(a, 0)),
                only(sub != SUB - 1, down(a, 0)),
            )

        own_zm, own_zp = z_pair(own)
        oy_zm, oy_zp = z_pair(oy)
        before_own = ox_s[plane(0), :] if edge < 0 else own_s[at, :]
        after_own = ox_s[plane(3), :] if edge > 0 else own_s[after, :]
        q0 = (
            diagonal * own - txm * before_own - txp * after_own
            - tym * up(swap_m, 1) - typ * down(swap_p, 1) - tzm * own_zm - tzp * own_zp
        )
        qy = (
            diagonal * oy - tym * up(keep_m, 1) - typ * down(keep_p, 1)
            - tzm * oy_zm - tzp * oy_zp
        )
        if edge >= 0:
            qy = qy - txm * oy_s[at, :]
        if edge <= 0:
            qy = qy - txp * oy_s[after, :]
        fields = (((0, 0, 0), q0), ((0, 0, 1), qy), (None, source))
        for kind, weight in ((OWN, own), (OY, oy)):
            for offset, field in fields:
                add((kind, offset, 0), weight * field)
        if edge < 0:
            ox = ox_s[plane(1), :]
            for offset, field in fields:
                add((OX, offset, -1), ox * field)
        if edge > 0:
            add((OX, None, 1), ox_s[plane(2), :] * source)

    def edge_products(i, edge):
        at, mid, row = plane(i), plane(i + 1), pl.ds(i, 1)
        diagonal, tzm, tzp, typ = d_s[at, :], tzm_s[at, :], tzp_s[at, :], typ_s[at, :]
        tym = up(typ, 1)
        txm, txp = txf[at, :], txf[mid, :]
        own, oy = own_s[mid, :], oy_s[mid, :]
        ox = ox_s[plane(1 if edge < 0 else 2), :]
        across, t_across = (plane(0), txm) if edge < 0 else (plane(nx + 1), txp)
        tymc, typc = only(cross_ym, tym), only(cross_yp, typ)
        tzmc, tzpc = only(cross_zm, tzm), only(cross_zp, tzp)
        ox_ym, ox_yp = up(ox, 1), down(ox, 1)
        ox_zm = jnp.where(sub == 0, zb[0, OX, row, :], up(ox, 0))
        ox_zp = jnp.where(sub == SUB - 1, zb[1, OX, row, :], down(ox, 0))
        qx = (
            diagonal * ox - t_across * own_s[across, :] - (tym - tymc) * ox_ym
            - (typ - typc) * ox_yp - (tzm - tzmc) * ox_zm - (tzp - tzpc) * ox_zp
        )
        qxy = -(t_across * oy_s[across, :] + tymc * ox_ym + typc * ox_yp)
        qxz = -(t_across * oz_s[across, :] + tzmc * ox_zm + tzpc * ox_zp)
        for offset, field in zip(EDGE_OFFSETS, (qx, qxy, qxz)):
            add((OX, offset, edge), ox * field)
            if edge > 0:
                for kind, weight in ((OWN, own), (OZ, oz_s[mid, :]), (OY, oy)):
                    add((kind, offset, 1), weight * field)
        if edge > 0:
            inward = -txm * ox
            for kind, ref in ((OWN, own_s), (OZ, oz_s), (OY, oy_s)):
                add((kind, EDGE_OFFSETS[0], 1), ref[at, :] * inward)

    for i in range(nx):
        products(i, -1 if i == 0 else int(i == nx - 1))

    wide_row = lax.broadcasted_iota(jnp.int32, (nx, ny), 0)
    wide_lane = lax.broadcasted_iota(jnp.int32, (nx, ny), 1)
    z1 = parity * (SUB - 1)
    z2 = 1 + parity * (SUB - 3)
    for i in range(nx):
        ze[1, pl.ds(i, 1), :] = own_s[pl.ds((i + 1) * SUB + z2, 1), :]
        ze[2, pl.ds(i, 1), :] = oy_s[pl.ds((i + 1) * SUB + z2, 1), :]
        ze[3, pl.ds(i, 1), :] = src[pl.ds(i * SUB + z1, 1), :]
        for side in (0, 1):
            at = pl.ds((i + 1) * SUB + side * (SUB - 1), 1)
            zw[side, 0, pl.ds(i, 1), :] = own_s[at, :]
            zw[side, 1, pl.ds(i, 1), :] = oy_s[at, :]
    first, last = wide_row == 0, wide_row == nx - 1
    wide_ym, wide_yp = wide_lane % EDGE == 0, wide_lane % EDGE == EDGE - 1
    k1 = zs[parity, 0]
    t_out = tz_edge[parity]
    t_in = VERTICAL_RATIO * harmonic(k1, zs[parity, 1])
    inner = harmonic(k1, up(k1, 0))
    txm = jnp.where(first, harmonic(k1, kx[pl.ds(SUB + z1, 1), :]), inner)
    txp = jnp.where(last, harmonic(k1, kx[pl.ds((nx + 2) * SUB + z1, 1), :]), down(inner, 0))
    typ = y_face(k1)
    tym = up(typ, 1)
    txmc, txpc = only(first, txm), only(last, txp)
    tymc, typc = only(wide_ym, tym), only(wide_yp, typ)
    diagonal, own, (ox, oz, oy) = basis(
        zs[parity, 2], ((txm, txp), (t_in, t_out), (tym, typ)),
        (txmc + txpc, t_out, tymc + typc),
    )
    ze[0] = oz
    txmn, txpn, tymn, typn = txm - txmc, txp - txpc, tym - tymc, typ - typc
    def rows_beside():
        wait_layers(1)
        wait_layers(2)
        for side in (0, 1):
            k1 = zr[side, 0]
            k2 = zr[side, 1]
            toward = tz_edge[side]
            inner = harmonic(k1, up(k1, 0))
            txm = jnp.where(wide_row == 0, harmonic(k1, crr[side]), inner)
            txp = jnp.where(wide_row == nx - 1, harmonic(k1, crr[2 + side]), down(inner, 0))
            typ = y_face(k1)
            tym = up(typ, 1)
            crosses = even if side == 0 else jnp.logical_not(even)
            crossing = (
                only(wide_row == 0, txm) + only(wide_row == nx - 1, txp),
                toward * crosses.astype(jnp.float32),
                only(wide_lane % EDGE == 0, tym) + only(wide_lane % EDGE == EDGE - 1, typ),
            )
            _, own, outer = basis(
                zr[side, 2],
                ((txm, txp), (toward, VERTICAL_RATIO * harmonic(k1, k2)), (tym, typ)),
                crossing,
            )
            zb[side, OWN] = own
            zb[side, OX] = outer[0]
            zb[side, OZ] = outer[1]
            zb[side, OY] = outer[2]
            zq[side, 0] = jnp.where(crosses, outer[1], own)
            zq[side, 1] = jnp.where(crosses, 0.0, outer[2])

    rows_beside()
    def add_rows(product, term):
        add(product, term[:SUB, :] + term[SUB:, :])

    for i, edge in ((0, -1), (nx - 1, 1)):
        edge_products(i, edge)
    for side in (0, 1):
        weights = (
            (OWN, 0, zw[side, 0]), (OY, 0, zw[side, 1]),
            (OX, -1, only(first, ox_s[pl.ds(SUB + side * (SUB - 1), 1), :])),
        )
        for n, offset in enumerate(FULL_OFFSETS[:2]):
            field = -tz_edge[side] * zq[side, n]
            for kind, at_side, weight in weights:
                add_rows((kind, offset, at_side), weight * field)

    own_in, oy_in, source = ze[1], ze[2], ze[3]
    ox_before, ox_after = ox_s[pl.ds(z1, 1), :], ox_s[pl.ds(3 * SUB + z1, 1), :]
    oz_ym, oz_yp = up(oz, 1), down(oz, 1)
    q0 = (
        diagonal * own - t_out * zb[parity, OZ] - t_in * own_in
        - txm * jnp.where(first, ox_before, up(own, 0))
        - txp * jnp.where(last, ox_after, down(own, 0))
        - tym * up(jnp.where(wide_yp, oy, own), 1) - typ * down(jnp.where(wide_ym, oy, own), 1)
    )
    qy = (
        diagonal * oy - t_in * oy_in - txmn * up(oy, 0) - txpn * down(oy, 0)
        - tym * up(jnp.where(wide_yp, own, oy), 1) - typ * down(jnp.where(wide_ym, own, oy), 1)
    )
    qz = (
        diagonal * oz - t_out * zb[parity, OWN] - txmn * up(oz, 0) - txpn * down(oz, 0)
        - tymn * oz_ym - typn * oz_yp
    )
    qz_in = -t_in * oz
    qzy = -(tymc * oz_ym + typc * oz_yp + t_out * zb[parity, OY])

    for offset, field in zip(FULL_OFFSETS, (q0, qy, qz, qzy, source)):
        add_rows((OZ, offset, 0), oz * field)
    add_rows((OWN, FULL_OFFSETS[2], 0), own * qz + own_in * qz_in)
    add_rows((OY, FULL_OFFSETS[2], 0), oy * qz + oy_in * qz_in)
    add_rows((OWN, FULL_OFFSETS[3], 0), own * qzy)
    add_rows((OY, FULL_OFFSETS[3], 0), oy * qzy)
    add_rows((OX, FULL_OFFSETS[3], -1), only(first, ox * qzy))
    ox_in = only(first, ox_s[pl.ds(SUB + z2, 1), :])
    add_rows((OX, FULL_OFFSETS[2], -1), only(first, ox * qz) + ox_in * qz_in)
    def merge(a, b, distance):
        lower = sub // distance % 2 == 0
        if 2 * distance == SUB:
            return jnp.where(lower, a, b) + pltpu.roll(jnp.where(lower, b, a), distance, 0)
        return jnp.where(
            lower, a + pltpu.roll(a, SUB - distance, 0), b + pltpu.roll(b, distance, 0)
        )

    nothing = jnp.zeros((SUB, ny), jnp.float32)
    for first_row in range(0, PADDED, SUB):
        group_of = [
            sums_of[PRODUCTS[n]] if n < len(PRODUCTS) else nothing
            for n in range(first_row, first_row + SUB)
        ]
        while len(group_of) > 1:
            distance = len(group_of) // 2
            group_of = [
                merge(group_of[j], group_of[j + distance], distance) for j in range(distance)
            ]
        acc[pl.ds(first_row, SUB), :] = group_of[0]

    sums = split_dot(half_table[...], acc[...], swap=True)
    stacked = jnp.concatenate(
        [sums] + [pltpu.roll(sums, LANES - g * cells, 1) for g in (1, 2, 3)], axis=0
    )
    routed = split_dot(route[...], stacked)
    routed = jnp.where(
        lax.broadcasted_iota(jnp.int32, routed.shape, 1) < cells, routed, 0.0
    )
    beside_pair = pair + 2 * parity - 1
    near_pair = jnp.clip(beside_pair, 0, pairs - 1)
    for target in range(6):
        block = routed[target * VALUES : (target + 1) * VALUES, :]
        part[target] = tree_sum(
            [
                pltpu.roll(block[g * rows : (g + 1) * rows, :], g * cells, 1) if g else block[:rows, :]
                for g in range(VALUES // rows)
            ]
        )

    def fold_copy(sx, beside, which):
        to_pair = beside_pair if beside else pair
        role = layer - 2 * to_pair + 1
        slot = (1 - sx) * 4 + role
        n = ((sx + 1) * 2 + beside) * 2 + which
        return pltpu.make_async_remote_copy(
            part.at[(sx + 1) * 2 + beside], fold.at[slot], f_send.at[n], f_recv.at[slot],
            device_id=(tile + sx, 2 * to_pair + which), device_id_type=MESH,
        )

    def fold_valid(sx, beside, which):
        ok = (tile + sx >= 0) & (tile + sx < tiles)
        if beside:
            return ok & (beside_pair >= 0) & (beside_pair < pairs)
        return ok if sx else ok & (which != parity)

    fold_list = [(sx, b, w) for b in (1, 0) for sx in (-1, 1, 0) for w in (0, 1)]
    for item in fold_list:
        @pl.when(fold_valid(*item))
        def _():
            fold_copy(*item).start()

    for dt in (-1, 0, 1):
        for role in range(4):
            slot = (dt + 1) * 4 + role

            @pl.when(fold_from(dt, role))
            def _():
                pltpu.make_async_remote_copy(
                    part.at[0], fold.at[slot], f_send.at[0], f_recv.at[slot],
                    device_id=(tile, layer), device_id_type=MESH,
                ).wait_recv()

    terms = [part[2]] + [fold[slot] for slot in range(12)]
    gsend[...] = tree_sum(terms)

    def gather_copy(k):
        other = lax.rem(tile * pairs + pair + k, tiles * pairs)
        return pltpu.make_async_remote_copy(
            gsend, gath.at[tile * pairs + pair], g_send.at[k], g_recv.at[tile * pairs + pair],
            device_id=(other // pairs, 2 * (other % pairs) + parity), device_id_type=MESH,
        )

    far_first = sorted(
        range(1, tiles * pairs), key=lambda k: (k % pairs == 0, abs(k - tiles * pairs // 2))
    )
    for k in far_first:
        gather_copy(k).start()
    gath[tile * pairs + pair] = gsend[...]

    cell_at = lax.broadcasted_iota(jnp.int32, (LANES, ny), 0)
    fine_at = lax.broadcasted_iota(jnp.int32, (LANES, ny), 1)
    parent = fine_at // EDGE
    spread = jnp.where(cell_at == parent, 1.0, 0.0).astype(jnp.bfloat16)
    beside_y = parent + 2 * (fine_at // HALF % 2) - 1
    spread_y = jnp.where(cell_at == beside_y, 1.0, 0.0).astype(jnp.bfloat16)

    for sz in sides:
        @pl.when(has(0, sz))
        def _():
            for n in range(3):
                layer_copy(sz, n).wait_send()
    for sx in sides:
        @pl.when(has(sx, 0))
        def _():
            for copy in halo_copies(sx):
                copy.wait_send()
    for sx, sz in diagonals:
        @pl.when(has(sx, sz))
        def _():
            corner_copy(sx, sz).wait_send()
    for item in fold_list:
        @pl.when(fold_valid(*item))
        def _():
            fold_copy(*item).wait_send()
    for k in range(1, tiles * pairs):
        gather_copy(k).wait_send()

    for k in range(1, tiles * pairs):
        frm = lax.rem(tile * pairs + pair + tiles * pairs - k, tiles * pairs)
        pltpu.make_async_remote_copy(
            gsend, gath.at[frm], g_send.at[k], g_recv.at[frm],
            device_id=(tile, layer), device_id_type=MESH,
        ).wait_recv()

    for p in range(pairs):
        for t in range(tiles):
            gsum[pl.ds((p * tiles + t) * rows, rows), :] = gath[t * pairs + p]
    lane_t = lax.broadcasted_iota(jnp.int32, (tiles, LANES), 1)

    def value(v):
        total = None
        for p in range(pairs):
            a = gsum[pl.ds(p * tiles * rows + v % rows, tiles, stride=rows), :]
            shift = (p - v // rows) * cells % LANES
            a = only(lane_t // cells == p, pltpu.roll(a, shift, 1) if shift else a)
            total = a if total is None else total + a
        return total

    def shifted(a, offset):
        ox, oz, oy = offset
        along = -(oz * cells + oy) % LANES
        if along:
            a = pltpu.roll(a, along, 1)
        if ox:
            a = pltpu.roll(a, -ox % tiles, 0)
        return a

    offsets = [((v + 13) // 9 - 1, (v + 13) // 3 % 3 - 1, (v + 13) % 3 - 1) for v in range(14)]
    forward = [value(v) for v in range(14)]
    backward = [
        shifted(forward[v], [-d for d in offsets[v]]) if v else None for v in range(14)
    ]
    rhs = value(RHS)
    scale = COARSE_DAMPING / jnp.where(lane_t < span, forward[0], 1.0)
    coarse = rhs * scale
    for _ in range(SWEEPS - 1):
        terms = [forward[0] * coarse]
        for v in range(1, 14):
            terms.append(forward[v] * shifted(coarse, offsets[v]))
            terms.append(backward[v] * shifted(coarse, [-d for d in offsets[v]]))
        coarse = coarse + (rhs - tree_sum(terms)) * scale
    csc[...] = coarse

    def coarse_row(t, p):
        a = jnp.broadcast_to(csc[pl.ds(t, 1), :], (SUB, LANES))
        return pltpu.roll(a, (LANES - p * cells) % LANES, 1)

    center = coarse_row(tile, pair)
    four = jnp.concatenate(
        [
            center,
            coarse_row(tile, near_pair),
            coarse_row(jnp.maximum(tile - 1, 0), pair),
            coarse_row(jnp.minimum(tile + 1, tiles - 1), pair),
        ],
        axis=0,
    )
    wide = split_dot(spread, four, swap=True)
    c_own, c_z = wide[:SUB, :], wide[SUB : 2 * SUB, :]
    c_y = split_dot(spread_y, center, swap=True)
    ze[0] = ze[0] * jnp.concatenate([c_z] * (nx // SUB), axis=0)
    at_edge = sub == parity * (SUB - 1)
    for i in range(nx):
        at = plane(i + 1)
        result = own_s[at, :] * c_own + oy_s[at, :] * c_y
        result = result + only(at_edge, ze[0, pl.ds(i, 1), :])
        if i == 0:
            result = result + ox_s[plane(1), :] * wide[2 * SUB : 3 * SUB, :]
        if i == nx - 1:
            result = result + ox_s[plane(2), :] * wide[3 * SUB :, :]
        out_ref[plane(i), :] = result


def body(tiles, layers, classes, well_mask, source):
    nx, nz, ny = classes.shape
    assert nx == EDGE and nz == HALF == SUB and layers % 2 == 0
    cells, pairs = ny // EDGE, layers // 2
    assert 4 * cells == LANES and pairs * cells <= LANES
    rows = VALUES * cells // LANES
    flat = lambda a: a.reshape(nx * nz, ny)
    f32 = lambda *shape: pltpu.VMEM(shape, jnp.float32)
    dma = pltpu.SemaphoreType.DMA
    block = (nx * SUB, ny)
    wide = ((nx + 2) * SUB, ny)
    scratch = [
        pltpu.VMEM(block, jnp.int32), pltpu.VMEM(block, jnp.int32), f32(*block),
        pltpu.VMEM((6 * VALUES, 4 * PADDED), jnp.bfloat16),
        f32((nx + 4) * SUB, ny), f32(*wide), f32(2, 3, nx, ny), f32(2, 3, nx, ny),
        f32(4, 1, ny), f32(4, 1, ny),
        f32(2, 2, nx, ny), f32(2, 2, nx, ny), f32(4, nx, ny),
        f32(*block), f32(*block), f32((nx + 1) * SUB, ny), f32(*block), f32(*block), f32(*block),
        f32(*wide), f32(*wide), f32(*wide), f32(4 * SUB, ny), f32(2, nx, ny), f32(2, 4, nx, ny),
        pltpu.VMEM((6, nx, ny), jnp.int32), pltpu.VMEM((ny, LANES), jnp.bfloat16), f32(PADDED, ny), f32(6, rows, LANES), f32(12, rows, LANES), f32(rows, LANES),
        f32(tiles * pairs, rows, LANES), f32(pairs * tiles * rows, LANES), f32(tiles, LANES),
        dma((4,)), dma((2, 2)), dma((2, 2)), dma((2, 3)), dma((2, 3)), dma((4,)), dma((4,)),
        dma((12,)), dma((12,)), dma((tiles * pairs,)), dma((tiles * pairs,)),
    ]
    route = jnp.asarray(np.pad(routing_table(), ((0, 38), (0, 0), (0, 0))), jnp.bfloat16)
    result = pl.pallas_call(
        functools.partial(kernel, tiles, layers, nx, ny),
        out_shape=jax.ShapeDtypeStruct(block, jnp.float32),
        in_specs=[pl.BlockSpec(memory_space=pltpu.HBM)] * 4,
        out_specs=pl.BlockSpec(memory_space=pltpu.VMEM),
        scratch_shapes=scratch,
        compiler_params=pltpu.CompilerParams(
            collective_id=0, has_side_effects=True, vmem_limit_bytes=107 * 2**19
        ),
    )(flat(classes), flat(well_mask), flat(source), route)
    return result.reshape(nx, nz, ny)


def solution(mesh):
    spec = P("tile", "layer", None)
    return jax.shard_map(
        functools.partial(body, mesh.shape["tile"], mesh.shape["layer"]),
        mesh=mesh, in_specs=(spec, spec, spec), out_specs=spec, check_vma=False,
    )
```
